32 devices in a mesh: row: 4 (over y, x), col: 8 (over z, core).
Axes of the slice: x: 2, y: 2, z: 4, core: 2. Of those that a mesh axis runs over, the one named last changes fastest.
Arguments:
- tokens: bfloat16 [16384, 1024], P(('row', 'col')), may hold values from -6 to 6
- gain_attn: bfloat16 [1024], P(('row', 'col')), may hold values from 0.099609375 to 1.8984375
- w_query: bfloat16 [1024, 1024], P(('row', 'col')), may hold values from -0.1875 to 0.1875
- w_keyval: bfloat16 [1024, 256], P(('row', 'col')), may hold values from -0.1875 to 0.1875
- w_out: bfloat16 [1024, 1024], P(('row', 'col')), may hold values from -3 to 3
- gain_mlp: bfloat16 [1024], P(('row', 'col')), may hold values from 0.099609375 to 1.8984375
- w_gate: bfloat16 [1024, 3072], P('row', 'col'), may hold values from -0.1875 to 0.1875
- w_up: bfloat16 [1024, 3072], P('row', 'col'), may hold values from -0.1875 to 0.1875
- w_down: bfloat16 [3072, 1024], P('col', 'row'), may hold values from -0.109375 to 0.109375
- segment: int32 [16384], P(('row', 'col')), may hold values from 0 to 15, as said below
- cotangent: bfloat16 [16384, 1024], P(('row', 'col')), may hold values from -6 to 6
Outputs:
- output: bfloat16 [16384, 1024], P(('row', 'col'))
- grad_tokens: float32 [16384, 1024], P(('row', 'col'))
- grad_gain_attn: float32 [1024], P(('row', 'col'))
- grad_query: float32 [1024, 1024], P(('row', 'col'))
- grad_keyval: float32 [1024, 256], P(('row', 'col'))
- grad_out: float32 [1024, 1024], P(('row', 'col'))
- grad_gain_mlp: float32 [1024], P(('row', 'col'))
- grad_gate: float32 [1024, 3072], P('row', 'col')
- grad_up: float32 [1024, 3072], P('row', 'col')
- grad_down: float32 [3072, 1024], P('col', 'row')
The draws below stay inside these ranges and needn't reach their ends.
Inputs may be any that keep to these rules, and one draw needn't show every extreme that they name: `segment`: never falling; each pack of 2048 tokens holds two documents, numbered 2p and 2p + 1 for pack p; the first one is 512 to 1536 tokens long.
All inputs are finite; a program needn't handle non-finite values.
Results may differ from the reference program's by a relative error of at most 0.014.
Values may be sent and summed in bfloat16 or wider, within the bound.
A program may use at most 256 MiB of HBM per device.

```python
import math
import jax
import jax.numpy as jnp
from jax import lax

D = 1024
H = 8
DH = 128
FF = 3072
WINDOW = 1024
PACK = 2048
TOKENS = 16384


def draw_segment(key, part):
    key = jax.random.fold_in(key, 7)
    packs = TOKENS // PACK
    cuts = jax.random.randint(key, (packs,), PACK // 4, 3 * PACK // 4 + 1, dtype=jnp.int32)
    places = jnp.arange(TOKENS, dtype=jnp.int32)
    owner = places // PACK
    later = (places % PACK >= cuts[owner]).astype(jnp.int32)
    return 2 * owner + later


def levels(rng, dims, split, low, largest):
    level, own = 1.0, jax.random.fold_in(rng, 6)
    for axis_at, blocks in split:
        heights = jnp.exp(jax.random.uniform(jax.random.fold_in(own, axis_at), (blocks,), jnp.float32, low / len(split), largest / len(split)))
        level = level * jnp.repeat(heights, dims[axis_at] // blocks).reshape([-1 if axis == axis_at else 1 for axis in range(len(dims))])
    return level


def normal_values(own_key, dims, spread, reach, split=(), held_as=jnp.bfloat16):
    level = levels(own_key, dims, split, -0.22, 0.18) if split else 1.0
    values = jax.random.normal(own_key, dims, jnp.float32) * spread * level
    return jnp.minimum(jnp.maximum(values, -reach), reach).astype(held_as)


def setup_inputs(seed: int = 0) -> dict:
    streams_of = jax.random.split(jax.random.key(seed), 12)
    return {
        "tokens": normal_values(streams_of[0], (TOKENS, D), 1.0, 6.0, ((0, 32),)),
        "gain_attn": jnp.clip(1.0 + 0.18 * jax.random.normal(streams_of[1], (D,), jnp.float32), 0.099609375, 1.8984375).astype(jnp.bfloat16),
        "w_query": normal_values(streams_of[2], (D, H * DH), D ** -0.5, 0.1875, ((0, 32),)),
        "w_keyval": normal_values(streams_of[3], (D, 2 * DH), D ** -0.5, 0.1875, ((0, 32),)),
        "w_out": normal_values(streams_of[4], (H * DH, D), 4 ** -0.5, 3.0, ((0, 32),)),
        "gain_mlp": jnp.clip(1.0 + 0.18 * jax.random.normal(streams_of[5], (D,), jnp.float32), 0.099609375, 1.8984375).astype(jnp.bfloat16),
        "w_gate": normal_values(streams_of[6], (D, FF), D ** -0.5, 0.1875, ((0, 4), (1, 8))),
        "w_up": normal_values(streams_of[7], (D, FF), D ** -0.5, 0.1875, ((0, 4), (1, 8))),
        "w_down": normal_values(streams_of[8], (FF, D), FF ** -0.5, 0.109375, ((0, 8), (1, 4))),
        "segment": draw_segment(jax.random.fold_in(streams_of[11], 71), 0),
        "cotangent": normal_values(streams_of[10], (TOKENS, D), 1.0, 6.0, ((0, 32),)),
    }


EPS = 1e-06
NEGATIVE = -1e+30

@jax.custom_vjp
def low(v):
    return lax.optimization_barrier(v.astype(jnp.bfloat16)).astype(jnp.float32)

@jax.custom_vjp
def low_back(v):
    return v

def low_keep(v):
    return (low(v), None)

def low_pass(kept, grad):
    return (grad,)

def back_keep(v):
    return (v, None)

def back_low(kept, grad):
    return (low(grad),)
low.defvjp(low_keep, low_pass)
low_back.defvjp(back_keep, back_low)

def rounded(value):
    return low(low_back(value))

def normalize(value):
    return value * lax.rsqrt(lax.optimization_barrier(jnp.mean(value * value, axis=-1, keepdims=True)) + EPS)

def matmul(left, right):
    return jnp.dot(left, right, precision=lax.Precision.HIGHEST, preferred_element_type=jnp.float32)

def attend(block):
    query, keys, values, marks = block
    heads = query.reshape(PACK, H, DH)
    scale = 1.0 / math.sqrt(DH)
    scores = jnp.einsum('qhd,kd->hqk', heads, keys, precision=lax.Precision.HIGHEST) * scale
    scores = low_back(scores)
    places = jnp.arange(PACK, dtype=jnp.int32)
    gap = places[:, None] - places[None, :]
    allowed = (marks[:, None] == marks[None, :]) & (gap >= 0) & (gap < WINDOW)
    scores = jnp.where(allowed[None], scores, NEGATIVE)
    top = lax.optimization_barrier(jnp.max(scores, axis=-1, keepdims=True))
    expo = jnp.where(allowed[None], jnp.exp(scores - top), 0.0)
    probs = expo / lax.optimization_barrier(jnp.sum(expo, axis=-1, keepdims=True))
    mixed = jnp.einsum('hqk,kd->qhd', low(probs), values, precision=lax.Precision.HIGHEST)
    return rounded(mixed.reshape(PACK, H * DH))

def forward(inputs, gain_first, query_weight, keyval_weight, out_weight, gain_second, gate_weight, up_weight, down_weight, segment):
    attn_in = low(normalize(inputs) * gain_first)
    query = rounded(matmul(attn_in, query_weight))
    keyval = rounded(matmul(attn_in, keyval_weight))
    packs = inputs.shape[0] // PACK
    blocks = (query.reshape(packs, PACK, H * DH), keyval[:, :DH].reshape(packs, PACK, DH), keyval[:, DH:].reshape(packs, PACK, DH), segment.reshape(packs, PACK))
    attended = lax.map(jax.checkpoint(attend), blocks).reshape(packs * PACK, H * DH)
    middle = inputs + low_back(matmul(attended, out_weight))
    mlp_in = low(normalize(middle) * gain_second)
    gate = low_back(matmul(mlp_in, gate_weight))
    up = low_back(matmul(mlp_in, up_weight))
    hidden = low(jax.nn.gelu(gate, approximate=True) * up)
    return middle + low_back(matmul(hidden, down_weight))

def reference(tokens, gain_attn, w_query, w_keyval, w_out, gain_mlp, w_gate, w_up, w_down, segment, cotangent):
    floats = [a.astype(jnp.float32) for a in (tokens, gain_attn, w_query, w_keyval, w_out, gain_mlp, w_gate, w_up, w_down)]

    def closed(*values):
        return forward(*values, segment)
    result, pullback = jax.vjp(closed, *floats)
    grads = pullback(cotangent.astype(jnp.float32))
    return (result.astype(jnp.bfloat16), grads[0], grads[1], grads[2], grads[3], grads[4], grads[5], grads[6], grads[7], grads[8])
```

```python
import functools
import math

import jax
import jax.numpy as jnp
from jax import lax
from jax.experimental import pallas as pl
from jax.experimental.pallas import tpu as pltpu
from jax.sharding import PartitionSpec as P

H = 8
DH = 128
WINDOW = 1024

EPS = 1e-06
NEGATIVE = -1e30
MESH = pl.DeviceIdType.MESH
BF = jnp.bfloat16
F32 = jnp.float32


def product(left, right):
    return jnp.dot(left, right, preferred_element_type=jnp.float32)


def inner(left, right):
    return lax.dot_general(
        left, right, (((0,), (0,)), ((), ())), preferred_element_type=jnp.float32
    )


def against(left, right):
    return lax.dot_general(
        left, right, (((1,), (1,)), ((), ())), preferred_element_type=jnp.float32
    )


class Place:
    def __init__(self, shape):
        rows, cols = shape
        self.X = math.isqrt(rows)
        while rows % self.X:
            self.X -= 1
        self.Y = rows // self.X
        self.Z = cols // 2
        self.R = rows
        self.row, self.col = lax.axis_index("row"), lax.axis_index("col")
        self.y, self.x = self.row // self.X, self.row % self.X
        self.z, self.core = self.col // 2, self.col % 2
        self.xs, self.ys, self.zs = range(1, self.X), range(1, self.Y), range(1, self.Z)

    def row_at(self, dy=0, dx=0):
        return lax.rem(self.y + dy + self.Y, self.Y) * self.X + lax.rem(
            self.x + dx + self.X, self.X
        )

    def z_at(self, dz):
        return lax.rem(self.z + dz + self.Z, self.Z)

    def device(self, dy=0, dx=0, dz=0, other=False):
        core = 1 - self.core if other else self.core
        return (self.row_at(dy, dx), self.z_at(dz) * 2 + core)

    def greet(self):
        barrier = pltpu.get_barrier_semaphore()
        mates = [self.device(dx=d) for d in self.xs]
        mates += [self.device(dy=d) for d in self.ys]
        mates += [self.device(dz=d) for d in self.zs]
        mates.append(self.device(other=True))
        for mate in mates:
            pl.semaphore_signal(barrier, inc=1, device_id=mate, device_id_type=MESH)
        pl.semaphore_wait(barrier, len(mates))


def remote(src, dst, send, recv, device):
    return pltpu.make_async_remote_copy(
        src_ref=src, dst_ref=dst, send_sem=send, recv_sem=recv, device_id=device,
        device_id_type=MESH,
    )


class Sems:
    def __init__(self, send, recv):
        self.send, self.recv, self.count = send, recv, 0

    def take(self):
        self.count += 1
        return self.send.at[self.count - 1], self.recv.at[self.count - 1]


def gather_count(X, Y, Z):
    return (Z - 1) + Z * ((X - 1) + (Y - 1) + 2 * (X - 1) * (Y - 1))


class Gather:
    def __init__(self, at, here, sems, own):
        self.at, self.p, self.own = at, here, own
        self.sent = []
        p = here
        self.zsem = {k: sems.take() for k in p.zs}
        self.xsem = {(s, d): sems.take() for s in range(p.Z) for d in p.xs}
        self.ysem = {(s, d): sems.take() for s in range(p.Z) for d in p.ys}
        self.dsem = {
            (s, h, dx, dy): sems.take()
            for s in range(p.Z) for h in (0, 1) for dx in p.xs for dy in p.ys
        }

    def push(self, src, dst, sem, device):
        copy = remote(src, dst, sem[0], sem[1], device)
        copy.start()
        self.sent.append(copy)

    def arrive(self, place, sem):
        remote(place, place, sem[0], sem[1], self.p.device(other=True)).wait_recv()

    def spread_z(self):
        p = self.p
        for k in p.zs:
            self.push(self.own, self.at(p.z, p.row, None), self.zsem[k], p.device(dz=-k))

    def spread_xy(self, s):
        p = self.p
        zc = p.z_at(s)
        place = self.at(zc, p.row, None)
        src = self.own
        if s:
            self.arrive(place, self.zsem[s])
            src = place
        for d in p.xs:
            self.push(src, place, self.xsem[s, d], p.device(dx=d))
        for d in p.ys:
            self.push(src, place, self.ysem[s, d], p.device(dy=d))

    def spread_diagonal(self, s):
        p = self.p
        zc = p.z_at(s)
        for d in p.xs:
            r = p.row_at(dx=-d)
            self.arrive(self.at(zc, r, None), self.xsem[s, d])
            half = self.at(zc, r, 0)
            for e in p.ys:
                self.push(half, half, self.dsem[s, 0, d, e], p.device(dy=e))
        for e in p.ys:
            r = p.row_at(dy=-e)
            self.arrive(self.at(zc, r, None), self.ysem[s, e])
            half = self.at(zc, r, 1)
            for d in p.xs:
                self.push(half, half, self.dsem[s, 1, d, e], p.device(dx=d))

    def close(self, s):
        p = self.p
        zc = p.z_at(s)
        for d in p.xs:
            for e in p.ys:
                r = p.row_at(dy=-e, dx=-d)
                for h in (0, 1):
                    self.arrive(self.at(zc, r, h), self.dsem[s, h, d, e])

    def finish(self):
        for copy in self.sent:
            copy.wait_send()


def scatter_count(X, Y, Z):
    return (Z - 1) + Z * (2 * (X - 1) * (Y - 1) + 2 * (X - 1) + 2 * (Y - 1))


class Scatter:
    def __init__(self, part, cut, here, sems, diag, fromx, fromy, sumx, sumy, sumz, fromz):
        self.part, self.cut, self.p = part, cut, here
        self.diag, self.fromx, self.fromy = diag, fromx, fromy
        self.sumx, self.sumy, self.sumz, self.fromz = sumx, sumy, sumz, fromz
        self.sent = []
        p = here
        self.zsem = {k: sems.take() for k in p.zs}
        self.xsem = {(s, h, d): sems.take() for s in range(p.Z) for h in (0, 1) for d in p.xs}
        self.ysem = {(s, h, d): sems.take() for s in range(p.Z) for h in (0, 1) for d in p.ys}
        self.dsem = {
            (s, h, dx, dy): sems.take()
            for s in range(p.Z) for h in (0, 1) for dx in p.xs for dy in p.ys
        }

    def push(self, src, dst, sem, device):
        copy = remote(src, dst, sem[0], sem[1], device)
        copy.start()
        self.sent.append(copy)

    def arrive(self, place, sem):
        remote(place, place, sem[0], sem[1], self.p.device(other=True)).wait_recv()

    def spot(self, d, e):
        return (d - 1) * (self.p.Y - 1) + e - 1

    def first(self, s):
        p, cut = self.p, self.cut
        zc = p.z_at(s)
        for d in p.xs:
            for e in p.ys:
                far = self.part(zc, p.row_at(dy=e, dx=d))
                n = self.spot(d, e)
                self.push(cut(far, 0), self.diag.at[s, 0, n], self.dsem[s, 0, d, e], p.device(dx=d))
                self.push(cut(far, 1), self.diag.at[s, 1, n], self.dsem[s, 1, d, e], p.device(dy=e))
        for d in p.xs:
            near = self.part(zc, p.row_at(dx=d))
            self.push(cut(near, 0), cut(self.fromx.at[s, d - 1], 0), self.xsem[s, 0, d], p.device(dx=d))
        for e in p.ys:
            near = self.part(zc, p.row_at(dy=e))
            self.push(cut(near, 1), cut(self.fromy.at[s, e - 1], 1), self.ysem[s, 1, e], p.device(dy=e))

    def second(self, s):
        p, cut = self.p, self.cut
        zc = p.z_at(s)
        for e in p.ys:
            total = cut(self.part(zc, p.row_at(dy=e)), 0)[...].astype(F32)
            for d in p.xs:
                place = self.diag.at[s, 0, self.spot(d, e)]
                self.arrive(place, self.dsem[s, 0, d, e])
                total = total + place[...].astype(F32)
            self.sumy[s, e - 1] = total.astype(BF)
            self.push(self.sumy.at[s, e - 1], cut(self.fromy.at[s, e - 1], 0), self.ysem[s, 0, e], p.device(dy=e))
        for d in p.xs:
            total = cut(self.part(zc, p.row_at(dx=d)), 1)[...].astype(F32)
            for e in p.ys:
                place = self.diag.at[s, 1, self.spot(d, e)]
                self.arrive(place, self.dsem[s, 1, d, e])
                total = total + place[...].astype(F32)
            self.sumx[s, d - 1] = total.astype(BF)
            self.push(self.sumx.at[s, d - 1], cut(self.fromx.at[s, d - 1], 1), self.xsem[s, 1, d], p.device(dx=d))

    def third(self, s):
        p, cut = self.p, self.cut
        total = self.part(p.z_at(s), p.row)[...].astype(F32)
        for d in p.xs:
            for h in (0, 1):
                self.arrive(cut(self.fromx.at[s, d - 1], h), self.xsem[s, h, d])
            total = total + self.fromx[s, d - 1].astype(F32)
        for e in p.ys:
            for h in (0, 1):
                self.arrive(cut(self.fromy.at[s, e - 1], h), self.ysem[s, h, e])
            total = total + self.fromy[s, e - 1].astype(F32)
        if s:
            self.sumz[s - 1] = total.astype(BF)
            self.push(self.sumz.at[s - 1], self.fromz.at[s - 1], self.zsem[s], p.device(dz=s))
            return None
        for k in p.zs:
            self.arrive(self.fromz.at[k - 1], self.zsem[k])
            total = total + self.fromz[k - 1].astype(F32)
        return total

    def finish(self):
        for copy in self.sent:
            copy.wait_send()


def scatter_scratch(X, Y, Z, block, half):
    return [
        pltpu.VMEM((Z, 2, (X - 1) * (Y - 1)) + half, BF),
        pltpu.VMEM((Z, X - 1) + block, BF),
        pltpu.VMEM((Z, Y - 1) + block, BF),
        pltpu.VMEM((Z, X - 1) + half, BF),
        pltpu.VMEM((Z, Y - 1) + half, BF),
        pltpu.VMEM((Z - 1,) + block, BF),
        pltpu.VMEM((Z - 1,) + block, BF),
    ]


def sides(shape):
    x = math.isqrt(shape[0])
    while shape[0] % x:
        x -= 1
    return x, shape[0] // x, shape[1] // 2


def gather_kernel(shape, with_slab, *refs):
    if with_slab:
        slab, ffn, slabs, ffns, asend, arecv, fsend, frecv, csend, crecv = refs
    else:
        ffn, ffns, fsend, frecv = refs
    p = Place(shape)
    p.greet()
    br = ffn.shape[1]

    def ffn_at(zc, r, half):
        if half is None:
            return ffns.at[zc, :, r]
        return ffns.at[zc, :, r, pl.ds(half * (br // 2), br // 2)]

    far = Gather(ffn_at, p, Sems(fsend, frecv), ffn)
    ffns[p.z, :, p.row] = ffn[...]
    if with_slab:
        ar = slab.shape[0]

        def slab_at(zc, r, half):
            if half is None:
                return slabs.at[r, zc, p.core]
            return slabs.at[r, zc, p.core, pl.ds(half * (ar // 2), ar // 2)]

        near = Gather(slab_at, p, Sems(asend, arecv), slab)
        slabs[p.row, p.z, p.core] = slab[...]
        mate = p.device(other=True)
        passed = []

        def hand(n, zc, r):
            place = slabs.at[r, zc, p.core]
            copy = remote(place, place, csend.at[n], crecv.at[n], mate)
            copy.start()
            passed.append((copy, zc, r, n))

        near.spread_z()
        near.spread_xy(0)
        for s in range(p.Z):
            if s + 1 < p.Z:
                near.spread_xy(s + 1)
            near.spread_diagonal(s)
        far.spread_z()
        far.spread_xy(0)
        n = 0
        for s in range(p.Z):
            near.close(s)
            zc = p.z_at(s)
            for dy in range(p.Y):
                for dx in range(p.X):
                    hand(n, zc, p.row_at(dy, dx))
                    n += 1
        for copy, zc, r, n in passed:
            copy.wait_send()
            place = slabs.at[r, zc, 1 - p.core]
            remote(place, place, csend.at[n], crecv.at[n], mate).wait_recv()
        near.finish()
    else:
        far.spread_z()
        far.spread_xy(0)
    for s in range(p.Z):
        if s + 1 < p.Z:
            far.spread_xy(s + 1)
        far.spread_diagonal(s)
    for s in range(p.Z):
        far.close(s)
    far.finish()


VM = pl.BlockSpec(memory_space=pltpu.VMEM)
DMA = pltpu.SemaphoreType.DMA


def gather_weights(shape, slab, ffn):
    X, Y, Z = sides(shape)
    R = shape[0]
    n = gather_count(X, Y, Z)
    with_slab = slab is not None
    ffns = jax.ShapeDtypeStruct((Z, 3, R) + ffn.shape[1:], BF)
    outs = [ffns]
    args = [ffn]
    scratch = [DMA((n,)), DMA((n,))]
    if with_slab:
        outs = [jax.ShapeDtypeStruct((R, Z, 2) + slab.shape, BF)] + outs
        args = [slab] + args
        scratch = [DMA((n,)), DMA((n,))] + scratch + [DMA((R * Z,)), DMA((R * Z,))]
    return pl.pallas_call(
        functools.partial(gather_kernel, shape, with_slab),
        out_shape=outs,
        in_specs=[VM] * len(args),
        out_specs=[VM] * len(outs),
        scratch_shapes=scratch,
        compiler_params=pltpu.CompilerParams(
            collective_id=0, has_side_effects=True, vmem_limit_bytes=48 << 20
        ),
        name="gather_weights",
    )(*args)


def scatter_kernel(shape, with_slab, *refs):
    if with_slab:
        slabs, ffns, slab_out, ffn_out = refs[:4]
        scratch = refs[4:]
        fwork, awork = scratch[:7], scratch[7:14]
        plane, crossed, fsend, frecv, asend, arecv, csem = scratch[14:]
    else:
        ffns, ffn_out = refs[:2]
        fwork = refs[2:9]
        fsend, frecv = refs[9:]
    p = Place(shape)
    p.greet()
    br = ffns.shape[3]

    far = Scatter(
        lambda zc, r: ffns.at[zc, :, r],
        lambda ref, h: ref.at[:, pl.ds(h * (br // 2), br // 2)],
        p, Sems(fsend, frecv), *fwork,
    )
    order = list(range(1, p.Z)) + [0]
    if with_slab:
        ar = slabs.shape[3]
        cross = remote(
            slabs.at[:, :, 1 - p.core], crossed, csem.at[0], csem.at[1], p.device(other=True)
        )
        cross.start()
    for s in order:
        far.first(s)
    if with_slab:
        cross.wait()

        def fold(n, carry):
            r, zc = n // p.Z, n % p.Z
            mine = slabs[r, zc, p.core].astype(F32) + crossed[r, zc].astype(F32)
            plane[r, zc] = mine.astype(BF)
            return carry

        lax.fori_loop(0, p.R * p.Z, fold, 0)
        near = Scatter(
            lambda zc, r: plane.at[r, zc],
            lambda ref, h: ref.at[pl.ds(h * (ar // 2), ar // 2)],
            p, Sems(asend, arecv), *awork,
        )
        for s in order:
            near.first(s)
    for s in order:
        far.second(s)
    if with_slab:
        for s in order:
            near.second(s)
    for s in order:
        total = far.third(s)
    ffn_out[...] = total
    if with_slab:
        for s in order:
            total = near.third(s)
        slab_out[...] = total
        near.finish()
    far.finish()


def scatter_grads(shape, slabs, ffns):
    X, Y, Z = sides(shape)
    R = shape[0]
    n = scatter_count(X, Y, Z)
    with_slab = slabs is not None
    block = (3,) + ffns.shape[3:]
    half = (3, ffns.shape[3] // 2, ffns.shape[4])
    outs = [jax.ShapeDtypeStruct(block, F32)]
    args = [ffns]
    scratch = scatter_scratch(X, Y, Z, block, half)
    if with_slab:
        ablock = slabs.shape[3:]
        ahalf = (ablock[0] // 2, ablock[1])
        outs = [jax.ShapeDtypeStruct(ablock, F32)] + outs
        args = [slabs] + args
        scratch += scatter_scratch(X, Y, Z, ablock, ahalf)
        scratch += [pltpu.VMEM((R, Z) + ablock, BF)] * 2
    scratch += [DMA((n,)), DMA((n,))]
    if with_slab:
        scratch += [DMA((n,)), DMA((n,)), DMA((2,))]
    return pl.pallas_call(
        functools.partial(scatter_kernel, shape, with_slab),
        out_shape=outs,
        in_specs=[VM] * len(args),
        out_specs=[VM] * len(outs),
        scratch_shapes=scratch,
        compiler_params=pltpu.CompilerParams(
            collective_id=1, has_side_effects=True, vmem_limit_bytes=60 << 20
        ),
        name="scatter_grads",
    )(*args)


def from_behind(block, axis, distance):
    devices = range(lax.axis_size(axis))
    route = [(i - distance, i) for i in devices if i - distance in devices]
    return lax.ppermute(block, axis, route)


def swap(block):
    return lax.ppermute(block, "col", [(i, i ^ 1) for i in range(lax.axis_size("col"))])


def gated(gate, up):
    return jax.nn.gelu(gate, approximate=True) * up


def norm_back(grad_normed, value, scale):
    return scale * grad_normed - value * scale**3 * jnp.mean(
        grad_normed * value, axis=-1, keepdims=True
    )


def shards(
    shape,
    tokens, gain_attn, w_query, w_keyval, w_out, gain_mlp, w_gate, w_up, w_down, segment, cotangent
):
    R, C = shape
    D = tokens.shape[1]
    with_slab = w_query.shape[0] % 32 == 0
    ffn = jnp.stack([w_gate, w_up, w_down.T])
    slab = jnp.concatenate(
        [w_query, w_keyval, w_out,
         jnp.pad(jnp.stack([gain_attn, gain_mlp], axis=1), ((0, 0), (0, 126)))], axis=1)
    if with_slab:
        slabs, ffns = gather_weights(shape, slab, ffn)
        slabs = slabs.reshape(D, slab.shape[1])
    else:
        slabs = lax.all_gather(slab, ("row", "col"), axis=0, tiled=True)
        (ffns,) = gather_weights(shape, None, ffn)
    E = H * DH
    query_weight = slabs[:, :E]
    keyval_weight = slabs[:, E : E + 2 * DH]
    out_weight = slabs[:, E + 2 * DH : 2 * E + 2 * DH]
    gain_first = slabs[:, 2 * E + 2 * DH].astype(F32)
    gain_second = slabs[:, 2 * E + 2 * DH + 1].astype(F32)
    Z = C // 2
    ffns = ffns.reshape(Z, 3, D, -1)

    rows = tokens.shape[0]
    inputs = tokens.astype(jnp.float32)
    scale_first = lax.rsqrt(jnp.mean(inputs * inputs, axis=-1, keepdims=True) + EPS)
    normed_first = inputs * scale_first
    attn_in = (normed_first * gain_first).astype(jnp.bfloat16)
    query = product(attn_in, query_weight).astype(jnp.bfloat16)
    keyval = product(attn_in, keyval_weight).astype(jnp.bfloat16)
    marks = segment + 1
    reach = (WINDOW + rows - 2) // rows
    pieces = [keyval]
    piece_marks = [marks]
    for offset in range(1, reach + 1):
        moved, moved_marks = from_behind((keyval, marks), "col", offset)
        pieces.insert(0, moved)
        piece_marks.insert(0, moved_marks)
    keys_all = jnp.concatenate(pieces, axis=0)
    marks_all = jnp.concatenate(piece_marks, axis=0)
    keys = keys_all[:, :DH]
    values = keys_all[:, DH:]
    query_places = reach * rows + jnp.arange(rows, dtype=jnp.int32)
    key_places = jnp.arange(keys_all.shape[0], dtype=jnp.int32)
    gap = query_places[:, None] - key_places[None, :]
    allowed = (marks[:, None] == marks_all[None, :]) & (gap >= 0) & (gap < WINDOW)
    group = min(H, max(1, 1024 // rows))
    blocks = H // group
    scale = 1.0 / math.sqrt(DH)
    query_groups = query.reshape(rows, blocks, group, DH).transpose(1, 2, 0, 3)

    def scores_of(part):
        scores = jnp.einsum("gqd,kd->gqk", part, keys, preferred_element_type=jnp.float32) * scale
        return jnp.where(allowed[None], scores, NEGATIVE)

    def forward_group(part):
        scores = scores_of(part)
        top = jnp.max(scores, axis=-1, keepdims=True)
        expo = jnp.where(allowed[None], jnp.exp(scores - top), 0.0)
        total = jnp.sum(expo, axis=-1, keepdims=True)
        probs = expo / total
        mixed = jnp.einsum(
            "gqk,kd->gqd", probs.astype(jnp.bfloat16), values, preferred_element_type=jnp.float32
        )
        return (mixed.astype(jnp.bfloat16), top + jnp.log(total))

    mixed_groups, logsum = lax.map(forward_group, query_groups)
    attended = mixed_groups.transpose(2, 0, 1, 3).reshape(rows, H * DH)
    middle = inputs + product(attended, out_weight)
    scale_second = lax.rsqrt(jnp.mean(middle * middle, axis=-1, keepdims=True) + EPS)
    normed_second = middle * scale_second
    mlp_in = (normed_second * gain_second).astype(jnp.bfloat16)

    other_in = swap(mlp_in)
    other_grad = swap(cotangent)
    both_in = jnp.concatenate([mlp_in, other_in])
    both_grad = jnp.concatenate([cotangent, other_grad])
    out_sum = 0.0
    grad_in_sum = 0.0
    weight_grads = []
    for zc in range(Z):
        gate_w, up_w, down_w = ffns[zc, 0], ffns[zc, 1], ffns[zc, 2]
        gate_rows, up_rows = product(both_in, gate_w), product(both_in, up_w)
        grad_hidden = product(both_grad, down_w)
        hidden, pull = jax.vjp(gated, gate_rows, up_rows)
        hidden = hidden.astype(BF)
        grad_gate, grad_up = pull(grad_hidden)
        grad_gate, grad_up = grad_gate.astype(BF), grad_up.astype(BF)
        out_sum += against(hidden, down_w)
        grad_in_sum += against(grad_gate, gate_w) + against(grad_up, up_w)
        weight_grads.append(
            jnp.stack([inner(both_in, grad_gate), inner(both_in, grad_up), inner(both_grad, hidden)]).astype(BF)
        )
    weight_grads = jnp.stack(weight_grads).reshape((Z, 3, R) + w_gate.shape)
    mlp_out = out_sum[:rows] + swap(out_sum[rows:].astype(BF)).astype(F32)
    grad_mlp_in = grad_in_sum[:rows] + swap(grad_in_sum[rows:])
    output = (middle + mlp_out).astype(jnp.bfloat16)

    grad_outputs = cotangent.astype(jnp.float32)
    gain_second_grad = jnp.sum(grad_mlp_in * normed_second, axis=0)
    grad_middle = grad_outputs + norm_back(grad_mlp_in * gain_second, middle, scale_second)
    grad_branch = grad_middle.astype(jnp.bfloat16)
    out_grad = inner(attended, grad_branch)
    grad_attended = against(grad_branch, out_weight).astype(jnp.bfloat16)
    grad_groups = grad_attended.reshape(rows, blocks, group, DH).transpose(1, 2, 0, 3)

    def backward_group(item):
        part, grad_part, logs = item
        scores = scores_of(part)
        probs = jnp.where(allowed[None], jnp.exp(scores - logs), 0.0)
        grad_probs = jnp.einsum(
            "gqd,kd->gqk", grad_part, values, preferred_element_type=jnp.float32
        )
        centre = jnp.sum(probs * grad_probs, axis=-1, keepdims=True)
        grad_scores = (probs * (grad_probs - centre)).astype(jnp.bfloat16)
        grad_part_query = (
            jnp.einsum("gqk,kd->gqd", grad_scores, keys, preferred_element_type=jnp.float32) * scale
        )
        grad_keys = (
            jnp.einsum("gqk,gqd->kd", grad_scores, part, preferred_element_type=jnp.float32) * scale
        )
        grad_values = jnp.einsum(
            "gqk,gqd->kd", probs.astype(jnp.bfloat16), grad_part, preferred_element_type=jnp.float32
        )
        return (grad_part_query, grad_keys, grad_values)

    query_parts, key_parts, value_parts = lax.map(
        backward_group, (query_groups, grad_groups, logsum)
    )
    grad_query_act = query_parts.transpose(2, 0, 1, 3).reshape(rows, H * DH).astype(jnp.bfloat16)
    grad_keyval_all = jnp.concatenate(
        [jnp.sum(key_parts, axis=0), jnp.sum(value_parts, axis=0)], axis=1
    )
    grad_own = grad_keyval_all[reach * rows :]
    for offset in range(1, reach + 1):
        sent = grad_keyval_all[(reach - offset) * rows : (reach - offset + 1) * rows]
        grad_own = grad_own + from_behind(sent.astype(jnp.bfloat16), "col", -offset).astype(
            sent.dtype
        )
    grad_keyval_act = grad_own.astype(jnp.bfloat16)
    grad_attn_in = against(grad_query_act, query_weight) + against(grad_keyval_act, keyval_weight)
    query_grad = inner(attn_in, grad_query_act)
    keyval_grad = inner(attn_in, grad_keyval_act)
    gain_first_grad = jnp.sum(grad_attn_in * normed_first, axis=0)
    grad_inputs = grad_middle + norm_back(grad_attn_in * gain_first, inputs, scale_first)

    gains = jnp.pad(jnp.stack([gain_first_grad, gain_second_grad], axis=1), ((0, 0), (0, 126)))
    slab_grads = jnp.concatenate([query_grad, keyval_grad, out_grad, gains], axis=1)
    if with_slab:
        slab_grad, ffn_grad = scatter_grads(
            shape, slab_grads.astype(BF).reshape((R, Z, 2) + slab.shape), weight_grads
        )
    else:
        slab_grad = lax.psum_scatter(slab_grads, ("row", "col"), scatter_dimension=0, tiled=True)
        (ffn_grad,) = scatter_grads(shape, None, weight_grads)
    return (
        output,
        grad_inputs,
        slab_grad[:, 2 * E + 2 * DH],
        slab_grad[:, :E],
        slab_grad[:, E : E + 2 * DH],
        slab_grad[:, E + 2 * DH : 2 * E + 2 * DH],
        slab_grad[:, 2 * E + 2 * DH + 1],
        ffn_grad[0],
        ffn_grad[1],
        ffn_grad[2].T,
    )


def solution(mesh):
    shape = (mesh.shape["row"], mesh.shape["col"])
    return jax.shard_map(
        functools.partial(shards, shape),
        mesh=mesh,
        in_specs=(
            P(("row", "col"), None),
            P(("row", "col")),
            P(("row", "col"), None),
            P(("row", "col"), None),
            P(("row", "col"), None),
            P(("row", "col")),
            P("row", "col"),
            P("row", "col"),
            P("col", "row"),
            P(("row", "col")),
            P(("row", "col"), None),
        ),
        out_specs=(
            P(("row", "col"), None),
            P(("row", "col"), None),
            P(("row", "col")),
            P(("row", "col"), None),
            P(("row", "col"), None),
            P(("row", "col"), None),
            P(("row", "col")),
            P("row", "col"),
            P("row", "col"),
            P("col", "row"),
        ),
        check_vma=False,
    )
```

```python
import functools
import math

import jax
import jax.numpy as jnp
from jax import lax
from jax.experimental import pallas as pl
from jax.experimental.pallas import tpu as pltpu
from jax.sharding import PartitionSpec as P

H = 8
DH = 128
WINDOW = 1024
PACK = 2048

EPS = 1e-06
NEGATIVE = -1e30
MESH = pl.DeviceIdType.MESH
BF = jnp.bfloat16
F32 = jnp.float32


def product(left, right):
    return jnp.dot(left, right, preferred_element_type=jnp.float32)


def inner(left, right):
    return lax.dot_general(
        left, right, (((0,), (0,)), ((), ())), preferred_element_type=jnp.float32
    )


def against(left, right):
    return lax.dot_general(
        left, right, (((1,), (1,)), ((), ())), preferred_element_type=jnp.float32
    )


class Place:
    def __init__(self, shape):
        rows, cols = shape
        self.X = math.isqrt(rows)
        while rows % self.X:
            self.X -= 1
        self.Y = rows // self.X
        self.Z = cols // 2
        self.R = rows
        self.row, self.col = lax.axis_index("row"), lax.axis_index("col")
        self.y, self.x = self.row // self.X, self.row % self.X
        self.z, self.core = self.col // 2, self.col % 2
        self.xs, self.ys, self.zs = range(1, self.X), range(1, self.Y), range(1, self.Z)

    def row_at(self, dy=0, dx=0):
        return lax.rem(self.y + dy + self.Y, self.Y) * self.X + lax.rem(
            self.x + dx + self.X, self.X
        )

    def z_at(self, dz):
        return lax.rem(self.z + dz + self.Z, self.Z)

    def device(self, dy=0, dx=0, dz=0, other=False):
        core = 1 - self.core if other else self.core
        return (self.row_at(dy, dx), self.z_at(dz) * 2 + core)

    def greet(self):
        barrier = pltpu.get_barrier_semaphore()
        mates = [self.device(dx=d) for d in self.xs]
        mates += [self.device(dy=d) for d in self.ys]
        mates += [self.device(dz=d) for d in self.zs]
        mates.append(self.device(other=True))
        for mate in mates:
            pl.semaphore_signal(barrier, inc=1, device_id=mate, device_id_type=MESH)
        pl.semaphore_wait(barrier, len(mates))


def remote(src, dst, send, recv, device):
    return pltpu.make_async_remote_copy(
        src_ref=src, dst_ref=dst, send_sem=send, recv_sem=recv, device_id=device,
        device_id_type=MESH,
    )


class Sems:
    def __init__(self, send, recv):
        self.send, self.recv, self.count = send, recv, 0

    def take(self):
        self.count += 1
        return self.send.at[self.count - 1], self.recv.at[self.count - 1]


def gather_count(X, Y, Z):
    return (Z - 1) + Z * ((X - 1) + (Y - 1) + 2 * (X - 1) * (Y - 1))


class Gather:
    def __init__(self, at, here, sems, own):
        self.at, self.p, self.own = at, here, own
        self.sent = []
        p = here
        self.zsem = {k: sems.take() for k in p.zs}
        self.xsem = {(s, d): sems.take() for s in range(p.Z) for d in p.xs}
        self.ysem = {(s, d): sems.take() for s in range(p.Z) for d in p.ys}
        self.dsem = {
            (s, h, dx, dy): sems.take()
            for s in range(p.Z) for h in (0, 1) for dx in p.xs for dy in p.ys
        }

    def push(self, src, dst, sem, device):
        copy = remote(src, dst, sem[0], sem[1], device)
        copy.start()
        self.sent.append(copy)

    def arrive(self, place, sem):
        remote(place, place, sem[0], sem[1], self.p.device(other=True)).wait_recv()

    def spread_z(self):
        p = self.p
        for k in p.zs:
            self.push(self.own, self.at(p.z, p.row, None), self.zsem[k], p.device(dz=-k))

    def spread_xy(self, s):
        p = self.p
        zc = p.z_at(s)
        place = self.at(zc, p.row, None)
        src = self.own
        if s:
            self.arrive(place, self.zsem[s])
            src = place
        for d in p.xs:
            self.push(src, place, self.xsem[s, d], p.device(dx=d))
        for d in p.ys:
            self.push(src, place, self.ysem[s, d], p.device(dy=d))

    def spread_diagonal(self, s):
        p = self.p
        zc = p.z_at(s)
        for d in p.xs:
            r = p.row_at(dx=-d)
            self.arrive(self.at(zc, r, None), self.xsem[s, d])
            half = self.at(zc, r, 0)
            for e in p.ys:
                self.push(half, half, self.dsem[s, 0, d, e], p.device(dy=e))
        for e in p.ys:
            r = p.row_at(dy=-e)
            self.arrive(self.at(zc, r, None), self.ysem[s, e])
            half = self.at(zc, r, 1)
            for d in p.xs:
                self.push(half, half, self.dsem[s, 1, d, e], p.device(dx=d))

    def close(self, s):
        p = self.p
        zc = p.z_at(s)
        for d in p.xs:
            for e in p.ys:
                r = p.row_at(dy=-e, dx=-d)
                for h in (0, 1):
                    self.arrive(self.at(zc, r, h), self.dsem[s, h, d, e])

    def finish(self):
        for copy in self.sent:
            copy.wait_send()


def scatter_count(X, Y, Z):
    return (Z - 1) + Z * (2 * (X - 1) * (Y - 1) + 2 * (X - 1) + 2 * (Y - 1))


class Scatter:
    def __init__(self, part, cut, here, sems, diag, fromx, fromy, sumx, sumy, sumz, fromz):
        self.part, self.cut, self.p = part, cut, here
        self.diag, self.fromx, self.fromy = diag, fromx, fromy
        self.sumx, self.sumy, self.sumz, self.fromz = sumx, sumy, sumz, fromz
        self.sent = []
        p = here
        self.zsem = {k: sems.take() for k in p.zs}
        self.xsem = {(s, h, d): sems.take() for s in range(p.Z) for h in (0, 1) for d in p.xs}
        self.ysem = {(s, h, d): sems.take() for s in range(p.Z) for h in (0, 1) for d in p.ys}
        self.dsem = {
            (s, h, dx, dy): sems.take()
            for s in range(p.Z) for h in (0, 1) for dx in p.xs for dy in p.ys
        }

    def push(self, src, dst, sem, device):
        copy = remote(src, dst, sem[0], sem[1], device)
        copy.start()
        self.sent.append(copy)

    def arrive(self, place, sem):
        remote(place, place, sem[0], sem[1], self.p.device(other=True)).wait_recv()

    def spot(self, d, e):
        return (d - 1) * (self.p.Y - 1) + e - 1

    def first(self, s):
        p, cut = self.p, self.cut
        zc = p.z_at(s)
        for d in p.xs:
            for e in p.ys:
                far = self.part(zc, p.row_at(dy=e, dx=d))
                n = self.spot(d, e)
                self.push(cut(far, 0), self.diag.at[s, 0, n], self.dsem[s, 0, d, e], p.device(dx=d))
                self.push(cut(far, 1), self.diag.at[s, 1, n], self.dsem[s, 1, d, e], p.device(dy=e))
        for d in p.xs:
            near = self.part(zc, p.row_at(dx=d))
            self.push(cut(near, 0), cut(self.fromx.at[s, d - 1], 0), self.xsem[s, 0, d], p.device(dx=d))
        for e in p.ys:
            near = self.part(zc, p.row_at(dy=e))
            self.push(cut(near, 1), cut(self.fromy.at[s, e - 1], 1), self.ysem[s, 1, e], p.device(dy=e))

    def second(self, s):
        p, cut = self.p, self.cut
        zc = p.z_at(s)
        for e in p.ys:
            total = cut(self.part(zc, p.row_at(dy=e)), 0)[...].astype(F32)
            for d in p.xs:
                place = self.diag.at[s, 0, self.spot(d, e)]
                self.arrive(place, self.dsem[s, 0, d, e])
                total = total + place[...].astype(F32)
            self.sumy[s, e - 1] = total.astype(BF)
            self.push(self.sumy.at[s, e - 1], cut(self.fromy.at[s, e - 1], 0), self.ysem[s, 0, e], p.device(dy=e))
        for d in p.xs:
            total = cut(self.part(zc, p.row_at(dx=d)), 1)[...].astype(F32)
            for e in p.ys:
                place = self.diag.at[s, 1, self.spot(d, e)]
                self.arrive(place, self.dsem[s, 1, d, e])
                total = total + place[...].astype(F32)
            self.sumx[s, d - 1] = total.astype(BF)
            self.push(self.sumx.at[s, d - 1], cut(self.fromx.at[s, d - 1], 1), self.xsem[s, 1, d], p.device(dx=d))

    def third(self, s):
        p, cut = self.p, self.cut
        total = self.part(p.z_at(s), p.row)[...].astype(F32)
        for d in p.xs:
            for h in (0, 1):
                self.arrive(cut(self.fromx.at[s, d - 1], h), self.xsem[s, h, d])
            total = total + self.fromx[s, d - 1].astype(F32)
        for e in p.ys:
            for h in (0, 1):
                self.arrive(cut(self.fromy.at[s, e - 1], h), self.ysem[s, h, e])
            total = total + self.fromy[s, e - 1].astype(F32)
        if s:
            self.sumz[s - 1] = total.astype(BF)
            self.push(self.sumz.at[s - 1], self.fromz.at[s - 1], self.zsem[s], p.device(dz=s))
            return None
        for k in p.zs:
            self.arrive(self.fromz.at[k - 1], self.zsem[k])
            total = total + self.fromz[k - 1].astype(F32)
        return total

    def finish(self):
        for copy in self.sent:
            copy.wait_send()


def scatter_scratch(X, Y, Z, block, half):
    return [
        pltpu.VMEM((Z, 2, (X - 1) * (Y - 1)) + half, BF),
        pltpu.VMEM((Z, X - 1) + block, BF),
        pltpu.VMEM((Z, Y - 1) + block, BF),
        pltpu.VMEM((Z, X - 1) + half, BF),
        pltpu.VMEM((Z, Y - 1) + half, BF),
        pltpu.VMEM((Z - 1,) + block, BF),
        pltpu.VMEM((Z - 1,) + block, BF),
    ]


def sides(shape):
    x = math.isqrt(shape[0])
    while shape[0] % x:
        x -= 1
    return x, shape[0] // x, shape[1] // 2


VM = pl.BlockSpec(memory_space=pltpu.VMEM)
ANY = pl.BlockSpec(memory_space=pl.ANY)
DMA = pltpu.SemaphoreType.DMA
LOG2E = math.log2(math.e)
BLOCK = 256


def loop(count, body):
    def step(t, carry):
        body(t)
        return carry

    lax.fori_loop(0, count, step, 0)


def at(t, size):
    return pl.ds(pl.multiple_of(t * size, size), size)


def rms_scale(value):
    return lax.rsqrt(jnp.mean(value * value, axis=-1, keepdims=True) + EPS)


def gelu_parts(gate):
    square = gate * gate
    t = jnp.tanh(gate * (0.7978845608 + (0.7978845608 * 0.044715) * square))
    half = 0.5 + 0.5 * t
    slope = half + (0.5 * gate) * (1.0 - t * t) * (
        0.7978845608 + (3 * 0.7978845608 * 0.044715) * square
    )
    return gate * half, slope


def forward_kernel(shape, with_slab, sizes, *refs):
    D, T, E, W, hz = sizes
    (tokens, cot, marks, slab, ffn,
     output, grad_in, middle, slabs_out, query_out, window_out, bias_out, att_out, lse_out, grads_out,
     slabs, ffns, query, window, values_t, marks_all, bias, att, lse, gains, mlp, mlp_t, cots, cots_t,
     grad_sum, out_sum, hidden, grad_act, stage, out_send,
     asend, arecv, fsend, frecv, csend, crecv, ksend, krecv, xsend, xrecv, lsem, gsem) = refs
    p = Place(shape)
    pack = PACK // T
    spot = lax.rem(p.col, pack)
    QK = E + 2 * DH
    B = T // BLOCK
    span = WINDOW + BLOCK
    loads = []

    def local(src, dst, n):
        copy = pltpu.make_async_copy(src, dst, lsem.at[n])
        copy.start()
        return copy

    barrier = pltpu.get_barrier_semaphore()
    across = (p.row, lax.rem(p.z + 1, 2) + p.z // 2 * 2)
    across = (across[0], across[1] * 2 + 1 - p.core)
    mates = [p.device(dx=d) for d in p.xs] + [p.device(dy=d) for d in p.ys]
    mates += [p.device(dz=d) for d in p.zs] + [p.device(other=True), across]
    for mate in mates:
        pl.semaphore_signal(barrier, inc=1, device_id=mate, device_id_type=MESH)
    load_cot = local(cot, cots.at[pl.ds(0, T)], 0)
    if not with_slab:
        load_slab = local(slab, slabs, 1)
    pl.semaphore_wait(barrier, len(mates))
    mate = p.device(other=True)

    br = ffn.shape[0]

    def ffn_at(zc, r, half):
        if half is None:
            return ffns.at[zc, at(r, br)]
        return ffns.at[zc, pl.ds(pl.multiple_of(r * br + half * (br // 2), br // 2), br // 2)]

    far = Gather(ffn_at, p, Sems(fsend, frecv), ffn)

    if with_slab:
        ar = slab.shape[0]

        def slab_row(r, zc, core):
            return ((r * p.Z + zc) * 2 + core) * ar

        def slab_at(zc, r, half):
            if half is None:
                return slabs.at[pl.ds(pl.multiple_of(slab_row(r, zc, p.core), ar), ar)]
            return slabs.at[
                pl.ds(pl.multiple_of(slab_row(r, zc, p.core) + half * (ar // 2), ar // 2), ar // 2)
            ]

        near = Gather(slab_at, p, Sems(asend, arecv), slab)
        near.spread_z()
        near.spread_xy(0)

    load_cot.wait()
    cot_copy = remote(cots.at[pl.ds(0, T)], cots.at[pl.ds(T, T)], xsend.at[0], xrecv.at[0], mate)
    cot_copy.start()
    marks_all[:, pl.ds(2 * T, T)] = marks[...]

    @pl.when(spot == 0)
    def _():
        window[pl.ds(0, 2 * T), :] = jnp.zeros((2 * T, 2 * DH), BF)
        marks_all[:, pl.ds(0, 2 * T)] = jnp.full((8, 2 * T), -1.0, F32)

    @pl.when(spot == 1)
    def _():
        window[pl.ds(0, T), :] = jnp.zeros((T, 2 * DH), BF)
        marks_all[:, pl.ds(0, T)] = jnp.full((8, T), -1.0, F32)

    def behind(src, place, n, op):
        for d in (1, 2):
            to = (p.row, lax.rem(p.col + d, 2 * p.Z))
            copy = remote(src, place(2 - d), ksend.at[n + d], krecv.at[n + d], to)
            if op == "start":
                pl.when(spot + d < pack)(copy.start)
            elif op == "arrive":
                pl.when(spot - d >= 0)(copy.wait_recv)
            else:
                pl.when(spot + d < pack)(copy.wait_send)

    mark_place = lambda k: marks_all.at[:, pl.ds(k * T, T)]
    mark_own = mark_place(2)
    behind(mark_own, mark_place, 0, "start")
    if with_slab:
        slabs[pl.ds(pl.multiple_of(slab_row(p.row, p.z, p.core), ar), ar)] = slab[...]
    ffns[p.z, at(p.row, br)] = ffn[...]

    def turn_cot(t):
        cots_t[:, at(t, BLOCK)] = cots[at(t, BLOCK)].T

    loop(B, turn_cot)
    if with_slab:
        for s in range(p.Z):
            if s + 1 < p.Z:
                near.spread_xy(s + 1)
            near.spread_diagonal(s)
        far.spread_z()
        far.spread_xy(0)
        passed = []
        n = 0
        for s in range(p.Z):
            near.close(s)
            zc = p.z_at(s)
            for dy in range(p.Y):
                for dx in range(p.X):
                    r = p.row_at(dy, dx)
                    place = slab_at(zc, r, None)
                    copy = remote(place, place, csend.at[n], crecv.at[n], mate)
                    copy.start()
                    theirs = slabs.at[pl.ds(pl.multiple_of(slab_row(r, zc, 1 - p.core), ar), ar)]
                    passed.append((copy, remote(theirs, theirs, csend.at[n], crecv.at[n], mate)))
                    n += 1
        cot_copy.wait()
        loop(B, lambda t: turn_cot(t + B))
        for copy, arrival in passed:
            copy.wait_send()
            arrival.wait_recv()
    else:
        far.spread_z()
        far.spread_xy(0)
        cot_copy.wait()
        loop(B, lambda t: turn_cot(t + B))
        load_slab.wait()
    save_slabs = local(slabs, slabs_out, 1)
    gains[...] = slabs[:, QK + E :].astype(F32).T[0:8]

    def first_norm(t):
        rows = at(t, 64)
        value = tokens[rows].astype(F32)
        mlp[rows] = (value * rms_scale(value) * gains[0:1]).astype(BF)

    loop(T // 64, first_norm)
    window[pl.ds(2 * T, T)] = product(mlp[pl.ds(0, T)], slabs[:, E : E + 2 * DH]).astype(BF)
    key_place = lambda k: window.at[pl.ds(k * T, T)]
    behind(key_place(2), key_place, 3, "start")

    def project(t):
        query[at(t, BLOCK)] = product(mlp[at(t, BLOCK)], slabs[:, 0:E]).astype(BF)

    loop(B, project)
    if p.Z > 1:
        far.spread_xy(1)
    save_query = local(query, query_out, 2)
    behind(mark_own, mark_place, 0, "arrive")
    column = jnp.broadcast_to(marks_all[0:1], (128, 3 * T)).T
    for i in range(B):
        keys_at = jnp.concatenate([column[i * BLOCK : i * BLOCK + span]] * (BLOCK // 128), axis=1)
        own = marks_all[0:1, 2 * T + i * BLOCK : 2 * T + (i + 1) * BLOCK]
        gap = (
            WINDOW
            + lax.broadcasted_iota(jnp.int32, (span, BLOCK), 1)
            - lax.broadcasted_iota(jnp.int32, (span, BLOCK), 0)
        )
        allowed = (keys_at == own) & (gap >= 0) & (gap < WINDOW)
        bias[i] = jnp.where(allowed, 0.0, NEGATIVE)
    save_bias = local(bias, bias_out, 3)
    behind(key_place(2), key_place, 3, "arrive")
    save_window = local(window, window_out, 4)
    values_t[...] = window[:, DH:].T
    factor = LOG2E / math.sqrt(DH)

    def head(i, h):
        lanes = at(h, DH)
        keys = window[pl.ds(i * BLOCK, span), 0:DH]
        scores = against(keys, query[pl.ds(i * BLOCK, BLOCK), lanes]) * factor + bias[i]
        top = jnp.max(scores, axis=0, keepdims=True)
        expo = jnp.exp2(scores - top)
        total = jnp.sum(expo, axis=0, keepdims=True)
        mixed = product(values_t[:, pl.ds(i * BLOCK, span)], expo.astype(BF))
        att[lanes, pl.ds(i * BLOCK, BLOCK)] = (mixed / total).astype(BF)
        lse[h * B + i] = jnp.broadcast_to(top + jnp.log2(total), (8, BLOCK))

    far.spread_diagonal(0)
    for i in range(B):
        loop(H // 2, lambda h: head(i, h))
        if i == 0 and p.Z > 2:
            far.spread_xy(2)
        loop(H // 2, lambda h: head(i, h + H // 2))
        if i == 0 and p.Z > 1:
            far.spread_diagonal(1)
    save_att = local(att, att_out, 5)
    save_lse = local(lse, lse_out, 6)

    def out_project(t):
        cols = at(t, BLOCK)
        middle[cols] = product(att[:, cols].T, slabs[:, QK : QK + E]) + tokens[cols].astype(F32)

    loop(B, out_project)

    def second_norm(t):
        rows = at(t, 64)
        value = middle[rows]
        mlp[rows] = (value * rms_scale(value) * gains[1:2]).astype(BF)

    loop(T // 64, second_norm)
    mlp_copy = remote(mlp.at[pl.ds(0, T)], mlp.at[pl.ds(T, T)], xsend.at[1], xrecv.at[1], mate)
    mlp_copy.start()

    def turn_mlp(t):
        mlp_t[:, at(t, BLOCK)] = mlp[at(t, BLOCK)].T

    loop(B, turn_mlp)
    if p.Z > 3:
        far.spread_xy(3)
    mlp_copy.wait()
    loop(B, lambda t: turn_mlp(t + B))
    for s in range(4, p.Z):
        far.spread_xy(s)

    saves = []
    for s in range(p.Z):
        zc = p.z_at(s)
        if s + 2 < p.Z:
            far.spread_diagonal(s + 2)
        far.close(s)
        slot = s % 2

        def tile(t):
            rows = at(t, BLOCK)
            gate_up = product(mlp[rows], ffns[zc, :, 0 : 2 * hz])
            grad_hidden = product(cots[rows], ffns[zc, :, 2 * hz :])
            up = gate_up[:, hz:]
            act, slope = gelu_parts(gate_up[:, :hz])
            hid = (act * up).astype(BF)
            hidden[rows] = hid
            grad_gate = (grad_hidden * up * slope).astype(BF)
            grad_up = (grad_hidden * act).astype(BF)
            grad_act[rows, 0:hz] = grad_gate
            grad_act[rows, hz : 2 * hz] = grad_up
            outs = against(hid, ffns[zc, :, 2 * hz :])
            grads = against(grad_act[rows], ffns[zc, :, 0 : 2 * hz])
            if s == 0:
                out_sum[rows] = outs
                grad_sum[rows] = grads
            else:
                out_sum[rows] += outs
                grad_sum[rows] += grads

        loop(2 * B, tile)
        if s > 1:
            saves[s - 2].wait()

        def weight_tile(t):
            rows = at(t, BLOCK)
            stage[slot, rows, 0 : 2 * hz] = product(mlp_t[rows], grad_act[...]).astype(BF)
            stage[slot, rows, 2 * hz :] = product(cots_t[rows], hidden[...]).astype(BF)

        loop(D // BLOCK, weight_tile)
        save = pltpu.make_async_copy(stage.at[slot], grads_out.at[zc], gsem.at[s])
        save.start()
        saves.append(save)

    grad_copy = remote(grad_sum.at[pl.ds(T, T)], grad_in, xsend.at[2], xrecv.at[2], mate)
    grad_copy.start()

    def narrow(t):
        out_send[at(t, 64)] = out_sum[pl.ds(pl.multiple_of(T + t * 64, 64), 64)].astype(BF)

    loop(T // 64, narrow)
    out_copy = remote(out_send, output, xsend.at[3], xrecv.at[3], mate)
    out_copy.start()
    for save in saves[max(0, p.Z - 2) :]:
        save.wait()
    for save in (save_slabs, save_query, save_bias, save_window, save_att, save_lse):
        save.wait()
    behind(mark_own, mark_place, 0, "sent")
    behind(key_place(2), key_place, 3, "sent")
    if with_slab:
        near.finish()
    far.finish()
    grad_copy.wait()

    def join(t):
        rows = at(t, 64)
        grad_in[rows] = grad_in[rows] + grad_sum[rows]

    loop(T // 64, join)
    out_copy.wait()

    def join_out(t):
        rows = at(t, 64)
        output[rows] = (middle[rows] + out_sum[rows] + output[rows].astype(F32)).astype(BF)

    loop(T // 64, join_out)


def forward(shape, with_slab, tokens, cot, marks, slab, ffn):
    X, Y, Z = sides(shape)
    T, D = tokens.shape
    E, hz = H * DH, ffn.shape[1] // 3
    W = slab.shape[1]
    B = T // BLOCK
    span = WINDOW + BLOCK
    n = gather_count(X, Y, Z)
    S = jax.ShapeDtypeStruct
    outs = [
        S((T, D), BF), S((T, D), F32), S((T, D), F32),
        S((D, W), BF), S((T, E), BF), S((3 * T, 2 * DH), BF), S((B, span, BLOCK), F32),
        S((E, T), BF), S((H * B, 8, BLOCK), F32), S((Z, D, 3 * hz), BF),
    ]
    V = pltpu.VMEM
    scratch = [
        V((D, W), BF), V((Z, D, 3 * hz), BF), V((T, E), BF), V((3 * T, 2 * DH), BF),
        V((DH, 3 * T), BF), V((8, 3 * T), F32), V((B, span, BLOCK), F32), V((E, T), BF),
        V((H * B, 8, BLOCK), F32), V((8, D), F32), V((2 * T, D), BF), V((D, 2 * T), BF),
        V((2 * T, D), BF), V((D, 2 * T), BF), V((2 * T, D), F32), V((2 * T, D), F32),
        V((2 * T, hz), BF), V((2 * T, 2 * hz), BF), V((2, D, 3 * hz), BF), V((T, D), BF),
        DMA((n,)), DMA((n,)), DMA((n,)), DMA((n,)),
        DMA((shape[0] * Z,)), DMA((shape[0] * Z,)), DMA((6,)), DMA((6,)), DMA((4,)), DMA((4,)),
        DMA((7,)), DMA((Z,)),
    ]
    return pl.pallas_call(
        functools.partial(forward_kernel, shape, with_slab, (D, T, E, W, hz)),
        out_shape=outs,
        in_specs=[VM, ANY, VM, VM if with_slab else ANY, VM],
        out_specs=[VM] * 3 + [ANY] * 7,
        scratch_shapes=scratch,
        compiler_params=pltpu.CompilerParams(
            collective_id=0, has_side_effects=True, vmem_limit_bytes=62 << 20
        ),
        name="forward",
    )(tokens, cot, marks, slab, ffn)


def scatter_kernel(shape, with_slab, *refs):
    if with_slab:
        slabs, ffns, slab_out, ffn_out = refs[:4]
        scratch = refs[4:]
        fwork, awork = scratch[:7], scratch[7:14]
        plane, crossed, fsend, frecv, asend, arecv, csem = scratch[14:]
    else:
        ffns, ffn_out = refs[:2]
        fwork = refs[2:9]
        fsend, frecv = refs[9:]
    p = Place(shape)
    p.greet()
    br = ffns.shape[3]

    far = Scatter(
        lambda zc, r: ffns.at[zc, :, r],
        lambda ref, h: ref.at[:, pl.ds(h * (br // 2), br // 2)],
        p, Sems(fsend, frecv), *fwork,
    )
    order = list(range(1, p.Z)) + [0]
    if with_slab:
        ar = slabs.shape[3]
        cross = remote(
            slabs.at[:, :, 1 - p.core], crossed, csem.at[0], csem.at[1], p.device(other=True)
        )
        cross.start()
    for s in order:
        far.first(s)
    if with_slab:
        cross.wait()

        def fold(n, carry):
            r, zc = n // p.Z, n % p.Z
            mine = slabs[r, zc, p.core].astype(F32) + crossed[r, zc].astype(F32)
            plane[r, zc] = mine.astype(BF)
            return carry

        lax.fori_loop(0, p.R * p.Z, fold, 0)
        near = Scatter(
            lambda zc, r: plane.at[r, zc],
            lambda ref, h: ref.at[pl.ds(h * (ar // 2), ar // 2)],
            p, Sems(asend, arecv), *awork,
        )
        for s in order:
            near.first(s)
    for s in order:
        far.second(s)
    if with_slab:
        for s in order:
            near.second(s)
    for s in order:
        total = far.third(s)
    ffn_out[...] = total
    if with_slab:
        for s in order:
            total = near.third(s)
        slab_out[...] = total
        near.finish()
    far.finish()


def scatter_grads(shape, slabs, ffns):
    X, Y, Z = sides(shape)
    R = shape[0]
    n = scatter_count(X, Y, Z)
    with_slab = slabs is not None
    block = (3,) + ffns.shape[3:]
    half = (3, ffns.shape[3] // 2, ffns.shape[4])
    outs = [jax.ShapeDtypeStruct(block, F32)]
    args = [ffns]
    scratch = scatter_scratch(X, Y, Z, block, half)
    if with_slab:
        ablock = slabs.shape[3:]
        ahalf = (ablock[0] // 2, ablock[1])
        outs = [jax.ShapeDtypeStruct(ablock, F32)] + outs
        args = [slabs] + args
        scratch += scatter_scratch(X, Y, Z, ablock, ahalf)
        scratch += [pltpu.VMEM((R, Z) + ablock, BF)] * 2
    scratch += [DMA((n,)), DMA((n,))]
    if with_slab:
        scratch += [DMA((n,)), DMA((n,)), DMA((2,))]
    return pl.pallas_call(
        functools.partial(scatter_kernel, shape, with_slab),
        out_shape=outs,
        in_specs=[VM] * len(args),
        out_specs=[VM] * len(outs),
        scratch_shapes=scratch,
        compiler_params=pltpu.CompilerParams(
            collective_id=1, has_side_effects=True, vmem_limit_bytes=60 << 20
        ),
        name="scatter_grads",
    )(*args)


def from_behind(block, axis, distance):
    devices = range(lax.axis_size(axis))
    route = [(i - distance, i) for i in devices if i - distance in devices]
    return lax.ppermute(block, axis, route)


def swap(block):
    return lax.ppermute(block, "col", [(i, i ^ 1) for i in range(lax.axis_size("col"))])


def gated(gate, up):
    return jax.nn.gelu(gate, approximate=True) * up


def norm_back(grad_normed, value, scale):
    return scale * grad_normed - value * scale**3 * jnp.mean(
        grad_normed * value, axis=-1, keepdims=True
    )


def shards(
    shape,
    tokens, gain_attn, w_query, w_keyval, w_out, gain_mlp, w_gate, w_up, w_down, segment, cotangent
):
    R, C = shape
    D = tokens.shape[1]
    with_slab = w_query.shape[0] % 32 == 0
    ffn = jnp.concatenate([w_gate, w_up, w_down.T], axis=1)
    slab = jnp.concatenate(
        [w_query, w_keyval, w_out,
         jnp.pad(jnp.stack([gain_attn, gain_mlp], axis=1), ((0, 0), (0, 126)))], axis=1)
    W = slab.shape[1]
    Z = C // 2
    E = H * DH
    if not with_slab:
        slab = lax.all_gather(slab, ("row", "col"), axis=0, tiled=True)
    marks = jnp.broadcast_to(segment.astype(F32)[None], (8, segment.shape[0]))
    (output, grad_mlp_in, middle, slabs, query, keys_all, bias, att, lse, weight_grads) = forward(
        shape, with_slab, tokens, cotangent, marks, slab, ffn)
    query_weight = slabs[:, :E]
    keyval_weight = slabs[:, E : E + 2 * DH]
    out_weight = slabs[:, E + 2 * DH : 2 * E + 2 * DH]
    gain_first = slabs[:, 2 * E + 2 * DH].astype(F32)
    gain_second = slabs[:, 2 * E + 2 * DH + 1].astype(F32)
    rows = tokens.shape[0]
    reach = WINDOW // rows
    inputs = tokens.astype(jnp.float32)
    scale_first = lax.rsqrt(jnp.mean(inputs * inputs, axis=-1, keepdims=True) + EPS)
    normed_first = inputs * scale_first
    attn_in = (normed_first * gain_first).astype(jnp.bfloat16)
    scale_second = lax.rsqrt(jnp.mean(middle * middle, axis=-1, keepdims=True) + EPS)
    normed_second = middle * scale_second
    attended = att.T
    keys, values = keys_all[:, :DH], keys_all[:, DH:]
    group = 2
    blocks = H // group
    scale = 1.0 / math.sqrt(DH)
    query_groups = query.reshape(rows, blocks, group, DH).transpose(1, 2, 0, 3)
    full = jnp.full((rows, 3 * rows), NEGATIVE, F32)
    for i in range(rows // BLOCK):
        full = full.at[i * BLOCK : (i + 1) * BLOCK, i * BLOCK : i * BLOCK + WINDOW + BLOCK].set(bias[i].T)
    allowed = full == 0.0
    logsum = lse[:, 0].reshape(blocks, group, rows)[..., None] / LOG2E

    def scores_of(part):
        scores = jnp.einsum("gqd,kd->gqk", part, keys, preferred_element_type=jnp.float32) * scale
        return jnp.where(allowed[None], scores, NEGATIVE)

    weight_grads = weight_grads.reshape(Z, R, D // R, 3, -1).transpose(0, 3, 1, 2, 4)
    grad_outputs = cotangent.astype(jnp.float32)
    gain_second_grad = jnp.sum(grad_mlp_in * normed_second, axis=0)
    grad_middle = grad_outputs + norm_back(grad_mlp_in * gain_second, middle, scale_second)
    grad_branch = grad_middle.astype(jnp.bfloat16)
    out_grad = inner(attended, grad_branch)
    grad_attended = against(grad_branch, out_weight).astype(jnp.bfloat16)
    grad_groups = grad_attended.reshape(rows, blocks, group, DH).transpose(1, 2, 0, 3)

    def backward_group(item):
        part, grad_part, logs = item
        scores = scores_of(part)
        probs = jnp.where(allowed[None], jnp.exp(scores - logs), 0.0)
        grad_probs = jnp.einsum(
            "gqd,kd->gqk", grad_part, values, preferred_element_type=jnp.float32
        )
        centre = jnp.sum(probs * grad_probs, axis=-1, keepdims=True)
        grad_scores = (probs * (grad_probs - centre)).astype(jnp.bfloat16)
        grad_part_query = (
            jnp.einsum("gqk,kd->gqd", grad_scores, keys, preferred_element_type=jnp.float32) * scale
        )
        grad_keys = (
            jnp.einsum("gqk,gqd->kd", grad_scores, part, preferred_element_type=jnp.float32) * scale
        )
        grad_values = jnp.einsum(
            "gqk,gqd->kd", probs.astype(jnp.bfloat16), grad_part, preferred_element_type=jnp.float32
        )
        return (grad_part_query, grad_keys, grad_values)

    query_parts, key_parts, value_parts = lax.map(
        backward_group, (query_groups, grad_groups, logsum)
    )
    grad_query_act = query_parts.transpose(2, 0, 1, 3).reshape(rows, H * DH).astype(jnp.bfloat16)
    grad_keyval_all = jnp.concatenate(
        [jnp.sum(key_parts, axis=0), jnp.sum(value_parts, axis=0)], axis=1
    )
    grad_own = grad_keyval_all[reach * rows :]
    for offset in range(1, reach + 1):
        sent = grad_keyval_all[(reach - offset) * rows : (reach - offset + 1) * rows]
        grad_own = grad_own + from_behind(sent.astype(jnp.bfloat16), "col", -offset).astype(
            sent.dtype
        )
    grad_keyval_act = grad_own.astype(jnp.bfloat16)
    grad_attn_in = against(grad_query_act, query_weight) + against(grad_keyval_act, keyval_weight)
    query_grad = inner(attn_in, grad_query_act)
    keyval_grad = inner(attn_in, grad_keyval_act)
    gain_first_grad = jnp.sum(grad_attn_in * normed_first, axis=0)
    grad_inputs = grad_middle + norm_back(grad_attn_in * gain_first, inputs, scale_first)

    gains = jnp.pad(jnp.stack([gain_first_grad, gain_second_grad], axis=1), ((0, 0), (0, 126)))
    slab_grads = jnp.concatenate([query_grad, keyval_grad, out_grad, gains], axis=1)
    if with_slab:
        slab_grad, ffn_grad = scatter_grads(
            shape, slab_grads.astype(BF).reshape((R, Z, 2, D // (R * C), W)), weight_grads
        )
    else:
        slab_grad = lax.psum_scatter(slab_grads, ("row", "col"), scatter_dimension=0, tiled=True)
        (ffn_grad,) = scatter_grads(shape, None, weight_grads)
    return (
        output,
        grad_inputs,
        slab_grad[:, 2 * E + 2 * DH],
        slab_grad[:, :E],
        slab_grad[:, E : E + 2 * DH],
        slab_grad[:, E + 2 * DH : 2 * E + 2 * DH],
        slab_grad[:, 2 * E + 2 * DH + 1],
        ffn_grad[0],
        ffn_grad[1],
        ffn_grad[2].T,
    )


def solution(mesh):
    shape = (mesh.shape["row"], mesh.shape["col"])
    return jax.shard_map(
        functools.partial(shards, shape),
        mesh=mesh,
        in_specs=(
            P(("row", "col"), None),
            P(("row", "col")),
            P(("row", "col"), None),
            P(("row", "col"), None),
            P(("row", "col"), None),
            P(("row", "col")),
            P("row", "col"),
            P("row", "col"),
            P("col", "row"),
            P(("row", "col")),
            P(("row", "col"), None),
        ),
        out_specs=(
            P(("row", "col"), None),
            P(("row", "col"), None),
            P(("row", "col")),
            P(("row", "col"), None),
            P(("row", "col"), None),
            P(("row", "col"), None),
            P(("row", "col")),
            P("row", "col"),
            P("row", "col"),
            P("col", "row"),
        ),
        check_vma=False,
    )
```

```python
import functools
import math

import jax
import jax.numpy as jnp
from jax import lax
from jax.experimental import pallas as pl
from jax.experimental.pallas import tpu as pltpu
from jax.sharding import PartitionSpec as P

H = 8
DH = 128
WINDOW = 1024
PACK = 2048

EPS = 1e-06
NEGATIVE = -1e30
MESH = pl.DeviceIdType.MESH
BF = jnp.bfloat16
F32 = jnp.float32


def product(left, right):
    return jnp.dot(left, right, preferred_element_type=jnp.float32)


def against(left, right):
    return lax.dot_general(
        left, right, (((1,), (1,)), ((), ())), preferred_element_type=jnp.float32
    )


class Place:
    def __init__(self, shape):
        rows, cols = shape
        self.X = math.isqrt(rows)
        while rows % self.X:
            self.X -= 1
        self.Y = rows // self.X
        self.Z = cols // 2
        self.R = rows
        self.row, self.col = lax.axis_index("row"), lax.axis_index("col")
        self.y, self.x = self.row // self.X, self.row % self.X
        self.z, self.core = self.col // 2, self.col % 2
        self.xs, self.ys, self.zs = range(1, self.X), range(1, self.Y), range(1, self.Z)

    def row_at(self, dy=0, dx=0):
        return lax.rem(self.y + dy + self.Y, self.Y) * self.X + lax.rem(
            self.x + dx + self.X, self.X
        )

    def z_at(self, dz):
        return lax.rem(self.z + dz + self.Z, self.Z)

    def device(self, dy=0, dx=0, dz=0, other=False):
        core = 1 - self.core if other else self.core
        return (self.row_at(dy, dx), self.z_at(dz) * 2 + core)


def remote(src, dst, send, recv, device):
    return pltpu.make_async_remote_copy(
        src_ref=src, dst_ref=dst, send_sem=send, recv_sem=recv, device_id=device,
        device_id_type=MESH,
    )


class Sems:
    def __init__(self, send, recv):
        self.send, self.recv, self.count = send, recv, 0

    def take(self):
        self.count += 1
        return self.send.at[self.count - 1], self.recv.at[self.count - 1]


def gather_count(X, Y, Z):
    return (Z - 1) + Z * ((X - 1) + (Y - 1) + 2 * (X - 1) * (Y - 1))


class Gather:
    def __init__(self, at, here, sems, own):
        self.at, self.p, self.own = at, here, own
        self.sent = []
        p = here
        self.zsem = {k: sems.take() for k in p.zs}
        self.xsem = {(s, d): sems.take() for s in range(p.Z) for d in p.xs}
        self.ysem = {(s, d): sems.take() for s in range(p.Z) for d in p.ys}
        self.dsem = {
            (s, h, dx, dy): sems.take()
            for s in range(p.Z) for h in (0, 1) for dx in p.xs for dy in p.ys
        }

    def push(self, src, dst, sem, device):
        copy = remote(src, dst, sem[0], sem[1], device)
        copy.start()
        self.sent.append(copy)

    def arrive(self, place, sem):
        remote(place, place, sem[0], sem[1], self.p.device(other=True)).wait_recv()

    def spread_z(self):
        p = self.p
        for k in p.zs:
            self.push(self.own, self.at(p.z, p.row, None), self.zsem[k], p.device(dz=-k))

    def spread_xy(self, s):
        p = self.p
        zc = p.z_at(s)
        place = self.at(zc, p.row, None)
        src = self.own
        if s:
            self.arrive(place, self.zsem[s])
            src = place
        for d in p.xs:
            self.push(src, place, self.xsem[s, d], p.device(dx=d))
        for d in p.ys:
            self.push(src, place, self.ysem[s, d], p.device(dy=d))

    def spread_diagonal(self, s):
        p = self.p
        zc = p.z_at(s)
        for d in p.xs:
            r = p.row_at(dx=-d)
            self.arrive(self.at(zc, r, None), self.xsem[s, d])
            half = self.at(zc, r, 0)
            for e in p.ys:
                self.push(half, half, self.dsem[s, 0, d, e], p.device(dy=e))
        for e in p.ys:
            r = p.row_at(dy=-e)
            self.arrive(self.at(zc, r, None), self.ysem[s, e])
            half = self.at(zc, r, 1)
            for d in p.xs:
                self.push(half, half, self.dsem[s, 1, d, e], p.device(dx=d))

    def close(self, s):
        p = self.p
        zc = p.z_at(s)
        for d in p.xs:
            for e in p.ys:
                r = p.row_at(dy=-e, dx=-d)
                for h in (0, 1):
                    self.arrive(self.at(zc, r, h), self.dsem[s, h, d, e])

    def finish(self):
        for copy in self.sent:
            copy.wait_send()


def scatter_count(X, Y, Z):
    return (Z - 1) + Z * (2 * (X - 1) * (Y - 1) + 2 * (X - 1) + 2 * (Y - 1))


class Scatter:
    def __init__(self, part, cut, here, sems, termx, termy, own, diag, fromx, fromy, fromz):
        self.part, self.cut, self.p = part, cut, here
        self.termx, self.termy, self.own = termx, termy, own
        self.diag, self.fromx, self.fromy, self.fromz = diag, fromx, fromy, fromz
        self.sent = []
        p = here
        self.zsem = {k: sems.take() for k in p.zs}
        self.xsem = {(s, h, d): sems.take() for s in range(p.Z) for h in (0, 1) for d in p.xs}
        self.ysem = {(s, h, d): sems.take() for s in range(p.Z) for h in (0, 1) for d in p.ys}
        self.dsem = {
            (s, h, dx, dy): sems.take()
            for s in range(p.Z) for h in (0, 1) for dx in p.xs for dy in p.ys
        }

    def push(self, src, dst, sem, device):
        copy = remote(src, dst, sem[0], sem[1], device)
        copy.start()
        self.sent.append(copy)

    def arrive(self, place, sem):
        remote(place, place, sem[0], sem[1], self.p.device(other=True)).wait_recv()

    def spot(self, d, e):
        return (d - 1) * (self.p.Y - 1) + e - 1

    def first(self, s):
        p, cut = self.p, self.cut
        zc = p.z_at(s)
        for d in p.xs:
            for e in p.ys:
                far = self.part(zc, p.row_at(dy=e, dx=d))
                n = self.spot(d, e)
                self.push(cut(far, 0), self.diag.at[s, 0, n], self.dsem[s, 0, d, e], p.device(dx=d))
                self.push(cut(far, 1), self.diag.at[s, 1, n], self.dsem[s, 1, d, e], p.device(dy=e))
        for d in p.xs:
            near = self.part(zc, p.row_at(dx=d))
            self.push(cut(near, 0), cut(self.fromx.at[s, d - 1], 0), self.xsem[s, 0, d], p.device(dx=d))
        for e in p.ys:
            near = self.part(zc, p.row_at(dy=e))
            self.push(cut(near, 1), cut(self.fromy.at[s, e - 1], 1), self.ysem[s, 1, e], p.device(dy=e))

    def second(self, s):
        p, cut = self.p, self.cut
        for e in p.ys:
            term = self.termy(s, e)
            total = term[...].astype(F32)
            for d in p.xs:
                place = self.diag.at[s, 0, self.spot(d, e)]
                self.arrive(place, self.dsem[s, 0, d, e])
                total = total + place[...].astype(F32)
            term[...] = total.astype(BF)
            self.push(term, cut(self.fromy.at[s, e - 1], 0), self.ysem[s, 0, e], p.device(dy=e))
        for d in p.xs:
            term = self.termx(s, d)
            total = term[...].astype(F32)
            for e in p.ys:
                place = self.diag.at[s, 1, self.spot(d, e)]
                self.arrive(place, self.dsem[s, 1, d, e])
                total = total + place[...].astype(F32)
            term[...] = total.astype(BF)
            self.push(term, cut(self.fromx.at[s, d - 1], 1), self.xsem[s, 1, d], p.device(dx=d))

    def third(self, s, out=None):
        p, cut = self.p, self.cut
        own = self.own(s)
        total = own[...].astype(F32)
        for d in p.xs:
            for h in (0, 1):
                self.arrive(cut(self.fromx.at[s, d - 1], h), self.xsem[s, h, d])
            total = total + self.fromx[s, d - 1].astype(F32)
        for e in p.ys:
            for h in (0, 1):
                self.arrive(cut(self.fromy.at[s, e - 1], h), self.ysem[s, h, e])
            total = total + self.fromy[s, e - 1].astype(F32)
        if s:
            own[...] = total.astype(BF)
            self.push(own, self.fromz.at[s - 1], self.zsem[s], p.device(dz=s))
            return
        for k in p.zs:
            self.arrive(self.fromz.at[k - 1], self.zsem[k])
            total = total + self.fromz[k - 1].astype(F32)
        out[...] = total

    def finish(self):
        for copy in self.sent:
            copy.wait_send()


def scatter_scratch(X, Y, Z, block):
    half = (block[0] // 2, block[1])
    return [
        pltpu.VMEM((Z, 2, (X - 1) * (Y - 1)) + half, BF),
        pltpu.VMEM((Z, X - 1) + block, BF),
        pltpu.VMEM((Z, Y - 1) + block, BF),
        pltpu.VMEM((Z - 1,) + block, BF),
    ]


def sides(shape):
    x = math.isqrt(shape[0])
    while shape[0] % x:
        x -= 1
    return x, shape[0] // x, shape[1] // 2


VM = pl.BlockSpec(memory_space=pltpu.VMEM)
ANY = pl.BlockSpec(memory_space=pl.ANY)
DMA = pltpu.SemaphoreType.DMA
LOG2E = math.log2(math.e)
BLOCK = 256


def loop(count, body):
    def step(t, carry):
        body(t)
        return carry

    lax.fori_loop(0, count, step, 0)


def at(t, size):
    return pl.ds(pl.multiple_of(t * size, size), size)


def rms_scale(value):
    return lax.rsqrt(jnp.mean(value * value, axis=-1, keepdims=True) + EPS)


def gelu_parts(gate):
    square = gate * gate
    t = jnp.tanh(gate * (0.7978845608 + (0.7978845608 * 0.044715) * square))
    half = 0.5 + 0.5 * t
    slope = half + (0.5 * gate) * (1.0 - t * t) * (
        0.7978845608 + (3 * 0.7978845608 * 0.044715) * square
    )
    return gate * half, slope


def forward_kernel(shape, with_slab, sizes, *refs):
    D, T, E, W, hz = sizes
    (tokens, cot, marks, slab, ffn,
     output, grad_in, middle, slabs_out, query_out, window_out, bias_out, att_out, lse_out, grads_out,
     slabs, ffns, query, window, values_t, marks_all, bias, att, lse, gains, mlp, mlp_t, cots, cots_t,
     grad_sum, out_sum, hidden, grad_act, stage, out_send,
     asend, arecv, fsend, frecv, csend, crecv, ksend, krecv, xsend, xrecv, lsem, gsem) = refs
    p = Place(shape)
    pack = PACK // T
    spot = lax.rem(p.col, pack)
    QK = E + 2 * DH
    B = T // BLOCK
    span = WINDOW + BLOCK
    loads = []

    def local(src, dst, n):
        copy = pltpu.make_async_copy(src, dst, lsem.at[n])
        copy.start()
        return copy

    barrier = pltpu.get_barrier_semaphore()
    across = (p.row, lax.rem(p.z + 1, 2) + p.z // 2 * 2)
    across = (across[0], across[1] * 2 + 1 - p.core)
    mates = [p.device(dx=d) for d in p.xs] + [p.device(dy=d) for d in p.ys]
    mates += [p.device(dz=d) for d in p.zs] + [p.device(other=True), across]
    for mate in mates:
        pl.semaphore_signal(barrier, inc=1, device_id=mate, device_id_type=MESH)
    load_cot = local(cot, cots.at[pl.ds(0, T)], 0)
    if not with_slab:
        load_slab = local(slab, slabs, 1)
    pl.semaphore_wait(barrier, len(mates))
    mate = p.device(other=True)

    br = ffn.shape[0]

    def ffn_at(zc, r, half):
        if half is None:
            return ffns.at[zc, at(r, br)]
        return ffns.at[zc, pl.ds(pl.multiple_of(r * br + half * (br // 2), br // 2), br // 2)]

    far = Gather(ffn_at, p, Sems(fsend, frecv), ffn)

    if with_slab:
        ar = slab.shape[0]

        def slab_row(r, zc, core):
            return ((r * p.Z + zc) * 2 + core) * ar

        def slab_at(zc, r, half):
            if half is None:
                return slabs.at[pl.ds(pl.multiple_of(slab_row(r, zc, p.core), ar), ar)]
            return slabs.at[
                pl.ds(pl.multiple_of(slab_row(r, zc, p.core) + half * (ar // 2), ar // 2), ar // 2)
            ]

        near = Gather(slab_at, p, Sems(asend, arecv), slab)
        near.spread_z()
        near.spread_xy(0)

    load_cot.wait()
    cot_copy = remote(cots.at[pl.ds(0, T)], cots.at[pl.ds(T, T)], xsend.at[0], xrecv.at[0], mate)
    cot_copy.start()
    marks_all[:, pl.ds(2 * T, T)] = marks[...]

    @pl.when(spot == 0)
    def _():
        window[pl.ds(0, 2 * T), :] = jnp.zeros((2 * T, 2 * DH), BF)
        marks_all[:, pl.ds(0, 2 * T)] = jnp.full((8, 2 * T), -1.0, F32)

    @pl.when(spot == 1)
    def _():
        window[pl.ds(0, T), :] = jnp.zeros((T, 2 * DH), BF)
        marks_all[:, pl.ds(0, T)] = jnp.full((8, T), -1.0, F32)

    def behind(src, place, n, op):
        for d in (1, 2):
            to = (p.row, lax.rem(p.col + d, 2 * p.Z))
            copy = remote(src, place(2 - d), ksend.at[n + d], krecv.at[n + d], to)
            if op == "start":
                pl.when(spot + d < pack)(copy.start)
            elif op == "arrive":
                pl.when(spot - d >= 0)(copy.wait_recv)
            else:
                pl.when(spot + d < pack)(copy.wait_send)

    mark_place = lambda k: marks_all.at[:, pl.ds(k * T, T)]
    mark_own = mark_place(2)
    behind(mark_own, mark_place, 0, "start")
    if with_slab:
        slabs[pl.ds(pl.multiple_of(slab_row(p.row, p.z, p.core), ar), ar)] = slab[...]
    ffns[p.z, at(p.row, br)] = ffn[...]

    def turn_cot(t):
        cots_t[:, at(t, BLOCK)] = cots[at(t, BLOCK)].T

    loop(B, turn_cot)
    if with_slab:
        for s in range(p.Z):
            if s + 1 < p.Z:
                near.spread_xy(s + 1)
            near.spread_diagonal(s)
        far.spread_z()
        far.spread_xy(0)
        passed = []
        n = 0
        for s in range(p.Z):
            near.close(s)
            zc = p.z_at(s)
            for dy in range(p.Y):
                for dx in range(p.X):
                    r = p.row_at(dy, dx)
                    place = slab_at(zc, r, None)
                    copy = remote(place, place, csend.at[n], crecv.at[n], mate)
                    copy.start()
                    theirs = slabs.at[pl.ds(pl.multiple_of(slab_row(r, zc, 1 - p.core), ar), ar)]
                    passed.append((copy, remote(theirs, theirs, csend.at[n], crecv.at[n], mate)))
                    n += 1
        cot_copy.wait()
        loop(B, lambda t: turn_cot(t + B))
        for copy, arrival in passed:
            copy.wait_send()
            arrival.wait_recv()
    else:
        far.spread_z()
        far.spread_xy(0)
        cot_copy.wait()
        loop(B, lambda t: turn_cot(t + B))
        load_slab.wait()
    save_slabs = local(slabs, slabs_out, 1)
    gains[...] = slabs[:, QK + E :].astype(F32).T[0:8]

    def first_norm(t):
        rows = at(t, 64)
        value = tokens[rows].astype(F32)
        mlp[rows] = (value * rms_scale(value) * gains[0:1]).astype(BF)

    loop(T // 64, first_norm)
    window[pl.ds(2 * T, T)] = product(mlp[pl.ds(0, T)], slabs[:, E : E + 2 * DH]).astype(BF)
    key_place = lambda k: window.at[pl.ds(k * T, T)]
    behind(key_place(2), key_place, 3, "start")

    def project(t):
        query[at(t, BLOCK)] = product(mlp[at(t, BLOCK)], slabs[:, 0:E]).astype(BF)

    loop(B, project)
    if p.Z > 1:
        far.spread_xy(1)
    save_query = local(query, query_out, 2)
    behind(mark_own, mark_place, 0, "arrive")
    column = jnp.broadcast_to(marks_all[0:1], (128, 3 * T)).T
    for i in range(B):
        keys_at = jnp.concatenate([column[i * BLOCK : i * BLOCK + span]] * (BLOCK // 128), axis=1)
        own = marks_all[0:1, 2 * T + i * BLOCK : 2 * T + (i + 1) * BLOCK]
        gap = (
            WINDOW
            + lax.broadcasted_iota(jnp.int32, (span, BLOCK), 1)
            - lax.broadcasted_iota(jnp.int32, (span, BLOCK), 0)
        )
        allowed = (keys_at == own) & (gap >= 0) & (gap < WINDOW)
        bias[i] = jnp.where(allowed, 0.0, NEGATIVE)
    save_bias = local(bias, bias_out, 3)
    behind(key_place(2), key_place, 3, "arrive")
    save_window = local(window, window_out, 4)
    values_t[...] = window[:, DH:].T
    factor = LOG2E / math.sqrt(DH)

    def head(i, h):
        lanes = at(h, DH)
        keys = window[pl.ds(i * BLOCK, span), 0:DH]
        scores = against(keys, query[pl.ds(i * BLOCK, BLOCK), lanes]) * factor + bias[i]
        top = jnp.max(scores, axis=0, keepdims=True)
        expo = jnp.exp2(scores - top)
        total = jnp.sum(expo, axis=0, keepdims=True)
        mixed = product(values_t[:, pl.ds(i * BLOCK, span)], expo.astype(BF))
        att[lanes, pl.ds(i * BLOCK, BLOCK)] = (mixed / total).astype(BF)
        lse[h * B + i] = jnp.broadcast_to(top + jnp.log2(total), (8, BLOCK))

    far.spread_diagonal(0)
    for i in range(B):
        loop(H // 2, lambda h: head(i, h))
        if i == 0 and p.Z > 2:
            far.spread_xy(2)
        loop(H // 2, lambda h: head(i, h + H // 2))
        if i == 0 and p.Z > 1:
            far.spread_diagonal(1)
    save_att = local(att, att_out, 5)
    save_lse = local(lse, lse_out, 6)

    def out_project(t):
        cols = at(t, BLOCK)
        middle[cols] = product(att[:, cols].T, slabs[:, QK : QK + E]) + tokens[cols].astype(F32)

    loop(B, out_project)

    def second_norm(t):
        rows = at(t, 64)
        value = middle[rows]
        mlp[rows] = (value * rms_scale(value) * gains[1:2]).astype(BF)

    loop(T // 64, second_norm)
    mlp_copy = remote(mlp.at[pl.ds(0, T)], mlp.at[pl.ds(T, T)], xsend.at[1], xrecv.at[1], mate)
    mlp_copy.start()

    def turn_mlp(t):
        mlp_t[:, at(t, BLOCK)] = mlp[at(t, BLOCK)].T

    loop(B, turn_mlp)
    if p.Z > 3:
        far.spread_xy(3)
    mlp_copy.wait()
    loop(B, lambda t: turn_mlp(t + B))
    for s in range(4, p.Z):
        far.spread_xy(s)

    saves = []
    for s in range(p.Z):
        zc = p.z_at(s)
        if s + 2 < p.Z:
            far.spread_diagonal(s + 2)
        far.close(s)
        slot = s % 2

        def tile(t):
            rows = at(t, BLOCK)
            gate_up = product(mlp[rows], ffns[zc, :, 0 : 2 * hz])
            grad_hidden = product(cots[rows], ffns[zc, :, 2 * hz :])
            up = gate_up[:, hz:]
            act, slope = gelu_parts(gate_up[:, :hz])
            hid = (act * up).astype(BF)
            hidden[rows] = hid
            grad_gate = (grad_hidden * up * slope).astype(BF)
            grad_up = (grad_hidden * act).astype(BF)
            grad_act[rows, 0:hz] = grad_gate
            grad_act[rows, hz : 2 * hz] = grad_up
            outs = against(hid, ffns[zc, :, 2 * hz :])
            grads = against(grad_act[rows], ffns[zc, :, 0 : 2 * hz])
            if s == 0:
                out_sum[rows] = outs
                grad_sum[rows] = grads
            else:
                out_sum[rows] += outs
                grad_sum[rows] += grads

        loop(2 * B, tile)
        if s > 1:
            saves[s - 2].wait()

        def weight_tile(t):
            rows = at(t, BLOCK)
            stage[slot, rows, 0 : 2 * hz] = product(mlp_t[rows], grad_act[...]).astype(BF)
            stage[slot, rows, 2 * hz :] = product(cots_t[rows], hidden[...]).astype(BF)

        loop(D // BLOCK, weight_tile)
        save = pltpu.make_async_copy(stage.at[slot], grads_out.at[zc], gsem.at[s])
        save.start()
        saves.append(save)

    grad_copy = remote(grad_sum.at[pl.ds(T, T)], grad_in, xsend.at[2], xrecv.at[2], mate)
    grad_copy.start()

    def narrow(t):
        out_send[at(t, 64)] = out_sum[pl.ds(pl.multiple_of(T + t * 64, 64), 64)].astype(BF)

    loop(T // 64, narrow)
    out_copy = remote(out_send, output, xsend.at[3], xrecv.at[3], mate)
    out_copy.start()
    for save in saves[max(0, p.Z - 2) :]:
        save.wait()
    for save in (save_slabs, save_query, save_bias, save_window, save_att, save_lse):
        save.wait()
    behind(mark_own, mark_place, 0, "sent")
    behind(key_place(2), key_place, 3, "sent")
    if with_slab:
        near.finish()
    far.finish()
    grad_copy.wait()

    def join(t):
        rows = at(t, 64)
        grad_in[rows] = grad_in[rows] + grad_sum[rows]

    loop(T // 64, join)
    out_copy.wait()

    def join_out(t):
        rows = at(t, 64)
        output[rows] = (middle[rows] + out_sum[rows] + output[rows].astype(F32)).astype(BF)

    loop(T // 64, join_out)


def forward(shape, with_slab, tokens, cot, marks, slab, ffn):
    X, Y, Z = sides(shape)
    T, D = tokens.shape
    E, hz = H * DH, ffn.shape[1] // 3
    W = slab.shape[1]
    B = T // BLOCK
    span = WINDOW + BLOCK
    n = gather_count(X, Y, Z)
    S = jax.ShapeDtypeStruct
    outs = [
        S((T, D), BF), S((T, D), F32), S((T, D), F32),
        S((D, W), BF), S((T, E), BF), S((3 * T, 2 * DH), BF), S((B, span, BLOCK), F32),
        S((E, T), BF), S((H * B, 8, BLOCK), F32), S((Z, D, 3 * hz), BF),
    ]
    V = pltpu.VMEM
    scratch = [
        V((D, W), BF), V((Z, D, 3 * hz), BF), V((T, E), BF), V((3 * T, 2 * DH), BF),
        V((DH, 3 * T), BF), V((8, 3 * T), F32), V((B, span, BLOCK), F32), V((E, T), BF),
        V((H * B, 8, BLOCK), F32), V((8, D), F32), V((2 * T, D), BF), V((D, 2 * T), BF),
        V((2 * T, D), BF), V((D, 2 * T), BF), V((2 * T, D), F32), V((2 * T, D), F32),
        V((2 * T, hz), BF), V((2 * T, 2 * hz), BF), V((2, D, 3 * hz), BF), V((T, D), BF),
        DMA((n,)), DMA((n,)), DMA((n,)), DMA((n,)),
        DMA((shape[0] * Z,)), DMA((shape[0] * Z,)), DMA((6,)), DMA((6,)), DMA((4,)), DMA((4,)),
        DMA((7,)), DMA((Z,)),
    ]
    return pl.pallas_call(
        functools.partial(forward_kernel, shape, with_slab, (D, T, E, W, hz)),
        out_shape=outs,
        in_specs=[VM, ANY, VM, VM if with_slab else ANY, VM],
        out_specs=[VM] * 3 + [ANY] * 7,
        scratch_shapes=scratch,
        compiler_params=pltpu.CompilerParams(
            collective_id=0, has_side_effects=True, vmem_limit_bytes=62 << 20
        ),
        name="forward",
    )(tokens, cot, marks, slab, ffn)


def backward_kernel(shape, with_slab, sizes, *refs):
    D, T, E, W, hz = sizes
    QK = E + 2 * DH
    B = T // BLOCK
    span = WINDOW + BLOCK
    (tokens_in, cot_in, middle_in, grad_in_in, slabs_in, query_in, window_in, bias_in, att_in, lse_in, grads,
     grad_tokens, ffn_out, out_slab, act_slab) = refs[:15]
    (tokens, cot, middle, grad_in, slabs, query, window, bias, att, lse,
     gains, keys_t, branch, att_grad, query_grad_t, query_grad, kv_sum, kv_send, kv_recv, kv_grad, attn_in_t,
     out_grads, act_grads, gain_rows, termx, termy, own) = refs[15:42]
    fwork = refs[42:46]
    rest = refs[46:]
    if with_slab:
        out_cross, act_cross = rest[:2]
        owork, awork = rest[2:6], rest[6:10]
        (fsend, frecv, ksend, krecv, lsem, psem, tsem, osend, orecv, asend, arecv, xsend, xrecv) = rest[10:]
    else:
        fsend, frecv, ksend, krecv, lsem, psem, tsem = rest
    p = Place(shape)
    pack = PACK // T
    spot = lax.rem(p.col, pack)
    mate = p.device(other=True)

    barrier = pltpu.get_barrier_semaphore()
    across = (p.row, (lax.rem(p.z + 1, 2) + p.z // 2 * 2) * 2 + 1 - p.core)
    mates = [p.device(dx=d) for d in p.xs] + [p.device(dy=d) for d in p.ys]
    mates += [p.device(dz=d) for d in p.zs] + [mate, across]
    for other in mates:
        pl.semaphore_signal(barrier, inc=1, device_id=other, device_id_type=MESH)

    br = D // p.R

    def part(zc, r):
        return grads.at[zc, at(r, br)]

    def cut(ref, h):
        rows = ref.shape[0] // 2
        return ref.at[pl.ds(h * rows, rows)]

    order = list(range(1, p.Z)) + [0]
    terms = {}
    for s in order:
        zc = p.z_at(s)
        copies = []
        n = s * (p.X + p.Y - 1)
        for d in p.xs:
            copies.append((cut(part(zc, p.row_at(dx=d)), 1), termx.at[s, d - 1]))
        for e in p.ys:
            copies.append((cut(part(zc, p.row_at(dy=e)), 0), termy.at[s, e - 1]))
        copies.append((part(zc, p.row), own.at[s]))
        terms[s] = [
            pltpu.make_async_copy(a, b, tsem.at[n + i]) for i, (a, b) in enumerate(copies)
        ]
    pairs = [
        (middle_in, middle), (grad_in_in, grad_in), (cot_in, cot), (slabs_in, slabs), (att_in, att),
        (tokens_in, tokens), (window_in, window), (query_in, query), (bias_in, bias), (lse_in, lse),
    ]
    loads = [pltpu.make_async_copy(a, b, lsem.at[n]) for n, (a, b) in enumerate(pairs)]
    for load in loads:
        load.start()
    for s in order:
        for copy in terms[s]:
            copy.start()
    pl.semaphore_wait(barrier, len(mates))
    far = Scatter(
        part, cut, p, Sems(fsend, frecv),
        lambda s, d: termx.at[s, d - 1], lambda s, e: termy.at[s, e - 1], lambda s: own.at[s], *fwork
    )
    ticks = []
    for j in range(p.Z + 1):
        tick = []
        if j >= 1:
            tick.append((far.third, order[j - 1]))
        if j < p.Z:
            tick.append((far.second, order[j]))
        if j + 2 < p.Z:
            tick.append((far.first, order[j + 2]))
        ticks.append(tick)

    def advance():
        if ticks:
            for step, s in ticks.pop(0):
                if step == far.second:
                    for copy in terms[s]:
                        copy.wait()
                if step == far.third:
                    step(s, ffn_out)
                else:
                    step(s)

    for s in order[:2]:
        far.first(s)

    for load in loads[:4]:
        load.wait()
    gains[...] = slabs[:, QK + E :].astype(F32).T[0:8]
    gain_rows[...] = jnp.zeros_like(gain_rows)

    def fold_rows(value):
        return jnp.sum(value.reshape(value.shape[0] // 8, 8, D), axis=0)

    def second_norm(t, total):
        rows = at(t, 64)
        value, grad = middle[rows], grad_in[rows]
        scale = rms_scale(value)
        total = total + fold_rows(grad * (value * scale))
        n = grad * gains[1:2]
        out = cot[rows].astype(F32) + scale * n - value * (
            scale * scale * scale * jnp.mean(n * value, axis=-1, keepdims=True)
        )
        grad_in[rows] = out
        branch[rows] = out.astype(BF)
        return total

    total = lax.fori_loop(0, T // 64, second_norm, jnp.zeros((8, D), F32))
    gain_rows[1:2] = jnp.sum(total, axis=0, keepdims=True)

    def attended_grad(t):
        att_grad[at(t, BLOCK)] = against(
            slabs[at(t, BLOCK), QK : QK + E], branch[...]
        ).astype(BF)

    loop(E // BLOCK, attended_grad)
    loads[4].wait()
    ar = D // (p.R * p.Z * 2)
    blocks = BLOCK // (2 * ar)

    def put(ref, t, lanes, value):
        ref[pl.ds(t * blocks, blocks), :, :, lanes] = value.astype(BF).reshape(
            blocks, 2, ar, value.shape[1]
        )

    if not with_slab:
        def put(ref, t, lanes, value):
            ref[at(t, BLOCK), lanes] = value.astype(BF)

    def out_weight_grad(t):
        put(out_grads, t, slice(0, E), product(att[at(t, BLOCK)], branch[...]))

    loop(E // BLOCK, out_weight_grad)

    def crossing(ref, place, n):
        return remote(ref.at[:, 1 - p.core], place, xsend.at[n], xrecv.at[n], mate)

    def fold(ref, place):
        def step(n):
            ref[n, p.core] = (ref[n, p.core].astype(F32) + place[n].astype(F32)).astype(BF)

        loop(p.R * p.Z, step)

    def plane_scatter(ref, sems, work):
        def block(zc, r):
            return ref.at[r * p.Z + zc, p.core]

        return Scatter(
            block, cut, p, sems,
            lambda s, d: cut(block(p.z_at(s), p.row_at(dx=d)), 1),
            lambda s, e: cut(block(p.z_at(s), p.row_at(dy=e)), 0),
            lambda s: block(p.z_at(s), p.row), *work
        )

    if with_slab:
        out_copy = crossing(out_grads, out_cross, 0)
        out_copy.start()
        near_out = plane_scatter(out_grads, Sems(osend, orecv), owork)
        near_act = plane_scatter(act_grads, Sems(asend, arecv), awork)

    for load in loads[5:]:
        load.wait()

    def first_norm(t):
        cols = at(t, 128)
        value = tokens[cols].astype(F32)
        attn_in_t[:, cols] = (value * rms_scale(value) * gains[0:1]).astype(BF).T

    loop(T // 128, first_norm)
    keys_t[...] = window[:, 0:DH].T
    kv_sum[...] = jnp.zeros_like(kv_sum)
    advance()

    factor = LOG2E / math.sqrt(DH)
    scale = 1.0 / math.sqrt(DH)

    def head(i, h):
        lanes = at(h, DH)
        here = pl.ds(i * BLOCK, BLOCK)
        seen = pl.ds(i * BLOCK, span)
        part_query = query[here, lanes]
        part_grad = att_grad[lanes, here]
        scores = against(window[seen, 0:DH], part_query) * factor + bias[i]
        probs = jnp.exp2(scores - lse[h * B + i][0:1])
        grad_probs = product(window[seen, DH:], part_grad)
        centre = jnp.sum(
            att[lanes, here].astype(F32) * part_grad.astype(F32), axis=0, keepdims=True
        )
        grad_scores = (probs * (grad_probs - centre)).astype(BF)
        kv_sum[seen, DH:] += against(probs.astype(BF), part_grad)
        kv_sum[seen, 0:DH] += product(grad_scores, part_query)
        query_grad_t[lanes, here] = (product(keys_t[:, seen], grad_scores) * scale).astype(BF)

    pieces = [(i, g) for i in range(B) for g in range(4)]
    for n, (i, g) in enumerate(pieces):
        loop(H // 4, lambda k: head(i, g * (H // 4) + k))
        if with_slab and n == 1:
            out_copy.wait()
            fold(out_grads, out_cross)
            for s in order:
                near_out.first(s)
        if with_slab and n == 4:
            for s in order:
                near_out.second(s)
        if with_slab and n == 7:
            for s in order:
                near_out.third(s, out_slab)
        if n in (1, 4, 7):
            advance()

    kv_send[:, 0:DH] = (kv_sum[pl.ds(0, 2 * T), 0:DH] * scale).astype(BF)
    kv_send[:, DH:] = kv_sum[pl.ds(0, 2 * T), DH:].astype(BF)
    returns = []
    for d in (1, 2):
        to = (p.row, lax.rem(p.col - d + 2 * p.Z, 2 * p.Z))
        copy = remote(
            kv_send.at[pl.ds((2 - d) * T, T)], kv_recv.at[d - 1], ksend.at[d - 1], krecv.at[d - 1], to
        )
        pl.when(spot - d >= 0)(copy.start)
        returns.append((d, copy))

    def turn(t):
        query_grad[at(t, BLOCK)] = query_grad_t[:, at(t, BLOCK)].T

    loop(B, turn)

    def query_weight_grad(t):
        put(act_grads, t, slice(0, E), product(attn_in_t[at(t, BLOCK)], query_grad[...]))

    loop(D // BLOCK, query_weight_grad)
    kv_grad[:, 0:DH] = kv_sum[pl.ds(2 * T, T), 0:DH] * scale
    kv_grad[:, DH:] = kv_sum[pl.ds(2 * T, T), DH:]
    for d, copy in returns:
        @pl.when(spot + d < pack)
        def _():
            copy.wait_recv()
            kv_grad[...] += kv_recv[d - 1].astype(F32)

    window[pl.ds(0, T)] = kv_grad[...].astype(BF)

    def keyval_weight_grad(t):
        put(act_grads, t, slice(E, QK), product(attn_in_t[at(t, BLOCK)], window[pl.ds(0, T)]))

    loop(D // BLOCK, keyval_weight_grad)

    def input_grad(t, total):
        rows = at(t, 128)
        grad = against(query_grad[rows], slabs[:, 0:E]) + against(window[rows], slabs[:, E:QK])
        value = tokens[rows].astype(F32)
        scale_first = rms_scale(value)
        total = total + fold_rows(grad * (value * scale_first))
        m = grad * gains[0:1]
        grad_tokens[rows] = grad_in[rows] + scale_first * m - value * (
            scale_first * scale_first * scale_first * jnp.mean(m * value, axis=-1, keepdims=True)
        )
        return total

    total = lax.fori_loop(0, T // 128, input_grad, jnp.zeros((8, D), F32))
    gain_rows[0:1] = jnp.sum(total, axis=0, keepdims=True)

    def gain_grad(t):
        put(act_grads, t, slice(QK, QK + 128), gain_rows[:, at(t, BLOCK)].T)

    loop(D // BLOCK, gain_grad)
    if with_slab:
        act_copy = crossing(act_grads, act_cross, 1)
        act_copy.start()
        act_copy.wait()
        fold(act_grads, act_cross)
        for s in order:
            near_act.first(s)
        for s in order:
            near_act.second(s)
        for s in order:
            near_act.third(s, act_slab)
    else:
        out_slab[...] = out_grads[...]
        act_slab[...] = act_grads[...]
    while ticks:
        advance()
    for d, copy in returns:
        pl.when(spot - d >= 0)(copy.wait_send)
    far.finish()
    if with_slab:
        near_out.finish()
        near_act.finish()


def backward(shape, with_slab, tokens, cot, middle, grad_in, slabs, query, window, bias, att, lse, grads):
    X, Y, Z = sides(shape)
    R = shape[0]
    T, D = tokens.shape
    E, hz = H * DH, grads.shape[2] // 3
    W = slabs.shape[1]
    B = T // BLOCK
    span = WINDOW + BLOCK
    n = scatter_count(X, Y, Z)
    S, V = jax.ShapeDtypeStruct, pltpu.VMEM
    block = (D // R, 3 * hz)
    half = (block[0] // 2, block[1])
    A = E + 2 * DH + 128
    ar = D // (R * Z * 2)
    if with_slab:
        slab_outs = [S((ar, E), F32), S((ar, A), F32)]
        slab_work = [V((R * Z, 2, ar, E), BF), V((R * Z, 2, ar, A), BF)]
    else:
        slab_outs = [S((D, E), BF), S((D, A), BF)]
        slab_work = [V((D, E), BF), V((D, A), BF)]
    outs = [S((T, D), F32), S(block, F32)] + slab_outs
    scratch = [
        V((T, D), BF), V((T, D), BF), V((T, D), F32), V((T, D), F32), V((D, W), BF), V((T, E), BF),
        V((3 * T, 2 * DH), BF), V((B, span, BLOCK), F32), V((E, T), BF), V((H * B, 8, BLOCK), F32),
        V((8, D), F32), V((DH, 3 * T), BF), V((T, D), BF), V((E, T), BF), V((E, T), BF), V((T, E), BF),
        V((3 * T, 2 * DH), F32), V((2 * T, 2 * DH), BF), V((2, T, 2 * DH), BF), V((T, 2 * DH), F32),
        V((D, T), BF), *slab_work, V((128, D), F32),
        V((Z, X - 1) + half, BF), V((Z, Y - 1) + half, BF), V((Z,) + block, BF),
        *scatter_scratch(X, Y, Z, block),
    ]
    if with_slab:
        scratch += [V((R * Z, ar, E), BF), V((R * Z, ar, A), BF)]
        scratch += scatter_scratch(X, Y, Z, (ar, E)) + scatter_scratch(X, Y, Z, (ar, A))
    scratch += [
        DMA((n,)), DMA((n,)), DMA((2,)), DMA((2,)), DMA((10,)), DMA((1,)), DMA((Z * (X + Y - 1),)),
    ]
    if with_slab:
        scratch += [DMA((n,))] * 4 + [DMA((2,))] * 2
    return pl.pallas_call(
        functools.partial(backward_kernel, shape, with_slab, (D, T, E, W, hz)),
        out_shape=outs,
        in_specs=[ANY] * 11,
        out_specs=[VM] * 4,
        scratch_shapes=scratch,
        compiler_params=pltpu.CompilerParams(
            collective_id=1, has_side_effects=True, vmem_limit_bytes=62 << 20
        ),
        name="backward",
    )(tokens, cot, middle, grad_in, slabs, query, window, bias, att, lse, grads)


def shards(
    shape,
    tokens, gain_attn, w_query, w_keyval, w_out, gain_mlp, w_gate, w_up, w_down, segment, cotangent
):
    D = tokens.shape[1]
    with_slab = w_query.shape[0] % 32 == 0
    ffn = jnp.concatenate([w_gate, w_up, w_down.T], axis=1)
    slab = jnp.concatenate(
        [w_query, w_keyval, w_out,
         jnp.pad(jnp.stack([gain_attn, gain_mlp], axis=1), ((0, 0), (0, 126)))], axis=1)
    if not with_slab:
        slab = lax.all_gather(slab, ("row", "col"), axis=0, tiled=True)
    marks = jnp.broadcast_to(segment.astype(F32)[None], (8, segment.shape[0]))
    output, grad_in, middle, *kept = forward(shape, with_slab, tokens, cotangent, marks, slab, ffn)
    grad_tokens, ffn_grad, out_grad, act_grad = backward(
        shape, with_slab, tokens, cotangent, middle, grad_in, *kept)
    if not with_slab:
        out_grad, act_grad = (
            lax.psum_scatter(g.astype(F32), ("row", "col"), scatter_dimension=0, tiled=True)
            for g in (out_grad, act_grad)
        )
    E = H * DH
    hz = w_gate.shape[1]
    return (
        output,
        grad_tokens,
        act_grad[:, E + 2 * DH],
        act_grad[:, :E],
        act_grad[:, E : E + 2 * DH],
        out_grad,
        act_grad[:, E + 2 * DH + 1],
        ffn_grad[:, :hz],
        ffn_grad[:, hz : 2 * hz],
        ffn_grad[:, 2 * hz :].T,
    )


def solution(mesh):
    shape = (mesh.shape["row"], mesh.shape["col"])
    return jax.shard_map(
        functools.partial(shards, shape),
        mesh=mesh,
        in_specs=(
            P(("row", "col"), None),
            P(("row", "col")),
            P(("row", "col"), None),
            P(("row", "col"), None),
            P(("row", "col"), None),
            P(("row", "col")),
            P("row", "col"),
            P("row", "col"),
            P("col", "row"),
            P(("row", "col")),
            P(("row", "col"), None),
        ),
        out_specs=(
            P(("row", "col"), None),
            P(("row", "col"), None),
            P(("row", "col")),
            P(("row", "col"), None),
            P(("row", "col"), None),
            P(("row", "col"), None),
            P(("row", "col")),
            P("row", "col"),
            P("row", "col"),
            P("col", "row"),
        ),
        check_vma=False,
    )
```

```python
import functools
import math

import jax
import jax.numpy as jnp
from jax import lax
from jax.experimental import pallas as pl
from jax.experimental.pallas import tpu as pltpu
from jax.sharding import PartitionSpec as P

H = 8
DH = 128
WINDOW = 1024
PACK = 2048

EPS = 1e-06
NEGATIVE = -1e30
MESH = pl.DeviceIdType.MESH
BF = jnp.bfloat16
F32 = jnp.float32


def product(left, right):
    return jnp.dot(left, right, preferred_element_type=jnp.float32)


def inner(left, right):
    return lax.dot_general(
        left, right, (((0,), (0,)), ((), ())), preferred_element_type=jnp.float32
    )


def against(left, right):
    return lax.dot_general(
        left, right, (((1,), (1,)), ((), ())), preferred_element_type=jnp.float32
    )


class Place:
    def __init__(self, shape):
        rows, cols = shape
        self.X = math.isqrt(rows)
        while rows % self.X:
            self.X -= 1
        self.Y = rows // self.X
        self.Z = cols // 2
        self.R = rows
        self.row, self.col = lax.axis_index("row"), lax.axis_index("col")
        self.y, self.x = self.row // self.X, self.row % self.X
        self.z, self.core = self.col // 2, self.col % 2
        self.xs, self.ys, self.zs = range(1, self.X), range(1, self.Y), range(1, self.Z)

    def row_at(self, dy=0, dx=0):
        return lax.rem(self.y + dy + self.Y, self.Y) * self.X + lax.rem(
            self.x + dx + self.X, self.X
        )

    def z_at(self, dz):
        return lax.rem(self.z + dz + self.Z, self.Z)

    def device(self, dy=0, dx=0, dz=0, other=False):
        core = 1 - self.core if other else self.core
        return (self.row_at(dy, dx), self.z_at(dz) * 2 + core)


def remote(src, dst, send, recv, device):
    return pltpu.make_async_remote_copy(
        src_ref=src, dst_ref=dst, send_sem=send, recv_sem=recv, device_id=device,
        device_id_type=MESH,
    )


class Sems:
    def __init__(self, send, recv):
        self.send, self.recv, self.count = send, recv, 0

    def take(self):
        self.count += 1
        return self.send.at[self.count - 1], self.recv.at[self.count - 1]


def gather_count(X, Y, K):
    return (K - 1) + K * ((X - 1) + (Y - 1) + 2 * (X - 1) * (Y - 1))


class Gather:
    def __init__(self, at, dest, here, sems, own, stride=1):
        self.at, self.dest, self.p, self.own = at, dest, here, own
        self.stride, self.K = stride, here.Z // stride
        self.sent = []
        p = here
        self.zsem = {k: sems.take() for k in range(1, self.K)}
        self.xsem = {(s, d): sems.take() for s in range(self.K) for d in p.xs}
        self.ysem = {(s, d): sems.take() for s in range(self.K) for d in p.ys}
        self.dsem = {
            (s, h, dx, dy): sems.take()
            for s in range(self.K) for h in (0, 1) for dx in p.xs for dy in p.ys
        }

    def push(self, src, dst, sem, device):
        copy = remote(src, dst, sem[0], sem[1], device)
        copy.start()
        self.sent.append(copy)

    def arrive(self, place, sem):
        remote(place, place, sem[0], sem[1], self.p.device(other=True)).wait_recv()

    def spread_z(self):
        p = self.p
        for k in range(1, self.K):
            self.push(self.own, self.dest(k), self.zsem[k], p.device(dz=-self.stride * k))

    def spread_xy(self, s):
        if s >= self.K:
            return
        p = self.p
        place = self.at(s, p.row, None)
        src = self.own
        if s:
            self.arrive(place, self.zsem[s])
            src = place
        for d in p.xs:
            self.push(src, place, self.xsem[s, d], p.device(dx=d))
        for d in p.ys:
            self.push(src, place, self.ysem[s, d], p.device(dy=d))

    def spread_diagonal(self, s):
        if s >= self.K:
            return
        p = self.p
        for d in p.xs:
            r = p.row_at(dx=-d)
            self.arrive(self.at(s, r, None), self.xsem[s, d])
            half = self.at(s, r, 0)
            for e in p.ys:
                self.push(half, half, self.dsem[s, 0, d, e], p.device(dy=e))
        for e in p.ys:
            r = p.row_at(dy=-e)
            self.arrive(self.at(s, r, None), self.ysem[s, e])
            half = self.at(s, r, 1)
            for d in p.xs:
                self.push(half, half, self.dsem[s, 1, d, e], p.device(dx=d))

    def close(self, s):
        p = self.p
        for d in p.xs:
            for e in p.ys:
                r = p.row_at(dy=-e, dx=-d)
                for h in (0, 1):
                    self.arrive(self.at(s, r, h), self.dsem[s, h, d, e])

    def finish(self):
        for copy in self.sent:
            copy.wait_send()


def scatter_count(X, Y, K):
    return (K - 1) + K * (2 * (X - 1) * (Y - 1) + 2 * (X - 1) + 2 * (Y - 1))


class Scatter:
    def __init__(
        self, part, cut, here, sems, termx, termy, own, diag, fromx, fromy, fromz, stride=1
    ):
        self.part, self.cut, self.p = part, cut, here
        self.termx, self.termy, self.own = termx, termy, own
        self.diag, self.fromx, self.fromy, self.fromz = diag, fromx, fromy, fromz
        self.stride, self.K = stride, here.Z // stride
        self.sent = []
        p = here
        self.zsem = {k: sems.take() for k in range(1, self.K)}
        self.xsem = {(s, h, d): sems.take() for s in range(self.K) for h in (0, 1) for d in p.xs}
        self.ysem = {(s, h, d): sems.take() for s in range(self.K) for h in (0, 1) for d in p.ys}
        self.dsem = {
            (s, h, dx, dy): sems.take()
            for s in range(self.K) for h in (0, 1) for dx in p.xs for dy in p.ys
        }

    def push(self, src, dst, sem, device):
        copy = remote(src, dst, sem[0], sem[1], device)
        copy.start()
        self.sent.append(copy)

    def arrive(self, place, sem):
        remote(place, place, sem[0], sem[1], self.p.device(other=True)).wait_recv()

    def spot(self, d, e):
        return (d - 1) * (self.p.Y - 1) + e - 1

    def first(self, s):
        p, cut = self.p, self.cut
        for d in p.xs:
            for e in p.ys:
                far = self.part(s, p.row_at(dy=e, dx=d))
                n = self.spot(d, e)
                self.push(cut(far, 0), self.diag.at[s, 0, n], self.dsem[s, 0, d, e], p.device(dx=d))
                self.push(cut(far, 1), self.diag.at[s, 1, n], self.dsem[s, 1, d, e], p.device(dy=e))
        for d in p.xs:
            near = self.part(s, p.row_at(dx=d))
            self.push(cut(near, 0), cut(self.fromx.at[s, d - 1], 0), self.xsem[s, 0, d], p.device(dx=d))
        for e in p.ys:
            near = self.part(s, p.row_at(dy=e))
            self.push(cut(near, 1), cut(self.fromy.at[s, e - 1], 1), self.ysem[s, 1, e], p.device(dy=e))

    def second(self, s):
        p, cut = self.p, self.cut
        for e in p.ys:
            term = self.termy(s, e)
            total = term[...].astype(F32)
            for d in p.xs:
                place = self.diag.at[s, 0, self.spot(d, e)]
                self.arrive(place, self.dsem[s, 0, d, e])
                total = total + place[...].astype(F32)
            term[...] = total.astype(BF)
            self.push(term, cut(self.fromy.at[s, e - 1], 0), self.ysem[s, 0, e], p.device(dy=e))
        for d in p.xs:
            term = self.termx(s, d)
            total = term[...].astype(F32)
            for e in p.ys:
                place = self.diag.at[s, 1, self.spot(d, e)]
                self.arrive(place, self.dsem[s, 1, d, e])
                total = total + place[...].astype(F32)
            term[...] = total.astype(BF)
            self.push(term, cut(self.fromx.at[s, d - 1], 1), self.xsem[s, 1, d], p.device(dx=d))

    def third(self, s, out=None):
        p, cut = self.p, self.cut
        own = self.own(s)
        total = own[...].astype(F32)
        for d in p.xs:
            for h in (0, 1):
                self.arrive(cut(self.fromx.at[s, d - 1], h), self.xsem[s, h, d])
            total = total + self.fromx[s, d - 1].astype(F32)
        for e in p.ys:
            for h in (0, 1):
                self.arrive(cut(self.fromy.at[s, e - 1], h), self.ysem[s, h, e])
            total = total + self.fromy[s, e - 1].astype(F32)
        if s:
            own[...] = total.astype(BF)
            self.push(own, self.fromz.at[s - 1], self.zsem[s], p.device(dz=self.stride * s))
            return
        for k in range(1, self.K):
            self.arrive(self.fromz.at[k - 1], self.zsem[k])
            total = total + self.fromz[k - 1].astype(F32)
        out[...] = total

    def finish(self):
        for copy in self.sent:
            copy.wait_send()


def scatter_scratch(X, Y, K, block):
    half = (block[0] // 2, block[1])
    return [
        pltpu.VMEM((K, 2, (X - 1) * (Y - 1)) + half, BF),
        pltpu.VMEM((K, X - 1) + block, BF),
        pltpu.VMEM((K, Y - 1) + block, BF),
        pltpu.VMEM((max(K - 1, 1),) + block, BF),
    ]


def sides(shape):
    x = math.isqrt(shape[0])
    while shape[0] % x:
        x -= 1
    return x, shape[0] // x, shape[1] // 2


VM = pl.BlockSpec(memory_space=pltpu.VMEM)
ANY = pl.BlockSpec(memory_space=pl.ANY)
DMA = pltpu.SemaphoreType.DMA
LOG2E = math.log2(math.e)
BLOCK = 256


def loop(count, body):
    def step(t, carry):
        body(t)
        return carry

    lax.fori_loop(0, count, step, 0)


def at(t, size):
    return pl.ds(pl.multiple_of(t * size, size), size)


def rms_scale(value):
    return lax.rsqrt(jnp.mean(value * value, axis=-1, keepdims=True) + EPS)


def gelu_parts(gate):
    square = gate * gate
    t = jnp.tanh(gate * (0.7978845608 + (0.7978845608 * 0.044715) * square))
    half = 0.5 + 0.5 * t
    slope = half + (0.5 * gate) * (1.0 - t * t) * (
        0.7978845608 + (3 * 0.7978845608 * 0.044715) * square
    )
    return gate * half, slope


class Pack:
    def __init__(self, here, T):
        p = here
        self.p, self.size = p, PACK // T
        self.spot = lax.rem(p.col, self.size)
        pair = (p.z // 2) * 2 + 1 - lax.rem(p.z, 2)
        self.mate = p.device(other=True)
        self.pair = (p.row, pair * 2 + p.core)
        self.across = (p.row, pair * 2 + 1 - p.core)

    def greet(self):
        p = self.p
        barrier = pltpu.get_barrier_semaphore()
        mates = [p.device(dx=d) for d in p.xs] + [p.device(dy=d) for d in p.ys]
        mates += [p.device(dz=d) for d in p.zs] + [self.mate, self.across]
        for mate in mates:
            pl.semaphore_signal(barrier, inc=1, device_id=mate, device_id_type=MESH)
        return lambda: pl.semaphore_wait(barrier, len(mates))


def slab_lanes():
    E, QK = H * DH, H * DH + 2 * DH
    return E, QK, QK + 128


def forward_kernel(shape, with_slab, sizes, *refs):
    D, T, W, hz = sizes
    (tokens, cot, marks, slab, ffn,
     grad_in, middle, out_own, out_far, slabs_out, query_out, window_out, bias_out, att_out, lse_out, grads_out,
     slabs, ffns, query, window, values_t, marks_all, bias, att, lse, gains, mlp, cots,
     grad_tile, out_tile, hidden, grad_act, side_grad, side_out, cross_grad, cross_out, far_grad,
     mate_grad, mate_out, pre_grad, pre_out, pair_grad,
     asend, arecv, osend, orecv, fsend, frecv, csend, crecv, ksend, krecv, tsend, trecv, msend, mrecv,
     gsend, grecv, lsem, gsem) = refs
    p = Place(shape)
    pack = Pack(p, T)
    mate, pair, spot = pack.mate, pack.pair, pack.spot
    E, QK, WO = slab_lanes()
    B = T // BLOCK
    span = WINDOW + BLOCK
    K = p.Z // 2

    def local(src, dst, n):
        copy = pltpu.make_async_copy(src, dst, lsem.at[n])
        copy.start()
        return copy

    ready = pack.greet()
    load_cot = local(cot, cots.at[pl.ds(0, T)], 0)
    if not with_slab:
        load_slab = local(slab, slabs, 1)
    ready()

    br = ffn.shape[0]

    def ffn_at(s, r, half):
        if half is None:
            return ffns.at[s, at(r, br)]
        return ffns.at[s, pl.ds(pl.multiple_of(r * br + half * (br // 2), br // 2), br // 2)]

    far = Gather(ffn_at, lambda k: ffn_at(k, p.row, None), p, Sems(fsend, frecv), ffn, 2)

    if with_slab:
        ar = slab.shape[0]

        def slab_place(lanes, core):
            def place(s, r, half):
                start = ((r * p.Z + p.z_at(s)) * 2 + core) * ar
                if half is None:
                    return slabs.at[pl.ds(pl.multiple_of(start, ar), ar), lanes]
                start = pl.multiple_of(start + half * (ar // 2), ar // 2)
                return slabs.at[pl.ds(start, ar // 2), lanes]

            return place

        def slab_gather(lanes, sems):
            place = slab_place(lanes, p.core)
            return Gather(place, lambda k: place(0, p.row, None), p, sems, slab.at[:, lanes])

        act_lanes, out_lanes = slice(0, WO), slice(WO, W)
        near = slab_gather(act_lanes, Sems(asend, arecv))
        near_out = slab_gather(out_lanes, Sems(osend, orecv))
        hands = Sems(csend, crecv)

        def hand(gather, lanes):
            mine, theirs = slab_place(lanes, p.core), slab_place(lanes, 1 - p.core)
            passed = []
            for s in range(p.Z):
                gather.close(s)
                for dy in range(p.Y):
                    for dx in range(p.X):
                        r = p.row_at(dy, dx)
                        send, recv = hands.take()
                        place, other = mine(s, r, None), theirs(s, r, None)
                        copy = remote(place, place, send, recv, mate)
                        copy.start()
                        passed.append((copy, remote(other, other, send, recv, mate)))
            return passed

        near.spread_z()
        near.spread_xy(0)
        near_out.spread_z()

    marks_all[:, pl.ds(2 * T, T)] = marks[...]

    @pl.when(spot == 0)
    def _():
        window[pl.ds(0, 2 * T), :] = jnp.zeros((2 * T, 2 * DH), BF)
        marks_all[:, pl.ds(0, 2 * T)] = jnp.full((8, 2 * T), -1.0, F32)

    @pl.when(spot == 1)
    def _():
        window[pl.ds(0, T), :] = jnp.zeros((T, 2 * DH), BF)
        marks_all[:, pl.ds(0, T)] = jnp.full((8, T), -1.0, F32)

    def behind(src, place, n, op):
        for d in (1, 2):
            to = (p.row, lax.rem(p.col + d, 2 * p.Z))
            copy = remote(src, place(2 - d), ksend.at[n + d], krecv.at[n + d], to)
            if op == "start":
                pl.when(spot + d < pack.size)(copy.start)
            elif op == "arrive":
                pl.when(spot - d >= 0)(copy.wait_recv)
            else:
                pl.when(spot + d < pack.size)(copy.wait_send)

    mark_place = lambda k: marks_all.at[:, pl.ds(k * T, T)]
    mark_own = mark_place(2)
    behind(mark_own, mark_place, 0, "start")

    def whole(ref, n):
        return ref.at[pl.ds(n * T, T)]

    load_cot.wait()
    cot_mate = remote(whole(cots, 0), whole(cots, 1), tsend.at[0], trecv.at[0], mate)
    cot_pair = remote(whole(cots, 0), whole(cots, 2), tsend.at[1], trecv.at[1], pair)
    cot_pass = remote(whole(cots, 2), whole(cots, 3), tsend.at[2], trecv.at[2], mate)
    cot_mate.start()
    if with_slab:
        slabs[pl.ds(pl.multiple_of(((p.row * p.Z + p.z) * 2 + p.core) * ar, ar), ar)] = slab[...]
    ffns[0, at(p.row, br)] = ffn[...]
    if with_slab:
        for s in range(p.Z):
            near.spread_xy(s + 1)
            if s == 0:
                near_out.spread_xy(0)
            near.spread_diagonal(s)
        far.spread_z()
        cot_pair.start()
        for s in range(1, p.Z):
            near_out.spread_xy(s)
        passed = hand(near, act_lanes)
        far.spread_xy(0)
        for s in range(p.Z):
            near_out.spread_diagonal(s)
        for copy, arrival in passed:
            copy.wait_send()
            arrival.wait_recv()
    else:
        far.spread_z()
        cot_pair.start()
        far.spread_xy(0)
        load_slab.wait()
    gains[...] = slabs[:, QK:WO].astype(F32).T[0:8]

    def first_norm(t):
        rows = at(t, 64)
        value = tokens[rows].astype(F32)
        mlp[rows] = (value * rms_scale(value) * gains[0:1]).astype(BF)

    loop(T // 64, first_norm)
    window[pl.ds(2 * T, T)] = product(mlp[pl.ds(0, T)], slabs[:, E:QK]).astype(BF)
    key_place = lambda k: window.at[pl.ds(k * T, T)]
    behind(key_place(2), key_place, 3, "start")

    def project(t):
        query[at(t, BLOCK)] = product(mlp[at(t, BLOCK)], slabs[:, 0:E]).astype(BF)

    loop(B, project)
    save_query = local(query, query_out, 2)
    if with_slab:
        passed = hand(near_out, out_lanes)
    behind(mark_own, mark_place, 0, "arrive")
    column = jnp.broadcast_to(marks_all[0:1], (128, 3 * T)).T
    for i in range(B):
        keys_at = jnp.concatenate([column[i * BLOCK : i * BLOCK + span]] * (BLOCK // 128), axis=1)
        own = marks_all[0:1, 2 * T + i * BLOCK : 2 * T + (i + 1) * BLOCK]
        gap = (
            WINDOW
            + lax.broadcasted_iota(jnp.int32, (span, BLOCK), 1)
            - lax.broadcasted_iota(jnp.int32, (span, BLOCK), 0)
        )
        allowed = (keys_at == own) & (gap >= 0) & (gap < WINDOW)
        bias[i] = jnp.where(allowed, 0.0, NEGATIVE)
    save_bias = local(bias, bias_out, 3)
    behind(key_place(2), key_place, 3, "arrive")
    save_window = local(window, window_out, 4)
    values_t[...] = window[:, DH:].T
    factor = LOG2E / math.sqrt(DH)

    def head(i, h):
        lanes = at(h, DH)
        keys = window[pl.ds(i * BLOCK, span), 0:DH]
        scores = against(keys, query[pl.ds(i * BLOCK, BLOCK), lanes]) * factor + bias[i]
        top = jnp.max(scores, axis=0, keepdims=True)
        expo = jnp.exp2(scores - top)
        total = jnp.sum(expo, axis=0, keepdims=True)
        mixed = product(values_t[:, pl.ds(i * BLOCK, span)], expo.astype(BF))
        att[lanes, pl.ds(i * BLOCK, BLOCK)] = (mixed / total).astype(BF)
        lse[h * B + i] = jnp.broadcast_to(top + jnp.log2(total), (8, BLOCK))

    def tile_of(ref, n, i):
        return ref.at[pl.ds(pl.multiple_of(n * T + i * BLOCK, BLOCK), BLOCK)]

    def mlp_copy(n, i):
        to = pair if n == 2 else mate
        src = 2 if n == 3 else 0
        sem = (n - 1) * B + i
        return remote(tile_of(mlp, src, i), tile_of(mlp, n, i), msend.at[sem], mrecv.at[sem], to)

    for i in range(B):
        if i == 0:
            loop(H // 2, lambda h: head(i, h))
            far.spread_xy(1)
            far.spread_diagonal(0)
            loop(H // 2, lambda h: head(i, h + H // 2))
            if with_slab:
                for copy, arrival in passed:
                    copy.wait_send()
                    arrival.wait_recv()
            save_slabs = local(slabs, slabs_out, 1)
        else:
            loop(H, lambda h: head(i, h))
        cols = pl.ds(i * BLOCK, BLOCK)
        middle[cols] = product(att[:, cols].T, slabs[:, WO:]) + tokens[cols].astype(F32)

        def second_norm(t):
            rows = pl.ds(pl.multiple_of(i * BLOCK + t * 64, 64), 64)
            value = middle[rows]
            mlp[rows] = (value * rms_scale(value) * gains[1:2]).astype(BF)

        loop(BLOCK // 64, second_norm)
        mlp_copy(1, i).start()
        mlp_copy(2, i).start()
        if i == 0:
            cot_pair.wait_recv()
            cot_pass.start()
    save_att = local(att, att_out, 5)
    save_lse = local(lse, lse_out, 6)
    for s in range(2, K):
        far.spread_xy(s)
    for s in range(1, K):
        far.spread_diagonal(s)
    mlp_copy(2, 0).wait_recv()
    mlp_copy(3, 0).start()
    for s in range(K):
        far.close(s)
    cot_mate.wait()
    cot_pass.wait_recv()

    def grad_copy(i):
        return [
            remote(tile_of(side_grad, 0, i), tile_of(mate_grad, 0, i), gsend.at[i], grecv.at[i], mate),
            remote(tile_of(side_out, 0, i), tile_of(mate_out, 0, i), gsend.at[B + i], grecv.at[B + i], mate),
        ]

    def cross_copy(i):
        n = 2 * B
        return [
            remote(tile_of(cross_grad, 0, i), tile_of(pre_grad, 0, i), gsend.at[n + i], grecv.at[n + i], mate),
            remote(tile_of(cross_out, 0, i), tile_of(pre_out, 0, i), gsend.at[n + B + i], grecv.at[n + B + i], mate),
        ]

    def far_copy(i):
        n = 4 * B + i
        return remote(tile_of(far_grad, 0, i), tile_of(pair_grad, 0, i), gsend.at[n], grecv.at[n], pair)

    def feed(t):
        i, kind = t // 4, lax.rem(t, 4)
        n = jnp.where(kind == 2, 3, jnp.where(kind == 3, 2, kind))

        @pl.when(kind == 1)
        def _():
            mlp_copy(1, i).wait_recv()

        @pl.when(kind == 2)
        def _():
            mlp_copy(3, i).wait_recv()

        rows = pl.ds(pl.multiple_of(n * T + i * BLOCK, BLOCK), BLOCK)
        for s in range(K):
            gate_up = product(mlp[rows], ffns[s, :, 0 : 2 * hz])
            grad_hidden = product(cots[rows], ffns[s, :, 2 * hz :])
            up = gate_up[:, hz:]
            act, slope = gelu_parts(gate_up[:, :hz])
            hidden[s, rows] = (act * up).astype(BF)
            grad_act[s, rows, 0:hz] = (grad_hidden * up * slope).astype(BF)
            grad_act[s, rows, hz : 2 * hz] = (grad_hidden * act).astype(BF)
            outs = against(hidden[s, rows], ffns[s, :, 2 * hz :])
            grads = against(grad_act[s, rows], ffns[s, :, 0 : 2 * hz])
            if s == 0:
                out_tile[...] = outs
                grad_tile[...] = grads
            else:
                out_tile[...] += outs
                grad_tile[...] += grads
        here = pl.ds(pl.multiple_of(i * BLOCK, BLOCK), BLOCK)

        @pl.when(kind == 0)
        def _():
            grad_in[here] = grad_tile[...]
            out_own[here] = middle[here] + out_tile[...]

        @pl.when(kind == 1)
        def _():
            side_grad[here] = grad_tile[...].astype(BF)
            side_out[here] = out_tile[...].astype(BF)
            for copy in grad_copy(i):
                copy.start()

        @pl.when(kind == 2)
        def _():
            cross_grad[here] = grad_tile[...].astype(BF)
            cross_out[here] = out_tile[...].astype(BF)
            for copy in cross_copy(i):
                copy.start()

        @pl.when(kind == 3)
        def _():
            for copy in cross_copy(i):
                copy.wait_recv()
            far_grad[here] = (grad_tile[...] + pre_grad[here].astype(F32)).astype(BF)
            out_far[here] = (out_tile[...] + pre_out[here].astype(F32)).astype(BF)
            far_copy(i).start()

    loop(4, feed)
    for i in range(1, B):
        mlp_copy(2, i).wait_recv()
        mlp_copy(3, i).start()
        loop(4, lambda t: feed(t + 4 * i))

    far.finish()

    def weight_tile(t):
        rows = at(t, BLOCK)
        for s in range(K):
            ffns[s, rows, 0 : 2 * hz] = inner(mlp[:, rows], grad_act[s]).astype(BF)
            ffns[s, rows, 2 * hz :] = inner(cots[:, rows], hidden[s]).astype(BF)

    loop(D // BLOCK, weight_tile)
    save_grads = pltpu.make_async_copy(ffns, grads_out, gsem.at[0])
    save_grads.start()

    def join(t):
        rows = at(t, 64)
        out_own[rows] = out_own[rows] + mate_out[rows].astype(F32)
        grad_in[rows] = grad_in[rows] + mate_grad[rows].astype(F32) + pair_grad[rows].astype(F32)

    for i in range(B):
        for copy in grad_copy(i):
            copy.wait()
        for copy in cross_copy(i):
            copy.wait_send()
        far_copy(i).wait()
        for n in (1, 2, 3):
            mlp_copy(n, i).wait_send()
    loop(T // 64, join)
    for save in (save_slabs, save_query, save_bias, save_window, save_att, save_lse, save_grads):
        save.wait()
    behind(mark_own, mark_place, 0, "sent")
    behind(key_place(2), key_place, 3, "sent")
    cot_pair.wait_send()
    cot_pass.wait_send()
    if with_slab:
        near.finish()
        near_out.finish()


def forward(shape, with_slab, tokens, cot, marks, slab, ffn):
    X, Y, Z = sides(shape)
    R = shape[0]
    T, D = tokens.shape
    E, hz = H * DH, ffn.shape[1] // 3
    W = slab.shape[1]
    B = T // BLOCK
    span = WINDOW + BLOCK
    K = Z // 2
    S, V = jax.ShapeDtypeStruct, pltpu.VMEM
    outs = [
        S((T, D), F32), S((T, D), F32), S((T, D), F32), S((T, D), BF),
        S((D, W), BF), S((T, E), BF), S((3 * T, 2 * DH), BF), S((B, span, BLOCK), F32),
        S((E, T), BF), S((H * B, 8, BLOCK), F32), S((K, D, 3 * hz), BF),
    ]
    near, far = gather_count(X, Y, Z), gather_count(X, Y, K)
    scratch = [
        V((D, W), BF), V((K, D, 3 * hz), BF), V((T, E), BF), V((3 * T, 2 * DH), BF),
        V((DH, 3 * T), BF), V((8, 3 * T), F32), V((B, span, BLOCK), F32), V((E, T), BF),
        V((H * B, 8, BLOCK), F32), V((8, D), F32), V((4 * T, D), BF), V((4 * T, D), BF),
        V((BLOCK, D), F32), V((BLOCK, D), F32), V((K, 4 * T, hz), BF), V((K, 4 * T, 2 * hz), BF),
        *[V((T, D), BF)] * 10,
        *[DMA((near,))] * 4, *[DMA((far,))] * 2, *[DMA((2 * R * Z,))] * 2, *[DMA((6,))] * 2,
        *[DMA((3,))] * 2, *[DMA((3 * B,))] * 2, *[DMA((5 * B,))] * 2, DMA((7,)), DMA((1,)),
    ]
    return pl.pallas_call(
        functools.partial(forward_kernel, shape, with_slab, (D, T, W, hz)),
        out_shape=outs,
        in_specs=[VM, ANY, VM, VM if with_slab else ANY, VM],
        out_specs=[VM] * 4 + [ANY] * 7,
        scratch_shapes=scratch,
        compiler_params=pltpu.CompilerParams(
            collective_id=0, has_side_effects=True, vmem_limit_bytes=62 << 20
        ),
        name="forward",
    )(tokens, cot, marks, slab, ffn)


def backward_kernel(shape, with_slab, sizes, *refs):
    D, T, W, hz = sizes
    E, QK, WO = slab_lanes()
    B = T // BLOCK
    span = WINDOW + BLOCK
    refs = list(refs)

    def some(n):
        taken = refs[:n]
        del refs[:n]
        return taken

    (tokens_in, cot_in, grad_in_in, middle_in, out_own_in, out_far,
     slabs_in, query_in, window_in, bias_in, att_in, lse_in, grads) = some(13)
    output, grad_tokens, ffn_out, out_slab, query_slab, rest_slab = some(6)
    (tokens, cot, middle, grad_in, slabs, query, window, bias, att, lse, out_own, out_pair,
     gains, keys_t, branch, att_grad, query_grad_t, query_grad, kv_sum, kv_send, kv_recv, kv_grad, attn_in_t,
     gain_rows, termx, termy, own) = some(27)
    weight_grads = some(3)
    fwork = some(4)
    if with_slab:
        crossed = some(3)
        works = [some(4) for _ in range(3)]
    fsend, frecv, ksend, krecv, lsem, tsem = some(6)
    if with_slab:
        nsems = some(6)
        xsend, xrecv = some(2)
    p = Place(shape)
    pack = Pack(p, T)
    mate, spot = pack.mate, pack.spot
    K = p.Z // 2
    br = D // p.R

    def part(s, r):
        return grads.at[s, at(r, br)]

    def cut(ref, h):
        rows = ref.shape[0] // 2
        return ref.at[pl.ds(h * rows, rows)]

    ready = pack.greet()
    order = list(range(1, K)) + [0]
    terms = {}
    for s in order:
        copies = []
        for d in p.xs:
            copies.append((cut(part(s, p.row_at(dx=d)), 1), termx.at[s, d - 1]))
        for e in p.ys:
            copies.append((cut(part(s, p.row_at(dy=e)), 0), termy.at[s, e - 1]))
        copies.append((part(s, p.row), own.at[s]))
        n = s * (p.X + p.Y - 1)
        terms[s] = [
            pltpu.make_async_copy(a, b, tsem.at[n + i]) for i, (a, b) in enumerate(copies)
        ]
    pairs = [
        (middle_in, middle), (grad_in_in, grad_in), (cot_in, cot), (slabs_in, slabs), (att_in, att),
        (tokens_in, tokens), (window_in, window), (query_in, query), (bias_in, bias), (lse_in, lse),
        (out_own_in, out_own),
    ]
    loads = [pltpu.make_async_copy(a, b, lsem.at[n]) for n, (a, b) in enumerate(pairs)]
    for load in loads:
        load.start()
    for s in order:
        for copy in terms[s]:
            copy.start()
    ready()
    far = Scatter(
        part, cut, p, Sems(fsend, frecv),
        lambda s, d: termx.at[s, d - 1], lambda s, e: termy.at[s, e - 1], lambda s: own.at[s],
        *fwork, 2
    )
    ticks = []
    for j in range(K + 1):
        tick = []
        if j >= 1:
            tick.append(("third", order[j - 1]))
        if j < K:
            tick.append(("second", order[j]))
        if j + 2 < K:
            tick.append(("first", order[j + 2]))
        ticks.append(tick)

    def advance():
        if ticks:
            for step, s in ticks.pop(0):
                if step == "first":
                    far.first(s)
                elif step == "second":
                    for copy in terms[s]:
                        copy.wait()
                    far.second(s)
                else:
                    far.third(s, ffn_out)

    for s in order[:2]:
        far.first(s)
    out_copy = remote(out_far, out_pair, ksend.at[2], krecv.at[2], pack.pair)
    out_copy.start()

    for load in loads[:4]:
        load.wait()
    gains[...] = slabs[:, QK:WO].astype(F32).T[0:8]
    gain_rows[...] = jnp.zeros_like(gain_rows)

    def fold_rows(value):
        return jnp.sum(value.reshape(value.shape[0] // 8, 8, D), axis=0)

    def second_norm(t, total):
        rows = at(t, 64)
        value, grad = middle[rows], grad_in[rows]
        scale = rms_scale(value)
        total = total + fold_rows(grad * (value * scale))
        n = grad * gains[1:2]
        out = cot[rows].astype(F32) + scale * n - value * (
            scale * scale * scale * jnp.mean(n * value, axis=-1, keepdims=True)
        )
        grad_in[rows] = out
        branch[rows] = out.astype(BF)
        return total

    total = lax.fori_loop(0, T // 64, second_norm, jnp.zeros((8, D), F32))
    gain_rows[1:2] = jnp.sum(total, axis=0, keepdims=True)

    def attended_grad(t):
        att_grad[at(t, BLOCK)] = against(slabs[at(t, BLOCK), WO:], branch[...]).astype(BF)

    loop(E // BLOCK, attended_grad)
    loads[4].wait()
    ar = D // (p.R * p.Z * 2)
    blocks = BLOCK // (2 * ar)

    def put(ref, t, lanes, value):
        if with_slab:
            ref[pl.ds(t * blocks, blocks), :, :, lanes] = value.astype(BF).reshape(
                blocks, 2, ar, value.shape[1]
            )
        else:
            ref[at(t, BLOCK), lanes] = value.astype(BF)

    def out_weight_grad(t):
        put(weight_grads[0], t, slice(0, E), product(att[at(t, BLOCK)], branch[...]))

    loop(E // BLOCK, out_weight_grad)

    class Near:
        def __init__(self, n):
            self.n, self.ref = n, weight_grads[n]
            self.copy = remote(
                self.ref.at[:, 1 - p.core], crossed[n], xsend.at[n], xrecv.at[n], mate
            )
            self.copy.start()

        def block(self, s, r):
            return self.ref.at[r * p.Z + p.z_at(s), p.core]

        def fold(self):
            self.copy.wait()
            ref, other = self.ref, crossed[self.n]

            def step(n):
                ref[n, p.core] = (ref[n, p.core].astype(F32) + other[n].astype(F32)).astype(BF)

            loop(p.R * p.Z, step)
            block = self.block
            self.scatter = Scatter(
                block, cut, p, Sems(*nsems[2 * self.n : 2 * self.n + 2]),
                lambda s, d: cut(block(s, p.row_at(dx=d)), 1),
                lambda s, e: cut(block(s, p.row_at(dy=e)), 0),
                lambda s: block(s, p.row), *works[self.n]
            )
            for s in self.order():
                self.scatter.first(s)

        def order(self):
            return list(range(1, p.Z)) + [0]

        def second(self):
            for s in self.order():
                self.scatter.second(s)

        def third(self):
            for s in self.order()[:-1]:
                self.scatter.third(s)

        def last(self, out):
            self.scatter.third(0, out)
            self.scatter.finish()

    if with_slab:
        near_out = Near(0)

    for load in loads[5:]:
        load.wait()

    def first_norm(t):
        cols = at(t, 128)
        value = tokens[cols].astype(F32)
        attn_in_t[:, cols] = (value * rms_scale(value) * gains[0:1]).astype(BF).T

    loop(T // 128, first_norm)
    keys_t[...] = window[:, 0:DH].T
    kv_sum[...] = jnp.zeros_like(kv_sum)
    if with_slab:
        near_out.fold()

    factor = LOG2E / math.sqrt(DH)
    scale = 1.0 / math.sqrt(DH)

    def head(i, h):
        lanes = at(h, DH)
        here = pl.ds(i * BLOCK, BLOCK)
        seen = pl.ds(i * BLOCK, span)
        part_query = query[here, lanes]
        part_grad = att_grad[lanes, here]
        scores = against(window[seen, 0:DH], part_query) * factor + bias[i]
        probs = jnp.exp2(scores - lse[h * B + i][0:1])
        grad_probs = product(window[seen, DH:], part_grad)
        centre = jnp.sum(
            att[lanes, here].astype(F32) * part_grad.astype(F32), axis=0, keepdims=True
        )
        grad_scores = (probs * (grad_probs - centre)).astype(BF)
        kv_sum[seen, DH:] += against(probs.astype(BF), part_grad)
        kv_sum[seen, 0:DH] += product(grad_scores, part_query)
        query_grad_t[lanes, here] = (product(keys_t[:, seen], grad_scores) * scale).astype(BF)

    pieces = [(i, g) for i in range(B) for g in range(4)]
    for n, (i, g) in enumerate(pieces):
        loop(H // 4, lambda k: head(i, g * (H // 4) + k))
        if with_slab and n == 2:
            near_out.second()
        if with_slab and n == 5:
            near_out.third()
        if n in (1, 4, 7):
            advance()

    kv_send[:, 0:DH] = (kv_sum[pl.ds(0, 2 * T), 0:DH] * scale).astype(BF)
    kv_send[:, DH:] = kv_sum[pl.ds(0, 2 * T), DH:].astype(BF)
    returns = []
    for d in (1, 2):
        to = (p.row, lax.rem(p.col - d + 2 * p.Z, 2 * p.Z))
        copy = remote(
            kv_send.at[pl.ds((2 - d) * T, T)], kv_recv.at[d - 1], ksend.at[d - 1], krecv.at[d - 1], to
        )
        pl.when(spot - d >= 0)(copy.start)
        returns.append((d, copy))

    def turn(t):
        query_grad[at(t, BLOCK)] = query_grad_t[:, at(t, BLOCK)].T

    loop(B, turn)

    def query_weight_grad(t):
        put(weight_grads[1], t, slice(0, E), product(attn_in_t[at(t, BLOCK)], query_grad[...]))

    loop(D // BLOCK, query_weight_grad)
    if with_slab:
        near_query = Near(1)

    def input_grad_query(t):
        rows = at(t, 128)
        grad_tokens[rows] = against(query_grad[rows], slabs[:, 0:E])

    loop(T // 128, input_grad_query)
    kv_grad[:, 0:DH] = kv_sum[pl.ds(2 * T, T), 0:DH] * scale
    kv_grad[:, DH:] = kv_sum[pl.ds(2 * T, T), DH:]
    if with_slab:
        near_query.fold()
    for d, copy in returns:
        @pl.when(spot + d < pack.size)
        def _():
            copy.wait_recv()
            kv_grad[...] += kv_recv[d - 1].astype(F32)

    window[pl.ds(0, T)] = kv_grad[...].astype(BF)

    def keyval_weight_grad(t):
        put(weight_grads[2], t, slice(0, 2 * DH), product(attn_in_t[at(t, BLOCK)], window[pl.ds(0, T)]))

    loop(D // BLOCK, keyval_weight_grad)

    def input_grad(t, total):
        rows = at(t, 128)
        grad = grad_tokens[rows] + against(window[rows], slabs[:, E:QK])
        value = tokens[rows].astype(F32)
        scale_first = rms_scale(value)
        total = total + fold_rows(grad * (value * scale_first))
        m = grad * gains[0:1]
        grad_tokens[rows] = grad_in[rows] + scale_first * m - value * (
            scale_first * scale_first * scale_first * jnp.mean(m * value, axis=-1, keepdims=True)
        )
        return total

    total = lax.fori_loop(0, T // 128, input_grad, jnp.zeros((8, D), F32))
    gain_rows[0:1] = jnp.sum(total, axis=0, keepdims=True)

    def gain_grad(t):
        put(weight_grads[2], t, slice(2 * DH, 2 * DH + 128), gain_rows[:, at(t, BLOCK)].T)

    loop(D // BLOCK, gain_grad)
    if with_slab:
        near_rest = Near(2)
        near_query.second()
        near_rest.fold()
        near_query.third()
        near_rest.second()
        near_out.last(out_slab)
        near_rest.third()
    else:
        for ref, out in zip(weight_grads, (out_slab, query_slab, rest_slab)):
            out[...] = ref[...]
    out_copy.wait_recv()

    def join(t):
        rows = at(t, 64)
        output[rows] = (out_own[rows] + out_pair[rows].astype(F32)).astype(BF)

    loop(T // 64, join)
    while ticks:
        advance()
    if with_slab:
        near_query.last(query_slab)
        near_rest.last(rest_slab)
    out_copy.wait_send()
    for d, copy in returns:
        pl.when(spot - d >= 0)(copy.wait_send)
    far.finish()


def backward(
    shape, with_slab, tokens, cot, grad_in, middle, out_own, out_far, slabs, query, window, bias, att, lse, grads
):
    X, Y, Z = sides(shape)
    R = shape[0]
    T, D = tokens.shape
    E, hz = H * DH, grads.shape[2] // 3
    W = slabs.shape[1]
    B = T // BLOCK
    span = WINDOW + BLOCK
    K = Z // 2
    near, far = scatter_count(X, Y, Z), scatter_count(X, Y, K)
    S, V = jax.ShapeDtypeStruct, pltpu.VMEM
    block = (D // R, 3 * hz)
    half = (block[0] // 2, block[1])
    widths = (E, E, 2 * DH + 128)
    ar = D // (R * Z * 2)
    if with_slab:
        slab_outs = [S((ar, w), F32) for w in widths]
        slab_work = [V((R * Z, 2, ar, w), BF) for w in widths]
    else:
        slab_outs = [S((D, w), BF) for w in widths]
        slab_work = [V((D, w), BF) for w in widths]
    outs = [S((T, D), BF), S((T, D), F32), S(block, F32)] + slab_outs
    scratch = [
        V((T, D), BF), V((T, D), BF), V((T, D), F32), V((T, D), F32), V((D, W), BF), V((T, E), BF),
        V((3 * T, 2 * DH), BF), V((B, span, BLOCK), F32), V((E, T), BF), V((H * B, 8, BLOCK), F32),
        V((T, D), F32), V((T, D), BF),
        V((8, D), F32), V((DH, 3 * T), BF), V((T, D), BF), V((E, T), BF), V((E, T), BF), V((T, E), BF),
        V((3 * T, 2 * DH), F32), V((2 * T, 2 * DH), BF), V((2, T, 2 * DH), BF), V((T, 2 * DH), F32),
        V((D, T), BF), V((128, D), F32),
        V((K, X - 1) + half, BF), V((K, Y - 1) + half, BF), V((K,) + block, BF),
        *slab_work,
        *scatter_scratch(X, Y, K, block),
    ]
    if with_slab:
        scratch += [V((R * Z, ar, w), BF) for w in widths]
        for w in widths:
            scratch += scatter_scratch(X, Y, Z, (ar, w))
    scratch += [
        DMA((far,)), DMA((far,)), DMA((3,)), DMA((3,)), DMA((11,)), DMA((K * (X + Y - 1),)),
    ]
    if with_slab:
        scratch += [DMA((near,))] * 6 + [DMA((3,))] * 2
    return pl.pallas_call(
        functools.partial(backward_kernel, shape, with_slab, (D, T, W, hz)),
        out_shape=outs,
        in_specs=[ANY] * 13,
        out_specs=[VM] * 6,
        scratch_shapes=scratch,
        compiler_params=pltpu.CompilerParams(
            collective_id=1, has_side_effects=True, vmem_limit_bytes=62 << 20
        ),
        name="backward",
    )(tokens, cot, grad_in, middle, out_own, out_far, slabs, query, window, bias, att, lse, grads)


def shards(
    shape,
    tokens, gain_attn, w_query, w_keyval, w_out, gain_mlp, w_gate, w_up, w_down, segment, cotangent
):
    with_slab = w_query.shape[0] % 32 == 0
    ffn = jnp.concatenate([w_gate, w_up, w_down.T], axis=1)
    gain_columns = jnp.pad(jnp.stack([gain_attn, gain_mlp], axis=1), ((0, 0), (0, 126)))
    slab = jnp.concatenate([w_query, w_keyval, gain_columns, w_out], axis=1)
    if not with_slab:
        slab = lax.all_gather(slab, ("row", "col"), axis=0, tiled=True)
    marks = jnp.broadcast_to(segment.astype(F32)[None], (8, segment.shape[0]))
    kept = forward(shape, with_slab, tokens, cotangent, marks, slab, ffn)
    output, grad_tokens, ffn_grad, *slab_grads = backward(shape, with_slab, tokens, cotangent, *kept)
    if not with_slab:
        slab_grads = [
            lax.psum_scatter(g.astype(F32), ("row", "col"), scatter_dimension=0, tiled=True)
            for g in slab_grads
        ]
    out_grad, query_grad, rest_grad = slab_grads
    hz = w_gate.shape[1]
    return (
        output,
        grad_tokens,
        rest_grad[:, 2 * DH],
        query_grad,
        rest_grad[:, : 2 * DH],
        out_grad,
        rest_grad[:, 2 * DH + 1],
        ffn_grad[:, :hz],
        ffn_grad[:, hz : 2 * hz],
        ffn_grad[:, 2 * hz :].T,
    )


def solution(mesh):
    shape = (mesh.shape["row"], mesh.shape["col"])
    return jax.shard_map(
        functools.partial(shards, shape),
        mesh=mesh,
        in_specs=(
            P(("row", "col"), None),
            P(("row", "col")),
            P(("row", "col"), None),
            P(("row", "col"), None),
            P(("row", "col"), None),
            P(("row", "col")),
            P("row", "col"),
            P("row", "col"),
            P("col", "row"),
            P(("row", "col")),
            P(("row", "col"), None),
        ),
        out_specs=(
            P(("row", "col"), None),
            P(("row", "col"), None),
            P(("row", "col")),
            P(("row", "col"), None),
            P(("row", "col"), None),
            P(("row", "col"), None),
            P(("row", "col")),
            P("row", "col"),
            P("row", "col"),
            P("col", "row"),
        ),
        check_vma=False,
    )
```

```python
import functools
import math

import jax
import jax.numpy as jnp
from jax import lax
from jax.experimental import pallas as pl
from jax.experimental.pallas import tpu as pltpu
from jax.sharding import PartitionSpec as P

H = 8
DH = 128
WINDOW = 1024
PACK = 2048

EPS = 1e-06
NEGATIVE = -1e30
MESH = pl.DeviceIdType.MESH
BF = jnp.bfloat16
F32 = jnp.float32


def product(left, right):
    return jnp.dot(left, right, preferred_element_type=jnp.float32)


def inner(left, right):
    return lax.dot_general(
        left, right, (((0,), (0,)), ((), ())), preferred_element_type=jnp.float32
    )


def against(left, right):
    return lax.dot_general(
        left, right, (((1,), (1,)), ((), ())), preferred_element_type=jnp.float32
    )


class Place:
    def __init__(self, shape):
        rows, cols = shape
        self.X = math.isqrt(rows)
        while rows % self.X:
            self.X -= 1
        self.Y = rows // self.X
        self.Z = cols // 2
        self.R = rows
        self.row, self.col = lax.axis_index("row"), lax.axis_index("col")
        self.y, self.x = self.row // self.X, self.row % self.X
        self.z, self.core = self.col // 2, self.col % 2
        self.xs, self.ys, self.zs = range(1, self.X), range(1, self.Y), range(1, self.Z)

    def row_at(self, dy=0, dx=0):
        return lax.rem(self.y + dy + self.Y, self.Y) * self.X + lax.rem(
            self.x + dx + self.X, self.X
        )

    def z_at(self, dz):
        return lax.rem(self.z + dz + self.Z, self.Z)

    def device(self, dy=0, dx=0, dz=0, other=False):
        core = 1 - self.core if other else self.core
        return (self.row_at(dy, dx), self.z_at(dz) * 2 + core)


def remote(src, dst, send, recv, device):
    return pltpu.make_async_remote_copy(
        src_ref=src, dst_ref=dst, send_sem=send, recv_sem=recv, device_id=device,
        device_id_type=MESH,
    )


class Sems:
    def __init__(self, send, recv):
        self.send, self.recv, self.count = send, recv, 0

    def take(self):
        self.count += 1
        return self.send.at[self.count - 1], self.recv.at[self.count - 1]


def gather_count(X, Y, K):
    return (K - 1) + K * ((X - 1) + (Y - 1) + 2 * (X - 1) * (Y - 1))


class Gather:
    def __init__(self, at, dest, here, sems, own, stride=1):
        self.at, self.dest, self.p, self.own = at, dest, here, own
        self.stride, self.K = stride, here.Z // stride
        self.sent = []
        p = here
        self.zsem = {k: sems.take() for k in range(1, self.K)}
        self.xsem = {(s, d): sems.take() for s in range(self.K) for d in p.xs}
        self.ysem = {(s, d): sems.take() for s in range(self.K) for d in p.ys}
        self.dsem = {
            (s, h, dx, dy): sems.take()
            for s in range(self.K) for h in (0, 1) for dx in p.xs for dy in p.ys
        }

    def push(self, src, dst, sem, device):
        copy = remote(src, dst, sem[0], sem[1], device)
        copy.start()
        self.sent.append(copy)

    def arrive(self, place, sem):
        remote(place, place, sem[0], sem[1], self.p.device(other=True)).wait_recv()

    def spread_z(self):
        p = self.p
        for k in range(1, self.K):
            self.push(self.own, self.dest(k), self.zsem[k], p.device(dz=-self.stride * k))

    def spread_xy(self, s):
        if s >= self.K:
            return
        p = self.p
        place = self.at(s, p.row, None)
        src = self.own
        if s:
            self.arrive(place, self.zsem[s])
            src = place
        for d in p.xs:
            self.push(src, place, self.xsem[s, d], p.device(dx=d))
        for d in p.ys:
            self.push(src, place, self.ysem[s, d], p.device(dy=d))

    def spread_diagonal(self, s):
        if s >= self.K:
            return
        p = self.p
        for d in p.xs:
            r = p.row_at(dx=-d)
            self.arrive(self.at(s, r, None), self.xsem[s, d])
            half = self.at(s, r, 0)
            for e in p.ys:
                self.push(half, half, self.dsem[s, 0, d, e], p.device(dy=e))
        for e in p.ys:
            r = p.row_at(dy=-e)
            self.arrive(self.at(s, r, None), self.ysem[s, e])
            half = self.at(s, r, 1)
            for d in p.xs:
                self.push(half, half, self.dsem[s, 1, d, e], p.device(dx=d))

    def close(self, s):
        p = self.p
        for d in p.xs:
            for e in p.ys:
                r = p.row_at(dy=-e, dx=-d)
                for h in (0, 1):
                    self.arrive(self.at(s, r, h), self.dsem[s, h, d, e])

    def finish(self):
        for copy in self.sent:
            copy.wait_send()


def scatter_count(X, Y, K):
    return (K - 1) + K * (2 * (X - 1) * (Y - 1) + 2 * (X - 1) + 2 * (Y - 1))


class Scatter:
    def __init__(
        self, part, cut, here, sems, termx, termy, own, diag, fromx, fromy, fromz, stride=1
    ):
        self.part, self.cut, self.p = part, cut, here
        self.termx, self.termy, self.own = termx, termy, own
        self.diag, self.fromx, self.fromy, self.fromz = diag, fromx, fromy, fromz
        self.stride, self.K = stride, here.Z // stride
        self.sent = []
        p = here
        self.zsem = {k: sems.take() for k in range(1, self.K)}
        self.xsem = {(s, h, d): sems.take() for s in range(self.K) for h in (0, 1) for d in p.xs}
        self.ysem = {(s, h, d): sems.take() for s in range(self.K) for h in (0, 1) for d in p.ys}
        self.dsem = {
            (s, h, dx, dy): sems.take()
            for s in range(self.K) for h in (0, 1) for dx in p.xs for dy in p.ys
        }

    def push(self, src, dst, sem, device):
        copy = remote(src, dst, sem[0], sem[1], device)
        copy.start()
        self.sent.append(copy)

    def arrive(self, place, sem):
        remote(place, place, sem[0], sem[1], self.p.device(other=True)).wait_recv()

    def spot(self, d, e):
        return (d - 1) * (self.p.Y - 1) + e - 1

    def first(self, s):
        p, cut = self.p, self.cut
        for d in p.xs:
            for e in p.ys:
                far = self.part(s, p.row_at(dy=e, dx=d))
                n = self.spot(d, e)
                self.push(cut(far, 0), self.diag.at[s, 0, n], self.dsem[s, 0, d, e], p.device(dx=d))
                self.push(cut(far, 1), self.diag.at[s, 1, n], self.dsem[s, 1, d, e], p.device(dy=e))
        for d in p.xs:
            near = self.part(s, p.row_at(dx=d))
            self.push(cut(near, 0), cut(self.fromx.at[s, d - 1], 0), self.xsem[s, 0, d], p.device(dx=d))
        for e in p.ys:
            near = self.part(s, p.row_at(dy=e))
            self.push(cut(near, 1), cut(self.fromy.at[s, e - 1], 1), self.ysem[s, 1, e], p.device(dy=e))

    def second(self, s):
        p, cut = self.p, self.cut
        for e in p.ys:
            term = self.termy(s, e)
            total = term[...].astype(F32)
            for d in p.xs:
                place = self.diag.at[s, 0, self.spot(d, e)]
                self.arrive(place, self.dsem[s, 0, d, e])
                total = total + place[...].astype(F32)
            term[...] = total.astype(BF)
            self.push(term, cut(self.fromy.at[s, e - 1], 0), self.ysem[s, 0, e], p.device(dy=e))
        for d in p.xs:
            term = self.termx(s, d)
            total = term[...].astype(F32)
            for e in p.ys:
                place = self.diag.at[s, 1, self.spot(d, e)]
                self.arrive(place, self.dsem[s, 1, d, e])
                total = total + place[...].astype(F32)
            term[...] = total.astype(BF)
            self.push(term, cut(self.fromx.at[s, d - 1], 1), self.xsem[s, 1, d], p.device(dx=d))

    def third(self, s, out=None):
        p, cut = self.p, self.cut
        own = self.own(s)
        total = own[...].astype(F32)
        for d in p.xs:
            for h in (0, 1):
                self.arrive(cut(self.fromx.at[s, d - 1], h), self.xsem[s, h, d])
            total = total + self.fromx[s, d - 1].astype(F32)
        for e in p.ys:
            for h in (0, 1):
                self.arrive(cut(self.fromy.at[s, e - 1], h), self.ysem[s, h, e])
            total = total + self.fromy[s, e - 1].astype(F32)
        if s:
            own[...] = total.astype(BF)
            self.push(own, self.fromz.at[s - 1], self.zsem[s], p.device(dz=self.stride * s))
            return
        for k in range(1, self.K):
            self.arrive(self.fromz.at[k - 1], self.zsem[k])
            total = total + self.fromz[k - 1].astype(F32)
        out[...] = total

    def finish(self):
        for copy in self.sent:
            copy.wait_send()


def scatter_scratch(X, Y, K, block):
    half = (block[0] // 2, block[1])
    return [
        pltpu.VMEM((K, 2, (X - 1) * (Y - 1)) + half, BF),
        pltpu.VMEM((K, X - 1) + block, BF),
        pltpu.VMEM((K, Y - 1) + block, BF),
        pltpu.VMEM((max(K - 1, 1),) + block, BF),
    ]


def sides(shape):
    x = math.isqrt(shape[0])
    while shape[0] % x:
        x -= 1
    return x, shape[0] // x, shape[1] // 2


VM = pl.BlockSpec(memory_space=pltpu.VMEM)
ANY = pl.BlockSpec(memory_space=pl.ANY)
DMA = pltpu.SemaphoreType.DMA
LOG2E = math.log2(math.e)
BLOCK = 256


def loop(count, body):
    def step(t, carry):
        body(t)
        return carry

    lax.fori_loop(0, count, step, 0)


def at(t, size):
    return pl.ds(pl.multiple_of(t * size, size), size)


def rms_scale(value):
    return lax.rsqrt(jnp.mean(value * value, axis=-1, keepdims=True) + EPS)


def gelu_parts(gate):
    square = gate * gate
    t = jnp.tanh(gate * (0.7978845608 + (0.7978845608 * 0.044715) * square))
    half = 0.5 + 0.5 * t
    slope = half + (0.5 * gate) * (1.0 - t * t) * (
        0.7978845608 + (3 * 0.7978845608 * 0.044715) * square
    )
    return gate * half, slope


class Pack:
    def __init__(self, here, T):
        p = here
        self.p, self.size = p, PACK // T
        self.spot = lax.rem(p.col, self.size)
        pair = (p.z // 2) * 2 + 1 - lax.rem(p.z, 2)
        self.mate = p.device(other=True)
        self.pair = (p.row, pair * 2 + p.core)
        self.across = (p.row, pair * 2 + 1 - p.core)

    def greet(self):
        p = self.p
        barrier = pltpu.get_barrier_semaphore()
        mates = [p.device(dx=d) for d in p.xs] + [p.device(dy=d) for d in p.ys]
        mates += [p.device(dz=d) for d in p.zs] + [self.mate, self.across]
        for mate in mates:
            pl.semaphore_signal(barrier, inc=1, device_id=mate, device_id_type=MESH)
        return lambda: pl.semaphore_wait(barrier, len(mates))


def slab_lanes():
    E, QK = H * DH, H * DH + 2 * DH
    return E, QK, QK + 128


def forward_kernel(shape, with_slab, sizes, *refs):
    D, T, W, hz = sizes
    (tokens, cot, segment, w_gate, w_up, w_down, *slab_in) = refs[: 10 if with_slab else 7]
    (grad_in, middle, out_own, out_far, slabs_out, query_out, window_out, bias_out, att_out, lse_out, grads_out,
     slabs, ffns, query, window, values_t, marks_all, bias, att, lse, gains, mlp, cots,
     grad_tile, out_tile, hidden, grad_act, side_grad, side_out, cross_grad, cross_out, far_grad,
     mate_grad, mate_out, pre_grad, pre_out, pair_grad,
     vsend, vrecv, asend, arecv, osend, orecv, fsend, frecv, csend, crecv, ksend, krecv, tsend, trecv,
     msend, mrecv, gsend, grecv, lsem, gsem) = refs[10 if with_slab else 7 :]
    p = Place(shape)
    pack = Pack(p, T)
    mate, pair, spot = pack.mate, pack.pair, pack.spot
    E, QK, WO = slab_lanes()
    B = T // BLOCK
    span = WINDOW + BLOCK
    K = p.Z // 2

    def local(src, dst, n):
        copy = pltpu.make_async_copy(src, dst, lsem.at[n])
        copy.start()
        return copy

    ready = pack.greet()
    load_cot = local(cot, cots.at[pl.ds(0, T)], 0)
    if not with_slab:
        load_slab = local(slab_in[0], slabs, 1)
    br = w_gate.shape[0]
    own_rows = at(p.row, br)
    ffns[0, own_rows, 0:hz] = w_gate[...]
    ffns[0, own_rows, hz : 2 * hz] = w_up[...]
    ffns[0, own_rows, 2 * hz :] = w_down[...].T

    def ffn_at(s, r, half):
        if half is None:
            return ffns.at[s, at(r, br)]
        return ffns.at[s, pl.ds(pl.multiple_of(r * br + half * (br // 2), br // 2), br // 2)]

    far = Gather(
        ffn_at, lambda k: ffn_at(k, p.row, None), p, Sems(fsend, frecv), ffn_at(0, p.row, None), 2
    )

    if with_slab:
        ar = slab_in[0].shape[0]
        slab_rows = pl.ds(pl.multiple_of(((p.row * p.Z + p.z) * 2 + p.core) * ar, ar), ar)
        widths = ((0, E), (E, QK), (QK, WO), (WO, W))
        for piece, (start, stop) in zip(slab_in, widths):
            slabs[slab_rows, start:stop] = piece[...]

        def slab_place(lanes, core):
            def place(s, r, half):
                start = ((r * p.Z + p.z_at(s)) * 2 + core) * ar
                if half is None:
                    return slabs.at[pl.ds(pl.multiple_of(start, ar), ar), lanes]
                start = pl.multiple_of(start + half * (ar // 2), ar // 2)
                return slabs.at[pl.ds(start, ar // 2), lanes]

            return place

        def slab_gather(lanes, sems):
            place = slab_place(lanes, p.core)
            own = place(0, p.row, None)
            return Gather(place, lambda k: own, p, sems, own)

        rest_lanes, act_lanes, out_lanes = slice(E, WO), slice(0, E), slice(WO, W)
        near_rest = slab_gather(rest_lanes, Sems(vsend, vrecv))
        near = slab_gather(act_lanes, Sems(asend, arecv))
        near_out = slab_gather(out_lanes, Sems(osend, orecv))
        hands = Sems(csend, crecv)

        def hand(gather, lanes):
            mine, theirs = slab_place(lanes, p.core), slab_place(lanes, 1 - p.core)
            passed = []
            for s in range(p.Z):
                gather.close(s)
                for dy in range(p.Y):
                    for dx in range(p.X):
                        r = p.row_at(dy, dx)
                        send, recv = hands.take()
                        place, other = mine(s, r, None), theirs(s, r, None)
                        copy = remote(place, place, send, recv, mate)
                        copy.start()
                        passed.append((copy, remote(other, other, send, recv, mate)))
            return passed

        def settle(passed):
            for copy, arrival in passed:
                copy.wait_send()
                arrival.wait_recv()

    ready()
    if with_slab:
        near_rest.spread_z()
        near_rest.spread_xy(0)
        near.spread_z()
        near.spread_xy(0)
        near_out.spread_z()

    marks_all[:, pl.ds(2 * T, T)] = jnp.broadcast_to(segment[...].astype(F32), (8, T))

    @pl.when(spot == 0)
    def _():
        window[pl.ds(0, 2 * T), :] = jnp.zeros((2 * T, 2 * DH), BF)
        marks_all[:, pl.ds(0, 2 * T)] = jnp.full((8, 2 * T), -1.0, F32)

    @pl.when(spot == 1)
    def _():
        window[pl.ds(0, T), :] = jnp.zeros((T, 2 * DH), BF)
        marks_all[:, pl.ds(0, T)] = jnp.full((8, T), -1.0, F32)

    def behind(src, place, n, op):
        for d in (1, 2):
            to = (p.row, lax.rem(p.col + d, 2 * p.Z))
            copy = remote(src, place(2 - d), ksend.at[n + d], krecv.at[n + d], to)
            if op == "start":
                pl.when(spot + d < pack.size)(copy.start)
            elif op == "arrive":
                pl.when(spot - d >= 0)(copy.wait_recv)
            else:
                pl.when(spot + d < pack.size)(copy.wait_send)

    mark_place = lambda k: marks_all.at[:, pl.ds(k * T, T)]
    mark_own = mark_place(2)
    behind(mark_own, mark_place, 0, "start")

    def whole(ref, n):
        return ref.at[pl.ds(n * T, T)]

    load_cot.wait()
    cot_mate = remote(whole(cots, 0), whole(cots, 1), tsend.at[0], trecv.at[0], mate)
    cot_mate.start()

    def tile_of(ref, n, i):
        return ref.at[pl.ds(pl.multiple_of(n * T + i * BLOCK, BLOCK), BLOCK)]

    def cot_copy(n, i):
        to, src, sem = (pair, 0, 1 + i) if n == 2 else (mate, 2, 1 + B + i)
        return remote(tile_of(cots, src, i), tile_of(cots, n, i), tsend.at[sem], trecv.at[sem], to)

    if with_slab:
        for s in range(p.Z):
            near_rest.spread_xy(s + 1)
            near_rest.spread_diagonal(s)
        for s in range(1, p.Z):
            near.spread_xy(s)
        passed = hand(near_rest, rest_lanes)
        for s in range(p.Z):
            near.spread_diagonal(s)
        settle(passed)
    else:
        load_slab.wait()
    gains[...] = slabs[:, QK:WO].astype(F32).T[0:8]

    def first_norm(t):
        rows = at(t, 64)
        value = tokens[rows].astype(F32)
        mlp[rows] = (value * rms_scale(value) * gains[0:1]).astype(BF)

    loop(T // 64, first_norm)
    window[pl.ds(2 * T, T)] = product(mlp[pl.ds(0, T)], slabs[:, E:QK]).astype(BF)
    key_place = lambda k: window.at[pl.ds(k * T, T)]
    behind(key_place(2), key_place, 3, "start")

    far.spread_z()
    cot_copy(2, 0).start()
    if with_slab:
        for s in range(p.Z):
            near_out.spread_xy(s)
        settle(hand(near, act_lanes))

    def project(t):
        query[at(t, BLOCK)] = product(mlp[at(t, BLOCK)], slabs[:, 0:E]).astype(BF)

    loop(B, project)
    save_query = local(query, query_out, 2)
    if with_slab:
        for s in range(p.Z):
            near_out.spread_diagonal(s)
    far.spread_xy(0)
    behind(mark_own, mark_place, 0, "arrive")
    column = jnp.broadcast_to(marks_all[0:1], (128, 3 * T)).T
    for i in range(B):
        keys_at = jnp.concatenate([column[i * BLOCK : i * BLOCK + span]] * (BLOCK // 128), axis=1)
        own = marks_all[0:1, 2 * T + i * BLOCK : 2 * T + (i + 1) * BLOCK]
        gap = (
            WINDOW
            + lax.broadcasted_iota(jnp.int32, (span, BLOCK), 1)
            - lax.broadcasted_iota(jnp.int32, (span, BLOCK), 0)
        )
        allowed = (keys_at == own) & (gap >= 0) & (gap < WINDOW)
        bias[i] = jnp.where(allowed, 0.0, NEGATIVE)
    save_bias = local(bias, bias_out, 3)
    if with_slab:
        passed = hand(near_out, out_lanes)
    behind(key_place(2), key_place, 3, "arrive")
    for i in range(1, B):
        cot_copy(2, i).start()
    save_window = local(window, window_out, 4)
    values_t[...] = window[:, DH:].T
    factor = LOG2E / math.sqrt(DH)

    def head(i, h):
        lanes = at(h, DH)
        keys = window[pl.ds(i * BLOCK, span), 0:DH]
        scores = against(keys, query[pl.ds(i * BLOCK, BLOCK), lanes]) * factor + bias[i]
        top = jnp.max(scores, axis=0, keepdims=True)
        expo = jnp.exp2(scores - top)
        total = jnp.sum(expo, axis=0, keepdims=True)
        mixed = product(values_t[:, pl.ds(i * BLOCK, span)], expo.astype(BF))
        att[lanes, pl.ds(i * BLOCK, BLOCK)] = (mixed / total).astype(BF)
        lse[h * B + i] = jnp.broadcast_to(top + jnp.log2(total), (8, BLOCK))

    def mlp_copy(n, i):
        to = pair if n == 2 else mate
        src = 2 if n == 3 else 0
        sem = (n - 1) * B + i
        return remote(tile_of(mlp, src, i), tile_of(mlp, n, i), msend.at[sem], mrecv.at[sem], to)

    for i in range(B):
        if i == 0:
            loop(H // 2, lambda h: head(i, h))
            far.spread_xy(1)
            far.spread_diagonal(0)
            loop(H // 2, lambda h: head(i, h + H // 2))
            if with_slab:
                settle(passed)
            save_slabs = local(slabs, slabs_out, 1)
        else:
            loop(H, lambda h: head(i, h))
        cols = pl.ds(i * BLOCK, BLOCK)
        middle[cols] = product(att[:, cols].T, slabs[:, WO:]) + tokens[cols].astype(F32)

        def second_norm(t):
            rows = pl.ds(pl.multiple_of(i * BLOCK + t * 64, 64), 64)
            value = middle[rows]
            mlp[rows] = (value * rms_scale(value) * gains[1:2]).astype(BF)

        loop(BLOCK // 64, second_norm)
        mlp_copy(1, i).start()
        mlp_copy(2, i).start()
        cot_copy(2, i).wait_recv()
        cot_copy(3, i).start()
    save_att = local(att, att_out, 5)
    save_lse = local(lse, lse_out, 6)
    for s in range(2, K):
        far.spread_xy(s)
    for s in range(1, K):
        far.spread_diagonal(s)
    mlp_copy(2, 0).wait_recv()
    mlp_copy(3, 0).start()
    for s in range(K):
        far.close(s)
    cot_mate.wait()
    for i in range(B):
        cot_copy(3, i).wait_recv()

    def grad_copy(i):
        return [
            remote(tile_of(side_grad, 0, i), tile_of(mate_grad, 0, i), gsend.at[i], grecv.at[i], mate),
            remote(tile_of(side_out, 0, i), tile_of(mate_out, 0, i), gsend.at[B + i], grecv.at[B + i], mate),
        ]

    def cross_copy(i):
        n = 2 * B
        return [
            remote(tile_of(cross_grad, 0, i), tile_of(pre_grad, 0, i), gsend.at[n + i], grecv.at[n + i], mate),
            remote(tile_of(cross_out, 0, i), tile_of(pre_out, 0, i), gsend.at[n + B + i], grecv.at[n + B + i], mate),
        ]

    def far_copy(i):
        n = 4 * B + i
        return remote(tile_of(far_grad, 0, i), tile_of(pair_grad, 0, i), gsend.at[n], grecv.at[n], pair)

    def feed(t):
        i, kind = t // 4, lax.rem(t, 4)
        n = jnp.where(kind == 2, 3, jnp.where(kind == 3, 2, kind))

        @pl.when(kind == 1)
        def _():
            mlp_copy(1, i).wait_recv()

        @pl.when(kind == 2)
        def _():
            mlp_copy(3, i).wait_recv()

        rows = pl.ds(pl.multiple_of(n * T + i * BLOCK, BLOCK), BLOCK)
        for s in range(K):
            gate_up = product(mlp[rows], ffns[s, :, 0 : 2 * hz])
            grad_hidden = product(cots[rows], ffns[s, :, 2 * hz :])
            up = gate_up[:, hz:]
            act, slope = gelu_parts(gate_up[:, :hz])
            hidden[s, rows] = (act * up).astype(BF)
            grad_act[s, rows, 0:hz] = (grad_hidden * up * slope).astype(BF)
            grad_act[s, rows, hz : 2 * hz] = (grad_hidden * act).astype(BF)
            outs = against(hidden[s, rows], ffns[s, :, 2 * hz :])
            grads = against(grad_act[s, rows], ffns[s, :, 0 : 2 * hz])
            if s == 0:
                out_tile[...] = outs
                grad_tile[...] = grads
            else:
                out_tile[...] += outs
                grad_tile[...] += grads
        here = pl.ds(pl.multiple_of(i * BLOCK, BLOCK), BLOCK)

        @pl.when(kind == 0)
        def _():
            grad_in[here] = grad_tile[...]
            out_own[here] = middle[here] + out_tile[...]

        @pl.when(kind == 1)
        def _():
            side_grad[here] = grad_tile[...].astype(BF)
            side_out[here] = out_tile[...].astype(BF)
            for copy in grad_copy(i):
                copy.start()

        @pl.when(kind == 2)
        def _():
            cross_grad[here] = grad_tile[...].astype(BF)
            cross_out[here] = out_tile[...].astype(BF)
            for copy in cross_copy(i):
                copy.start()

        @pl.when(kind == 3)
        def _():
            for copy in cross_copy(i):
                copy.wait_recv()
            far_grad[here] = (grad_tile[...] + pre_grad[here].astype(F32)).astype(BF)
            out_far[here] = (out_tile[...] + pre_out[here].astype(F32)).astype(BF)
            far_copy(i).start()

    loop(4, feed)
    for i in range(1, B):
        mlp_copy(2, i).wait_recv()
        mlp_copy(3, i).start()
        loop(4, lambda t: feed(t + 4 * i))

    far.finish()

    def weight_tile(t):
        rows = at(t, BLOCK)
        for s in range(K):
            ffns[s, rows, 0 : 2 * hz] = inner(mlp[:, rows], grad_act[s]).astype(BF)
            ffns[s, rows, 2 * hz :] = inner(cots[:, rows], hidden[s]).astype(BF)

    loop(D // BLOCK, weight_tile)
    save_grads = pltpu.make_async_copy(ffns, grads_out, gsem.at[0])
    save_grads.start()

    def join(t):
        rows = at(t, 64)
        out_own[rows] = out_own[rows] + mate_out[rows].astype(F32)
        grad_in[rows] = grad_in[rows] + mate_grad[rows].astype(F32) + pair_grad[rows].astype(F32)

    for i in range(B):
        for copy in grad_copy(i):
            copy.wait()
        for copy in cross_copy(i):
            copy.wait_send()
        far_copy(i).wait()
        for n in (1, 2, 3):
            mlp_copy(n, i).wait_send()
    loop(T // 64, join)
    for save in (save_slabs, save_query, save_bias, save_window, save_att, save_lse, save_grads):
        save.wait()
    behind(mark_own, mark_place, 0, "sent")
    behind(key_place(2), key_place, 3, "sent")
    for i in range(B):
        cot_copy(2, i).wait_send()
        cot_copy(3, i).wait_send()
    if with_slab:
        for gather in (near_rest, near, near_out):
            gather.finish()


def forward(shape, with_slab, tokens, cot, segment, w_gate, w_up, w_down, *slab):
    X, Y, Z = sides(shape)
    R = shape[0]
    T, D = tokens.shape
    E, hz = H * DH, w_gate.shape[1]
    W = 2 * E + 2 * DH + 128
    B = T // BLOCK
    span = WINDOW + BLOCK
    K = Z // 2
    S, V = jax.ShapeDtypeStruct, pltpu.VMEM
    outs = [
        S((T, D), F32), S((T, D), F32), S((T, D), F32), S((T, D), BF),
        S((D, W), BF), S((T, E), BF), S((3 * T, 2 * DH), BF), S((B, span, BLOCK), F32),
        S((E, T), BF), S((H * B, 8, BLOCK), F32), S((K, D, 3 * hz), BF),
    ]
    near, far = gather_count(X, Y, Z), gather_count(X, Y, K)
    scratch = [
        V((D, W), BF), V((K, D, 3 * hz), BF), V((T, E), BF), V((3 * T, 2 * DH), BF),
        V((DH, 3 * T), BF), V((8, 3 * T), F32), V((B, span, BLOCK), F32), V((E, T), BF),
        V((H * B, 8, BLOCK), F32), V((8, D), F32), V((4 * T, D), BF), V((4 * T, D), BF),
        V((BLOCK, D), F32), V((BLOCK, D), F32), V((K, 4 * T, hz), BF), V((K, 4 * T, 2 * hz), BF),
        *[V((T, D), BF)] * 10,
        *[DMA((near,))] * 6, *[DMA((far,))] * 2, *[DMA((3 * R * Z,))] * 2, *[DMA((6,))] * 2,
        *[DMA((1 + 2 * B,))] * 2, *[DMA((3 * B,))] * 2, *[DMA((5 * B,))] * 2, DMA((7,)), DMA((1,)),
    ]
    return pl.pallas_call(
        functools.partial(forward_kernel, shape, with_slab, (D, T, W, hz)),
        out_shape=outs,
        in_specs=[VM, ANY] + [VM] * 4 + [VM if with_slab else ANY] * len(slab),
        out_specs=[VM] * 4 + [ANY] * 7,
        scratch_shapes=scratch,
        compiler_params=pltpu.CompilerParams(
            collective_id=0, has_side_effects=True, vmem_limit_bytes=62 << 20
        ),
        name="forward",
    )(tokens, cot, segment, w_gate, w_up, w_down, *slab)


def backward_kernel(shape, with_slab, sizes, *refs):
    D, T, W, hz = sizes
    E, QK, WO = slab_lanes()
    B = T // BLOCK
    span = WINDOW + BLOCK
    refs = list(refs)

    def some(n):
        taken = refs[:n]
        del refs[:n]
        return taken

    (tokens_in, cot_in, grad_in_in, middle_in, out_own_in, out_far,
     slabs_in, query_in, window_in, bias_in, att_in, lse_in, grads) = some(13)
    output, grad_tokens, gate_out, up_out, down_out, out_slab, query_slab = some(7)
    keyval_slab, gain_slab = some(2) if with_slab else (some(1)[0], None)
    (tokens, cot, middle, grad_in, slabs, query, window, bias, att, lse, out_own, out_pair,
     gains, keys_t, branch, att_grad, query_grad_t, query_grad, kv_sum, kv_send, kv_recv, kv_grad, attn_in_t,
     gain_rows, termx, termy, own, ffn_sum) = some(28)
    weight_grads = some(3)
    fwork = some(4)
    if with_slab:
        rest_sum, *crossed = some(4)
        works = [some(4) for _ in range(3)]
    fsend, frecv, ksend, krecv, lsem, tsem = some(6)
    if with_slab:
        nsems = some(6)
        xsend, xrecv = some(2)
    p = Place(shape)
    pack = Pack(p, T)
    mate, spot = pack.mate, pack.spot
    K = p.Z // 2
    br = D // p.R

    def part(s, r):
        return grads.at[s, at(r, br)]

    def cut(ref, h):
        rows = ref.shape[0] // 2
        return ref.at[pl.ds(h * rows, rows)]

    ready = pack.greet()
    order = list(range(1, K)) + [0]
    terms = {}
    for s in order:
        copies = []
        for d in p.xs:
            copies.append((cut(part(s, p.row_at(dx=d)), 1), termx.at[s, d - 1]))
        for e in p.ys:
            copies.append((cut(part(s, p.row_at(dy=e)), 0), termy.at[s, e - 1]))
        copies.append((part(s, p.row), own.at[s]))
        n = s * (p.X + p.Y - 1)
        terms[s] = [
            pltpu.make_async_copy(a, b, tsem.at[n + i]) for i, (a, b) in enumerate(copies)
        ]
    pairs = [
        (middle_in, middle), (grad_in_in, grad_in), (cot_in, cot), (slabs_in, slabs), (att_in, att),
        (tokens_in, tokens), (window_in, window), (query_in, query), (bias_in, bias), (lse_in, lse),
        (out_own_in, out_own),
    ]
    loads = [pltpu.make_async_copy(a, b, lsem.at[n]) for n, (a, b) in enumerate(pairs)]
    for load in loads:
        load.start()
    for s in order:
        for copy in terms[s]:
            copy.start()
    ready()
    far = Scatter(
        part, cut, p, Sems(fsend, frecv),
        lambda s, d: termx.at[s, d - 1], lambda s, e: termy.at[s, e - 1], lambda s: own.at[s],
        *fwork, 2
    )
    ticks = []
    for j in range(K + 1):
        tick = []
        if j >= 1:
            tick.append(("third", order[j - 1]))
        if j < K:
            tick.append(("second", order[j]))
        if j + 2 < K:
            tick.append(("first", order[j + 2]))
        ticks.append(tick)

    def advance():
        if ticks:
            for step, s in ticks.pop(0):
                if step == "first":
                    far.first(s)
                elif step == "second":
                    for copy in terms[s]:
                        copy.wait()
                    far.second(s)
                else:
                    far.third(s, ffn_sum)

    for s in order[:2]:
        far.first(s)
    out_copy = remote(out_far, out_pair, ksend.at[2], krecv.at[2], pack.pair)
    out_copy.start()

    for load in loads[:4]:
        load.wait()
    gains[...] = slabs[:, QK:WO].astype(F32).T[0:8]
    gain_rows[...] = jnp.zeros_like(gain_rows)

    def fold_rows(value):
        return jnp.sum(value.reshape(value.shape[0] // 8, 8, D), axis=0)

    def second_norm(t, total):
        rows = at(t, 64)
        value, grad = middle[rows], grad_in[rows]
        scale = rms_scale(value)
        total = total + fold_rows(grad * (value * scale))
        n = grad * gains[1:2]
        out = cot[rows].astype(F32) + scale * n - value * (
            scale * scale * scale * jnp.mean(n * value, axis=-1, keepdims=True)
        )
        grad_in[rows] = out
        branch[rows] = out.astype(BF)
        return total

    total = lax.fori_loop(0, T // 64, second_norm, jnp.zeros((8, D), F32))
    gain_rows[1:2] = jnp.sum(total, axis=0, keepdims=True)

    def attended_grad(t):
        att_grad[at(t, BLOCK)] = against(slabs[at(t, BLOCK), WO:], branch[...]).astype(BF)

    loop(E // BLOCK, attended_grad)
    loads[4].wait()
    ar = D // (p.R * p.Z * 2)
    blocks = BLOCK // (2 * ar)

    def put(ref, t, lanes, value):
        if with_slab:
            ref[pl.ds(t * blocks, blocks), :, :, lanes] = value.astype(BF).reshape(
                blocks, 2, ar, value.shape[1]
            )
        else:
            ref[at(t, BLOCK), lanes] = value.astype(BF)

    def out_weight_grad(t):
        put(weight_grads[0], t, slice(0, E), product(att[at(t, BLOCK)], branch[...]))

    loop(E // BLOCK, out_weight_grad)

    class Near:
        def __init__(self, n):
            self.n, self.ref = n, weight_grads[n]
            self.copy = remote(
                self.ref.at[:, 1 - p.core], crossed[n], xsend.at[n], xrecv.at[n], mate
            )
            self.copy.start()

        def block(self, s, r):
            return self.ref.at[r * p.Z + p.z_at(s), p.core]

        def fold(self):
            self.copy.wait()
            ref, other = self.ref, crossed[self.n]

            def step(n):
                ref[n, p.core] = (ref[n, p.core].astype(F32) + other[n].astype(F32)).astype(BF)

            loop(p.R * p.Z, step)
            block = self.block
            self.scatter = Scatter(
                block, cut, p, Sems(*nsems[2 * self.n : 2 * self.n + 2]),
                lambda s, d: cut(block(s, p.row_at(dx=d)), 1),
                lambda s, e: cut(block(s, p.row_at(dy=e)), 0),
                lambda s: block(s, p.row), *works[self.n]
            )
            for s in self.order():
                self.scatter.first(s)

        def order(self):
            return list(range(1, p.Z)) + [0]

        def second(self):
            for s in self.order():
                self.scatter.second(s)

        def third(self):
            for s in self.order()[:-1]:
                self.scatter.third(s)

        def last(self, out):
            self.scatter.third(0, out)
            self.scatter.finish()

    if with_slab:
        near_out = Near(0)

    for load in loads[5:]:
        load.wait()

    def first_norm(t):
        cols = at(t, 128)
        value = tokens[cols].astype(F32)
        attn_in_t[:, cols] = (value * rms_scale(value) * gains[0:1]).astype(BF).T

    loop(T // 128, first_norm)
    keys_t[...] = window[:, 0:DH].T
    kv_sum[...] = jnp.zeros_like(kv_sum)
    if with_slab:
        near_out.fold()

    factor = LOG2E / math.sqrt(DH)
    scale = 1.0 / math.sqrt(DH)

    def head(i, h):
        lanes = at(h, DH)
        here = pl.ds(i * BLOCK, BLOCK)
        seen = pl.ds(i * BLOCK, span)
        part_query = query[here, lanes]
        part_grad = att_grad[lanes, here]
        scores = against(window[seen, 0:DH], part_query) * factor + bias[i]
        probs = jnp.exp2(scores - lse[h * B + i][0:1])
        grad_probs = product(window[seen, DH:], part_grad)
        centre = jnp.sum(
            att[lanes, here].astype(F32) * part_grad.astype(F32), axis=0, keepdims=True
        )
        grad_scores = (probs * (grad_probs - centre)).astype(BF)
        kv_sum[seen, DH:] += against(probs.astype(BF), part_grad)
        kv_sum[seen, 0:DH] += product(grad_scores, part_query)
        query_grad_t[lanes, here] = (product(keys_t[:, seen], grad_scores) * scale).astype(BF)

    for i in range(B):
        loop(H, lambda h: head(i, h))

    kv_send[:, 0:DH] = (kv_sum[pl.ds(0, 2 * T), 0:DH] * scale).astype(BF)
    kv_send[:, DH:] = kv_sum[pl.ds(0, 2 * T), DH:].astype(BF)
    returns = []
    for d in (1, 2):
        to = (p.row, lax.rem(p.col - d + 2 * p.Z, 2 * p.Z))
        copy = remote(
            kv_send.at[pl.ds((2 - d) * T, T)], kv_recv.at[d - 1], ksend.at[d - 1], krecv.at[d - 1], to
        )
        pl.when(spot - d >= 0)(copy.start)
        returns.append((d, copy))

    def turn(t):
        query_grad[at(t, BLOCK)] = query_grad_t[:, at(t, BLOCK)].T

    loop(B, turn)

    def query_weight_grad(t):
        put(weight_grads[1], t, slice(0, E), product(attn_in_t[at(t, BLOCK)], query_grad[...]))

    loop(D // BLOCK, query_weight_grad)
    if with_slab:
        near_query = Near(1)
    advance()

    def input_grad_query(t):
        rows = at(t, 128)
        grad_tokens[rows] = against(query_grad[rows], slabs[:, 0:E])

    loop(T // 128, input_grad_query)
    kv_grad[:, 0:DH] = kv_sum[pl.ds(2 * T, T), 0:DH] * scale
    kv_grad[:, DH:] = kv_sum[pl.ds(2 * T, T), DH:]
    if with_slab:
        near_query.fold()
        near_out.second()
    for d, copy in returns:
        @pl.when(spot + d < pack.size)
        def _():
            copy.wait_recv()
            kv_grad[...] += kv_recv[d - 1].astype(F32)

    window[pl.ds(0, T)] = kv_grad[...].astype(BF)

    def keyval_weight_grad(t):
        put(weight_grads[2], t, slice(0, 2 * DH), product(attn_in_t[at(t, BLOCK)], window[pl.ds(0, T)]))

    loop(D // BLOCK, keyval_weight_grad)

    def input_grad(t, total):
        rows = at(t, 128)
        grad = grad_tokens[rows] + against(window[rows], slabs[:, E:QK])
        value = tokens[rows].astype(F32)
        scale_first = rms_scale(value)
        total = total + fold_rows(grad * (value * scale_first))
        m = grad * gains[0:1]
        grad_tokens[rows] = grad_in[rows] + scale_first * m - value * (
            scale_first * scale_first * scale_first * jnp.mean(m * value, axis=-1, keepdims=True)
        )
        return total

    total = lax.fori_loop(0, T // 128, input_grad, jnp.zeros((8, D), F32))
    gain_rows[0:1] = jnp.sum(total, axis=0, keepdims=True)

    def gain_grad(t):
        put(weight_grads[2], t, slice(2 * DH, 2 * DH + 128), gain_rows[:, at(t, BLOCK)].T)

    loop(D // BLOCK, gain_grad)
    if with_slab:
        near_rest = Near(2)
        near_query.second()
        near_rest.fold()
        advance()
        near_out.third()
        near_query.third()
        near_rest.second()
        near_rest.third()
        near_out.last(out_slab)
    else:
        for ref, out in zip(weight_grads, (out_slab, query_slab, keyval_slab)):
            out[...] = ref[...]
    out_copy.wait_recv()

    def join(t):
        rows = at(t, 64)
        output[rows] = (out_own[rows] + out_pair[rows].astype(F32)).astype(BF)

    loop(T // 64, join)
    while ticks:
        advance()
    gate_out[...] = ffn_sum[:, 0:hz]
    up_out[...] = ffn_sum[:, hz : 2 * hz]
    down_out[...] = ffn_sum[:, 2 * hz :].T
    if with_slab:
        near_query.last(query_slab)
        near_rest.last(rest_sum)
        keyval_slab[...] = rest_sum[:, 0 : 2 * DH]
        gain_slab[...] = rest_sum[:, 2 * DH :]
    out_copy.wait_send()
    for d, copy in returns:
        pl.when(spot - d >= 0)(copy.wait_send)
    far.finish()


def backward(
    shape, with_slab, tokens, cot, grad_in, middle, out_own, out_far, slabs, query, window, bias, att, lse, grads
):
    X, Y, Z = sides(shape)
    R = shape[0]
    T, D = tokens.shape
    E, hz = H * DH, grads.shape[2] // 3
    W = slabs.shape[1]
    B = T // BLOCK
    span = WINDOW + BLOCK
    K = Z // 2
    near, far = scatter_count(X, Y, Z), scatter_count(X, Y, K)
    S, V = jax.ShapeDtypeStruct, pltpu.VMEM
    block = (D // R, 3 * hz)
    half = (block[0] // 2, block[1])
    widths = (E, E, 2 * DH + 128)
    ar = D // (R * Z * 2)
    if with_slab:
        slab_outs = [S((ar, w), F32) for w in (E, E, 2 * DH, 128)]
        slab_work = [V((R * Z, 2, ar, w), BF) for w in widths]
    else:
        slab_outs = [S((D, w), BF) for w in widths]
        slab_work = [V((D, w), BF) for w in widths]
    outs = [S((T, D), BF), S((T, D), F32)]
    outs += [S((D // R, hz), F32), S((D // R, hz), F32), S((hz, D // R), F32)] + slab_outs
    scratch = [
        V((T, D), BF), V((T, D), BF), V((T, D), F32), V((T, D), F32), V((D, W), BF), V((T, E), BF),
        V((3 * T, 2 * DH), BF), V((B, span, BLOCK), F32), V((E, T), BF), V((H * B, 8, BLOCK), F32),
        V((T, D), F32), V((T, D), BF),
        V((8, D), F32), V((DH, 3 * T), BF), V((T, D), BF), V((E, T), BF), V((E, T), BF), V((T, E), BF),
        V((3 * T, 2 * DH), F32), V((2 * T, 2 * DH), BF), V((2, T, 2 * DH), BF), V((T, 2 * DH), F32),
        V((D, T), BF), V((128, D), F32),
        V((K, X - 1) + half, BF), V((K, Y - 1) + half, BF), V((K,) + block, BF), V(block, F32),
        *slab_work,
        *scatter_scratch(X, Y, K, block),
    ]
    if with_slab:
        scratch += [V((ar, widths[2]), F32)] + [V((R * Z, ar, w), BF) for w in widths]
        for w in widths:
            scratch += scatter_scratch(X, Y, Z, (ar, w))
    scratch += [
        DMA((far,)), DMA((far,)), DMA((3,)), DMA((3,)), DMA((11,)), DMA((K * (X + Y - 1),)),
    ]
    if with_slab:
        scratch += [DMA((near,))] * 6 + [DMA((3,))] * 2
    return pl.pallas_call(
        functools.partial(backward_kernel, shape, with_slab, (D, T, W, hz)),
        out_shape=outs,
        in_specs=[ANY] * 13,
        out_specs=[VM] * len(outs),
        scratch_shapes=scratch,
        compiler_params=pltpu.CompilerParams(
            collective_id=1, has_side_effects=True, vmem_limit_bytes=62 << 20
        ),
        name="backward",
    )(tokens, cot, grad_in, middle, out_own, out_far, slabs, query, window, bias, att, lse, grads)


def shards(
    shape,
    tokens, gain_attn, w_query, w_keyval, w_out, gain_mlp, w_gate, w_up, w_down, segment, cotangent
):
    with_slab = w_query.shape[0] % 32 == 0
    gain_columns = jnp.pad(jnp.stack([gain_attn, gain_mlp], axis=1), ((0, 0), (0, 126)))
    slab = [w_query, w_keyval, gain_columns, w_out]
    if not with_slab:
        slab = [lax.all_gather(jnp.concatenate(slab, axis=1), ("row", "col"), axis=0, tiled=True)]
    kept = forward(shape, with_slab, tokens, cotangent, segment[None], w_gate, w_up, w_down, *slab)
    results = backward(shape, with_slab, tokens, cotangent, *kept)
    output, grad_tokens, gate_grad, up_grad, down_grad = results[:5]
    if with_slab:
        out_grad, query_grad, keyval_grad, gain_grad = results[5:]
    else:
        out_grad, query_grad, rest_grad = [
            lax.psum_scatter(g.astype(F32), ("row", "col"), scatter_dimension=0, tiled=True)
            for g in results[5:]
        ]
        keyval_grad, gain_grad = rest_grad[:, : 2 * DH], rest_grad[:, 2 * DH :]
    return (
        output,
        grad_tokens,
        gain_grad[:, 0],
        query_grad,
        keyval_grad,
        out_grad,
        gain_grad[:, 1],
        gate_grad,
        up_grad,
        down_grad,
    )


def solution(mesh):
    shape = (mesh.shape["row"], mesh.shape["col"])
    return jax.shard_map(
        functools.partial(shards, shape),
        mesh=mesh,
        in_specs=(
            P(("row", "col"), None),
            P(("row", "col")),
            P(("row", "col"), None),
            P(("row", "col"), None),
            P(("row", "col"), None),
            P(("row", "col")),
            P("row", "col"),
            P("row", "col"),
            P("col", "row"),
            P(("row", "col")),
            P(("row", "col"), None),
        ),
        out_specs=(
            P(("row", "col"), None),
            P(("row", "col"), None),
            P(("row", "col")),
            P(("row", "col"), None),
            P(("row", "col"), None),
            P(("row", "col"), None),
            P(("row", "col")),
            P("row", "col"),
            P("row", "col"),
            P("col", "row"),
        ),
        check_vma=False,
    )
```

```python
import functools
import math

import jax
import jax.numpy as jnp
from jax import lax
from jax.experimental import pallas as pl
from jax.experimental.pallas import tpu as pltpu
from jax.sharding import PartitionSpec as P

H = 8
DH = 128
WINDOW = 1024
PACK = 2048

EPS = 1e-06
NEGATIVE = -1e30
MESH = pl.DeviceIdType.MESH
BF = jnp.bfloat16
F32 = jnp.float32


def product(left, right):
    return jnp.dot(left, right, preferred_element_type=jnp.float32)


def inner(left, right):
    return lax.dot_general(
        left, right, (((0,), (0,)), ((), ())), preferred_element_type=jnp.float32
    )


def against(left, right):
    return lax.dot_general(
        left, right, (((1,), (1,)), ((), ())), preferred_element_type=jnp.float32
    )


class Place:
    def __init__(self, shape):
        rows, cols = shape
        self.X = math.isqrt(rows)
        while rows % self.X:
            self.X -= 1
        self.Y = rows // self.X
        self.Z = cols // 2
        self.R = rows
        self.row, self.col = lax.axis_index("row"), lax.axis_index("col")
        self.y, self.x = self.row // self.X, self.row % self.X
        self.z, self.core = self.col // 2, self.col % 2
        self.xs, self.ys, self.zs = range(1, self.X), range(1, self.Y), range(1, self.Z)

    def row_at(self, dy=0, dx=0):
        return lax.rem(self.y + dy + self.Y, self.Y) * self.X + lax.rem(
            self.x + dx + self.X, self.X
        )

    def z_at(self, dz):
        return lax.rem(self.z + dz + self.Z, self.Z)

    def device(self, dy=0, dx=0, dz=0, other=False):
        core = 1 - self.core if other else self.core
        return (self.row_at(dy, dx), self.z_at(dz) * 2 + core)


def remote(src, dst, send, recv, device):
    return pltpu.make_async_remote_copy(
        src_ref=src, dst_ref=dst, send_sem=send, recv_sem=recv, device_id=device,
        device_id_type=MESH,
    )


class Sems:
    def __init__(self, send, recv):
        self.send, self.recv, self.count = send, recv, 0

    def take(self):
        self.count += 1
        return self.send.at[self.count - 1], self.recv.at[self.count - 1]


def gather_count(X, Y, K):
    return (K - 1) + K * ((X - 1) + (Y - 1) + 2 * (X - 1) * (Y - 1))


class Gather:
    def __init__(self, at, dest, here, sems, own, stride=1):
        self.at, self.dest, self.p, self.own = at, dest, here, own
        self.stride, self.K = stride, here.Z // stride
        self.sent = []
        p = here
        self.zsem = {k: sems.take() for k in range(1, self.K)}
        self.xsem = {(s, d): sems.take() for s in range(self.K) for d in p.xs}
        self.ysem = {(s, d): sems.take() for s in range(self.K) for d in p.ys}
        self.dsem = {
            (s, h, dx, dy): sems.take()
            for s in range(self.K) for h in (0, 1) for dx in p.xs for dy in p.ys
        }

    def push(self, src, dst, sem, device):
        copy = remote(src, dst, sem[0], sem[1], device)
        copy.start()
        self.sent.append(copy)

    def arrive(self, place, sem):
        remote(place, place, sem[0], sem[1], self.p.device(other=True)).wait_recv()

    def spread_z(self):
        p = self.p
        for k in range(1, self.K):
            self.push(self.own, self.dest(k), self.zsem[k], p.device(dz=-self.stride * k))

    def spread_xy(self, s):
        if s >= self.K:
            return
        p = self.p
        place = self.at(s, p.row, None)
        src = self.own
        if s:
            self.arrive(place, self.zsem[s])
            src = place
        for d in p.xs:
            self.push(src, place, self.xsem[s, d], p.device(dx=d))
        for d in p.ys:
            self.push(src, place, self.ysem[s, d], p.device(dy=d))

    def spread_diagonal(self, s):
        if s >= self.K:
            return
        p = self.p
        for d in p.xs:
            r = p.row_at(dx=-d)
            self.arrive(self.at(s, r, None), self.xsem[s, d])
            half = self.at(s, r, 0)
            for e in p.ys:
                self.push(half, half, self.dsem[s, 0, d, e], p.device(dy=e))
        for e in p.ys:
            r = p.row_at(dy=-e)
            self.arrive(self.at(s, r, None), self.ysem[s, e])
            half = self.at(s, r, 1)
            for d in p.xs:
                self.push(half, half, self.dsem[s, 1, d, e], p.device(dx=d))

    def close(self, s):
        p = self.p
        for d in p.xs:
            for e in p.ys:
                r = p.row_at(dy=-e, dx=-d)
                for h in (0, 1):
                    self.arrive(self.at(s, r, h), self.dsem[s, h, d, e])

    def finish(self):
        for copy in self.sent:
            copy.wait_send()


def scatter_count(X, Y, K):
    return (K - 1) + K * (2 * (X - 1) * (Y - 1) + 2 * (X - 1) + 2 * (Y - 1))


class Scatter:
    def __init__(
        self, part, cut, here, sems, termx, termy, own, diag, fromx, fromy, fromz, stride=1
    ):
        self.part, self.cut, self.p = part, cut, here
        self.termx, self.termy, self.own = termx, termy, own
        self.diag, self.fromx, self.fromy, self.fromz = diag, fromx, fromy, fromz
        self.stride, self.K = stride, here.Z // stride
        self.sent = []
        p = here
        self.zsem = {k: sems.take() for k in range(1, self.K)}
        self.xsem = {(s, h, d): sems.take() for s in range(self.K) for h in (0, 1) for d in p.xs}
        self.ysem = {(s, h, d): sems.take() for s in range(self.K) for h in (0, 1) for d in p.ys}
        self.dsem = {
            (s, h, dx, dy): sems.take()
            for s in range(self.K) for h in (0, 1) for dx in p.xs for dy in p.ys
        }

    def push(self, src, dst, sem, device):
        copy = remote(src, dst, sem[0], sem[1], device)
        copy.start()
        self.sent.append(copy)

    def arrive(self, place, sem):
        remote(place, place, sem[0], sem[1], self.p.device(other=True)).wait_recv()

    def spot(self, d, e):
        return (d - 1) * (self.p.Y - 1) + e - 1

    def first(self, s):
        p, cut = self.p, self.cut
        for d in p.xs:
            for e in p.ys:
                far = self.part(s, p.row_at(dy=e, dx=d))
                n = self.spot(d, e)
                self.push(cut(far, 0), self.diag.at[s, 0, n], self.dsem[s, 0, d, e], p.device(dx=d))
                self.push(cut(far, 1), self.diag.at[s, 1, n], self.dsem[s, 1, d, e], p.device(dy=e))
        for d in p.xs:
            near = self.part(s, p.row_at(dx=d))
            self.push(cut(near, 0), cut(self.fromx.at[s, d - 1], 0), self.xsem[s, 0, d], p.device(dx=d))
        for e in p.ys:
            near = self.part(s, p.row_at(dy=e))
            self.push(cut(near, 1), cut(self.fromy.at[s, e - 1], 1), self.ysem[s, 1, e], p.device(dy=e))

    def second(self, s):
        p, cut = self.p, self.cut
        for e in p.ys:
            term = self.termy(s, e)
            total = term[...].astype(F32)
            for d in p.xs:
                place = self.diag.at[s, 0, self.spot(d, e)]
                self.arrive(place, self.dsem[s, 0, d, e])
                total = total + place[...].astype(F32)
            term[...] = total.astype(BF)
            self.push(term, cut(self.fromy.at[s, e - 1], 0), self.ysem[s, 0, e], p.device(dy=e))
        for d in p.xs:
            term = self.termx(s, d)
            total = term[...].astype(F32)
            for e in p.ys:
                place = self.diag.at[s, 1, self.spot(d, e)]
                self.arrive(place, self.dsem[s, 1, d, e])
                total = total + place[...].astype(F32)
            term[...] = total.astype(BF)
            self.push(term, cut(self.fromx.at[s, d - 1], 1), self.xsem[s, 1, d], p.device(dx=d))

    def third(self, s, out=None):
        p, cut = self.p, self.cut
        own = self.own(s)
        total = own[...].astype(F32)
        for d in p.xs:
            for h in (0, 1):
                self.arrive(cut(self.fromx.at[s, d - 1], h), self.xsem[s, h, d])
            total = total + self.fromx[s, d - 1].astype(F32)
        for e in p.ys:
            for h in (0, 1):
                self.arrive(cut(self.fromy.at[s, e - 1], h), self.ysem[s, h, e])
            total = total + self.fromy[s, e - 1].astype(F32)
        if s:
            own[...] = total.astype(BF)
            self.push(own, self.fromz.at[s - 1], self.zsem[s], p.device(dz=self.stride * s))
            return
        for k in range(1, self.K):
            self.arrive(self.fromz.at[k - 1], self.zsem[k])
            total = total + self.fromz[k - 1].astype(F32)
        out[...] = total

    def finish(self):
        for copy in self.sent:
            copy.wait_send()


def scatter_scratch(X, Y, K, block):
    half = (block[0] // 2, block[1])
    return [
        pltpu.VMEM((K, 2, (X - 1) * (Y - 1)) + half, BF),
        pltpu.VMEM((K, X - 1) + block, BF),
        pltpu.VMEM((K, Y - 1) + block, BF),
        pltpu.VMEM((max(K - 1, 1),) + block, BF),
    ]


def sides(shape):
    x = math.isqrt(shape[0])
    while shape[0] % x:
        x -= 1
    return x, shape[0] // x, shape[1] // 2


VM = pl.BlockSpec(memory_space=pltpu.VMEM)
ANY = pl.BlockSpec(memory_space=pl.ANY)
DMA = pltpu.SemaphoreType.DMA
LOG2E = math.log2(math.e)
BLOCK = 256


def loop(count, body):
    def step(t, carry):
        body(t)
        return carry

    lax.fori_loop(0, count, step, 0)


def at(t, size):
    return pl.ds(pl.multiple_of(t * size, size), size)


def rms_scale(value):
    return lax.rsqrt(jnp.mean(value * value, axis=-1, keepdims=True) + EPS)


def gelu_parts(gate):
    square = gate * gate
    t = jnp.tanh(gate * (0.7978845608 + (0.7978845608 * 0.044715) * square))
    half = 0.5 + 0.5 * t
    slope = half + (0.5 * gate) * (1.0 - t * t) * (
        0.7978845608 + (3 * 0.7978845608 * 0.044715) * square
    )
    return gate * half, slope


class Pack:
    def __init__(self, here, T):
        p = here
        self.p, self.size = p, PACK // T
        self.spot = lax.rem(p.col, self.size)
        pair = (p.z // 2) * 2 + 1 - lax.rem(p.z, 2)
        self.mate = p.device(other=True)
        self.pair = (p.row, pair * 2 + p.core)
        self.across = (p.row, pair * 2 + 1 - p.core)

    def greet(self):
        p = self.p
        barrier = pltpu.get_barrier_semaphore()
        mates = [p.device(dx=d) for d in p.xs] + [p.device(dy=d) for d in p.ys]
        mates += [p.device(dz=d) for d in p.zs] + [self.mate, self.across]
        for mate in mates:
            pl.semaphore_signal(barrier, inc=1, device_id=mate, device_id_type=MESH)
        return lambda: pl.semaphore_wait(barrier, len(mates))


def slab_lanes():
    E, QK = H * DH, H * DH + 2 * DH
    return E, QK, QK + 128


def forward_kernel(shape, with_slab, sizes, *refs):
    D, T, W, hz = sizes
    (tokens, cot, segment, w_gate, w_up, w_down, *slab_in) = refs[: 10 if with_slab else 7]
    (grad_in, middle, out_own, out_far, gains, slabs_out, query_out, window_out, bias_out, att_out, lse_out, grads_out,
     slabs, ffns, query, window, values_t, marks_all, bias, att, lse, mlp, cots,
     grad_tile, out_tile, hidden, grad_act, side_grad, side_out, cross_grad, cross_out, far_grad,
     mate_grad, mate_out, pre_grad, pre_out, pair_grad,
     vsend, vrecv, asend, arecv, osend, orecv, fsend, frecv, csend, crecv, ksend, krecv, tsend, trecv,
     msend, mrecv, gsend, grecv, lsem, gsem) = refs[10 if with_slab else 7 :]
    p = Place(shape)
    pack = Pack(p, T)
    mate, pair, spot = pack.mate, pack.pair, pack.spot
    E, QK, WO = slab_lanes()
    B = T // BLOCK
    span = WINDOW + BLOCK
    K = p.Z // 2

    def local(src, dst, n):
        copy = pltpu.make_async_copy(src, dst, lsem.at[n])
        copy.start()
        return copy

    ready = pack.greet()
    load_cot = local(cot, cots.at[pl.ds(0, T)], 0)
    if not with_slab:
        load_slab = local(slab_in[0], slabs, 1)
    br = w_gate.shape[0]
    own_rows = at(p.row, br)
    ffns[0, own_rows, 0:hz] = w_gate[...]
    ffns[0, own_rows, hz : 2 * hz] = w_up[...]
    ffns[0, own_rows, 2 * hz :] = w_down[...].T

    def ffn_at(s, r, half):
        if half is None:
            return ffns.at[s, at(r, br)]
        return ffns.at[s, pl.ds(pl.multiple_of(r * br + half * (br // 2), br // 2), br // 2)]

    far = Gather(
        ffn_at, lambda k: ffn_at(k, p.row, None), p, Sems(fsend, frecv), ffn_at(0, p.row, None), 2
    )

    if with_slab:
        ar = slab_in[0].shape[0]
        slab_rows = pl.ds(pl.multiple_of(((p.row * p.Z + p.z) * 2 + p.core) * ar, ar), ar)
        widths = ((0, E), (E, QK), (QK, WO), (WO, W))
        for piece, (start, stop) in zip(slab_in, widths):
            slabs[slab_rows, start:stop] = piece[...]

        def slab_place(lanes, core):
            def place(s, r, half):
                start = ((r * p.Z + p.z_at(s)) * 2 + core) * ar
                if half is None:
                    return slabs.at[pl.ds(pl.multiple_of(start, ar), ar), lanes]
                start = pl.multiple_of(start + half * (ar // 2), ar // 2)
                return slabs.at[pl.ds(start, ar // 2), lanes]

            return place

        def slab_gather(lanes, sems):
            place = slab_place(lanes, p.core)
            own = place(0, p.row, None)
            return Gather(place, lambda k: own, p, sems, own)

        rest_lanes, act_lanes, out_lanes = slice(E, WO), slice(0, E), slice(WO, W)
        near_rest = slab_gather(rest_lanes, Sems(vsend, vrecv))
        near = slab_gather(act_lanes, Sems(asend, arecv))
        near_out = slab_gather(out_lanes, Sems(osend, orecv))
        hands = Sems(csend, crecv)

        def hand(gather, lanes):
            mine, theirs = slab_place(lanes, p.core), slab_place(lanes, 1 - p.core)
            passed = []
            for s in range(p.Z):
                gather.close(s)
                for dy in range(p.Y):
                    for dx in range(p.X):
                        r = p.row_at(dy, dx)
                        send, recv = hands.take()
                        place, other = mine(s, r, None), theirs(s, r, None)
                        copy = remote(place, place, send, recv, mate)
                        copy.start()
                        passed.append((copy, remote(other, other, send, recv, mate)))
            return passed

        def settle(passed):
            for copy, arrival in passed:
                copy.wait_send()
                arrival.wait_recv()

    ready()
    if with_slab:
        near_rest.spread_z()
        near_rest.spread_xy(0)
        near.spread_z()
        near.spread_xy(0)
        near_out.spread_z()

    marks_all[:, pl.ds(2 * T, T)] = jnp.broadcast_to(segment[...].astype(F32), (8, T))

    @pl.when(spot == 0)
    def _():
        window[pl.ds(0, 2 * T), :] = jnp.zeros((2 * T, 2 * DH), BF)
        marks_all[:, pl.ds(0, 2 * T)] = jnp.full((8, 2 * T), -1.0, F32)

    @pl.when(spot == 1)
    def _():
        window[pl.ds(0, T), :] = jnp.zeros((T, 2 * DH), BF)
        marks_all[:, pl.ds(0, T)] = jnp.full((8, T), -1.0, F32)

    def behind(src, place, n, op):
        for d in (1, 2):
            to = (p.row, lax.rem(p.col + d, 2 * p.Z))
            copy = remote(src, place(2 - d), ksend.at[n + d], krecv.at[n + d], to)
            if op == "start":
                pl.when(spot + d < pack.size)(copy.start)
            elif op == "arrive":
                pl.when(spot - d >= 0)(copy.wait_recv)
            else:
                pl.when(spot + d < pack.size)(copy.wait_send)

    mark_place = lambda k: marks_all.at[:, pl.ds(k * T, T)]
    mark_own = mark_place(2)
    behind(mark_own, mark_place, 0, "start")

    def whole(ref, n):
        return ref.at[pl.ds(n * T, T)]

    load_cot.wait()
    cot_mate = remote(whole(cots, 0), whole(cots, 1), tsend.at[0], trecv.at[0], mate)
    cot_mate.start()

    def tile_of(ref, n, i):
        return ref.at[pl.ds(pl.multiple_of(n * T + i * BLOCK, BLOCK), BLOCK)]

    def cot_copy(n, i):
        to, src, sem = (pair, 0, 1 + i) if n == 2 else (mate, 2, 1 + B + i)
        return remote(tile_of(cots, src, i), tile_of(cots, n, i), tsend.at[sem], trecv.at[sem], to)

    if with_slab:
        for s in range(p.Z):
            near_rest.spread_xy(s + 1)
            near_rest.spread_diagonal(s)
        for s in range(1, p.Z):
            near.spread_xy(s)
        passed = hand(near_rest, rest_lanes)
        for s in range(p.Z):
            near.spread_diagonal(s)
        settle(passed)
    else:
        load_slab.wait()
    gains[...] = slabs[:, QK:WO].astype(F32).T[0:8]

    def first_norm(t):
        rows = at(t, 64)
        value = tokens[rows].astype(F32)
        mlp[rows] = (value * rms_scale(value) * gains[0:1]).astype(BF)

    loop(T // 64, first_norm)
    window[pl.ds(2 * T, T)] = product(mlp[pl.ds(0, T)], slabs[:, E:QK]).astype(BF)
    key_place = lambda k: window.at[pl.ds(k * T, T)]
    behind(key_place(2), key_place, 3, "start")

    far.spread_z()
    cot_copy(2, 0).start()
    if with_slab:
        for s in range(p.Z):
            near_out.spread_xy(s)
        settle(hand(near, act_lanes))

    def project(t):
        query[at(t, BLOCK)] = product(mlp[at(t, BLOCK)], slabs[:, 0:E]).astype(BF)

    loop(B, project)
    save_query = local(query, query_out, 2)
    if with_slab:
        for s in range(p.Z):
            near_out.spread_diagonal(s)
    far.spread_xy(0)
    behind(mark_own, mark_place, 0, "arrive")
    column = jnp.broadcast_to(marks_all[0:1], (128, 3 * T)).T
    for i in range(B):
        keys_at = jnp.concatenate([column[i * BLOCK : i * BLOCK + span]] * (BLOCK // 128), axis=1)
        own = marks_all[0:1, 2 * T + i * BLOCK : 2 * T + (i + 1) * BLOCK]
        gap = (
            WINDOW
            + lax.broadcasted_iota(jnp.int32, (span, BLOCK), 1)
            - lax.broadcasted_iota(jnp.int32, (span, BLOCK), 0)
        )
        allowed = (keys_at == own) & (gap >= 0) & (gap < WINDOW)
        bias[i] = jnp.where(allowed, 0.0, NEGATIVE)
    save_bias = local(bias, bias_out, 3)
    if with_slab:
        passed = hand(near_out, out_lanes)
    behind(key_place(2), key_place, 3, "arrive")
    for i in range(1, B):
        cot_copy(2, i).start()
    save_window = local(window, window_out, 4)
    values_t[...] = window[:, DH:].T
    factor = LOG2E / math.sqrt(DH)

    def head(i, h):
        lanes = at(h, DH)
        keys = window[pl.ds(i * BLOCK, span), 0:DH]
        scores = against(keys, query[pl.ds(i * BLOCK, BLOCK), lanes]) * factor + bias[i]
        top = jnp.max(scores, axis=0, keepdims=True)
        expo = jnp.exp2(scores - top)
        total = jnp.sum(expo, axis=0, keepdims=True)
        mixed = product(values_t[:, pl.ds(i * BLOCK, span)], expo.astype(BF))
        att[lanes, pl.ds(i * BLOCK, BLOCK)] = (mixed / total).astype(BF)
        lse[h * B + i] = jnp.broadcast_to(top + jnp.log2(total), (8, BLOCK))

    def mlp_copy(n, i):
        to = pair if n == 2 else mate
        src = 2 if n == 3 else 0
        sem = (n - 1) * B + i
        return remote(tile_of(mlp, src, i), tile_of(mlp, n, i), msend.at[sem], mrecv.at[sem], to)

    for i in range(B):
        if i == 0:
            loop(H // 2, lambda h: head(i, h))
            far.spread_xy(1)
            far.spread_diagonal(0)
            loop(H // 2, lambda h: head(i, h + H // 2))
            if with_slab:
                settle(passed)
            save_slabs = local(slabs, slabs_out, 1)
        else:
            loop(H, lambda h: head(i, h))
        cols = pl.ds(i * BLOCK, BLOCK)
        middle[cols] = product(att[:, cols].T, slabs[:, WO:]) + tokens[cols].astype(F32)

        def second_norm(t):
            rows = pl.ds(pl.multiple_of(i * BLOCK + t * 64, 64), 64)
            value = middle[rows]
            mlp[rows] = (value * rms_scale(value) * gains[1:2]).astype(BF)

        loop(BLOCK // 64, second_norm)
        mlp_copy(1, i).start()
        mlp_copy(2, i).start()
        cot_copy(2, i).wait_recv()
        cot_copy(3, i).start()
    save_att = local(att, att_out, 5)
    save_lse = local(lse, lse_out, 6)
    for s in range(2, K):
        far.spread_xy(s)
    for s in range(1, K):
        far.spread_diagonal(s)
    mlp_copy(2, 0).wait_recv()
    mlp_copy(3, 0).start()
    for s in range(K):
        far.close(s)
    cot_mate.wait()
    for i in range(B):
        cot_copy(3, i).wait_recv()

    def grad_copy(i):
        return [
            remote(tile_of(side_grad, 0, i), tile_of(mate_grad, 0, i), gsend.at[i], grecv.at[i], mate),
            remote(tile_of(side_out, 0, i), tile_of(mate_out, 0, i), gsend.at[B + i], grecv.at[B + i], mate),
        ]

    def cross_copy(i):
        n = 2 * B
        return [
            remote(tile_of(cross_grad, 0, i), tile_of(pre_grad, 0, i), gsend.at[n + i], grecv.at[n + i], mate),
            remote(tile_of(cross_out, 0, i), tile_of(pre_out, 0, i), gsend.at[n + B + i], grecv.at[n + B + i], mate),
        ]

    def far_copy(i):
        n = 4 * B + i
        return remote(tile_of(far_grad, 0, i), tile_of(pair_grad, 0, i), gsend.at[n], grecv.at[n], pair)

    def feed(t):
        i, kind = t // 4, lax.rem(t, 4)
        n = jnp.where(kind == 2, 3, jnp.where(kind == 3, 2, kind))

        @pl.when(kind == 1)
        def _():
            mlp_copy(1, i).wait_recv()

        @pl.when(kind == 2)
        def _():
            mlp_copy(3, i).wait_recv()

        rows = pl.ds(pl.multiple_of(n * T + i * BLOCK, BLOCK), BLOCK)
        for s in range(K):
            gate_up = product(mlp[rows], ffns[s, :, 0 : 2 * hz])
            grad_hidden = product(cots[rows], ffns[s, :, 2 * hz :])
            up = gate_up[:, hz:]
            act, slope = gelu_parts(gate_up[:, :hz])
            hidden[s, rows] = (act * up).astype(BF)
            grad_act[s, rows, 0:hz] = (grad_hidden * up * slope).astype(BF)
            grad_act[s, rows, hz : 2 * hz] = (grad_hidden * act).astype(BF)
            outs = against(hidden[s, rows], ffns[s, :, 2 * hz :])
            grads = against(grad_act[s, rows], ffns[s, :, 0 : 2 * hz])
            if s == 0:
                out_tile[...] = outs
                grad_tile[...] = grads
            else:
                out_tile[...] += outs
                grad_tile[...] += grads
        here = pl.ds(pl.multiple_of(i * BLOCK, BLOCK), BLOCK)

        @pl.when(kind == 0)
        def _():
            grad_in[here] = grad_tile[...]
            out_own[here] = middle[here] + out_tile[...]

        @pl.when(kind == 1)
        def _():
            side_grad[here] = grad_tile[...].astype(BF)
            side_out[here] = out_tile[...].astype(BF)
            for copy in grad_copy(i):
                copy.start()

        @pl.when(kind == 2)
        def _():
            cross_grad[here] = grad_tile[...].astype(BF)
            cross_out[here] = out_tile[...].astype(BF)
            for copy in cross_copy(i):
                copy.start()

        @pl.when(kind == 3)
        def _():
            for copy in cross_copy(i):
                copy.wait_recv()
            far_grad[here] = (grad_tile[...] + pre_grad[here].astype(F32)).astype(BF)
            out_far[here] = (out_tile[...] + pre_out[here].astype(F32)).astype(BF)
            far_copy(i).start()

    loop(4, feed)
    for i in range(1, B):
        mlp_copy(2, i).wait_recv()
        mlp_copy(3, i).start()
        loop(4, lambda t: feed(t + 4 * i))

    far.finish()

    def weight_tile(t):
        rows = at(t, BLOCK)
        for s in range(K):
            ffns[s, rows, 0 : 2 * hz] = inner(mlp[:, rows], grad_act[s]).astype(BF)
            ffns[s, rows, 2 * hz :] = inner(cots[:, rows], hidden[s]).astype(BF)
        save_grads(t).start()

    def save_grads(t):
        rows = at(t, BLOCK)
        return pltpu.make_async_copy(ffns.at[:, rows], grads_out.at[:, rows], gsem.at[t])

    loop(D // BLOCK, weight_tile)

    def join(t):
        rows = at(t, 64)
        out_own[rows] = out_own[rows] + mate_out[rows].astype(F32)
        grad_in[rows] = grad_in[rows] + mate_grad[rows].astype(F32) + pair_grad[rows].astype(F32)

    for i in range(B):
        for copy in grad_copy(i):
            copy.wait()
        for copy in cross_copy(i):
            copy.wait_send()
        far_copy(i).wait()
        for n in (1, 2, 3):
            mlp_copy(n, i).wait_send()
    loop(T // 64, join)
    for save in (save_slabs, save_query, save_bias, save_window, save_att, save_lse):
        save.wait()
    for t in range(D // BLOCK):
        save_grads(t).wait()
    behind(mark_own, mark_place, 0, "sent")
    behind(key_place(2), key_place, 3, "sent")
    for i in range(B):
        cot_copy(2, i).wait_send()
        cot_copy(3, i).wait_send()
    if with_slab:
        for gather in (near_rest, near, near_out):
            gather.finish()


def forward(shape, with_slab, tokens, cot, segment, w_gate, w_up, w_down, *slab):
    X, Y, Z = sides(shape)
    R = shape[0]
    T, D = tokens.shape
    E, hz = H * DH, w_gate.shape[1]
    W = 2 * E + 2 * DH + 128
    B = T // BLOCK
    span = WINDOW + BLOCK
    K = Z // 2
    S, V = jax.ShapeDtypeStruct, pltpu.VMEM
    outs = [
        S((T, D), F32), S((T, D), F32), S((T, D), F32), S((T, D), BF), S((8, D), F32),
        S((D, W), BF), S((T, E), BF), S((3 * T, 2 * DH), BF), S((B, span, BLOCK), F32),
        S((E, T), BF), S((H * B, 8, BLOCK), F32), S((K, D, 3 * hz), BF),
    ]
    near, far = gather_count(X, Y, Z), gather_count(X, Y, K)
    scratch = [
        V((D, W), BF), V((K, D, 3 * hz), BF), V((T, E), BF), V((3 * T, 2 * DH), BF),
        V((DH, 3 * T), BF), V((8, 3 * T), F32), V((B, span, BLOCK), F32), V((E, T), BF),
        V((H * B, 8, BLOCK), F32), V((4 * T, D), BF), V((4 * T, D), BF),
        V((BLOCK, D), F32), V((BLOCK, D), F32), V((K, 4 * T, hz), BF), V((K, 4 * T, 2 * hz), BF),
        *[V((T, D), BF)] * 10,
        *[DMA((near,))] * 6, *[DMA((far,))] * 2, *[DMA((3 * R * Z,))] * 2, *[DMA((6,))] * 2,
        *[DMA((1 + 2 * B,))] * 2, *[DMA((3 * B,))] * 2, *[DMA((5 * B,))] * 2, DMA((7,)), DMA((D // BLOCK,)),
    ]
    return pl.pallas_call(
        functools.partial(forward_kernel, shape, with_slab, (D, T, W, hz)),
        out_shape=outs,
        in_specs=[VM, ANY] + [VM] * 4 + [VM if with_slab else ANY] * len(slab),
        out_specs=[VM] * 5 + [ANY] * 7,
        scratch_shapes=scratch,
        compiler_params=pltpu.CompilerParams(
            collective_id=0, has_side_effects=True, vmem_limit_bytes=62 << 20
        ),
        name="forward",
    )(tokens, cot, segment, w_gate, w_up, w_down, *slab)


def backward_kernel(shape, with_slab, sizes, *refs):
    D, T, W, hz = sizes
    E, QK, WO = slab_lanes()
    B = T // BLOCK
    span = WINDOW + BLOCK
    refs = list(refs)

    def some(n):
        taken = refs[:n]
        del refs[:n]
        return taken

    (tokens_in, cot_in, grad_in_in, middle_in, out_own_in, out_far,
     gains_in, slabs_in, query_in, window_in, bias_in, att_in, lse_in, grads) = some(14)
    output, grad_tokens, gate_out, up_out, down_out, out_slab, query_slab = some(7)
    keyval_slab, gain_slab = some(2) if with_slab else (some(1)[0], None)
    (tokens, cot, middle, grad_in, slabs, query, window, bias, att, lse, out_own, out_pair,
     gains, keys_t, branch, att_grad, query_grad_t, query_grad, kv_sum, kv_send, kv_recv, kv_grad, attn_in_t,
     gain_rows, termx, termy, own, ffn_sum) = some(28)
    weight_grads = some(3)
    fwork = some(4)
    if with_slab:
        rest_sum, *crossed = some(4)
        works = [some(4) for _ in range(3)]
    fsend, frecv, ksend, krecv, lsem, tsem = some(6)
    if with_slab:
        nsems = some(6)
        xsend, xrecv = some(2)
    p = Place(shape)
    pack = Pack(p, T)
    mate, spot = pack.mate, pack.spot
    K = p.Z // 2
    br = D // p.R

    def part(s, r):
        return grads.at[s, at(r, br)]

    def cut(ref, h):
        rows = ref.shape[0] // 2
        return ref.at[pl.ds(h * rows, rows)]

    ready = pack.greet()
    order = list(range(1, K)) + [0]
    terms = {}
    for s in order:
        copies = []
        for d in p.xs:
            copies.append((cut(part(s, p.row_at(dx=d)), 1), termx.at[s, d - 1]))
        for e in p.ys:
            copies.append((cut(part(s, p.row_at(dy=e)), 0), termy.at[s, e - 1]))
        copies.append((part(s, p.row), own.at[s]))
        n = s * (p.X + p.Y - 1)
        terms[s] = [
            pltpu.make_async_copy(a, b, tsem.at[n + i]) for i, (a, b) in enumerate(copies)
        ]
    pairs = [
        (middle_in, middle), (grad_in_in, grad_in), (cot_in, cot), (gains_in, gains), (slabs_in, slabs), (att_in, att),
        (tokens_in, tokens), (window_in, window), (query_in, query), (bias_in, bias), (lse_in, lse),
        (out_own_in, out_own),
    ]
    loads = [pltpu.make_async_copy(a, b, lsem.at[n]) for n, (a, b) in enumerate(pairs)]
    for load in loads[:4]:
        load.start()
    ready()
    far = Scatter(
        part, cut, p, Sems(fsend, frecv),
        lambda s, d: termx.at[s, d - 1], lambda s, e: termy.at[s, e - 1], lambda s: own.at[s],
        *fwork, 2
    )
    def far_second():
        for s in order:
            for copy in terms[s]:
                copy.wait()
            far.second(s)

    for s in order:
        far.first(s)
    out_copy = remote(out_far, out_pair, ksend.at[2], krecv.at[2], pack.pair)
    out_copy.start()

    for load in loads[:4]:
        load.wait()
    for load in loads[4:]:
        load.start()
    for s in order:
        for copy in terms[s]:
            copy.start()
    gain_rows[...] = jnp.zeros_like(gain_rows)

    def fold_rows(value):
        return jnp.sum(value.reshape(value.shape[0] // 8, 8, D), axis=0)

    def second_norm(t, total):
        rows = at(t, 64)
        value, grad = middle[rows], grad_in[rows]
        scale = rms_scale(value)
        total = total + fold_rows(grad * (value * scale))
        n = grad * gains[1:2]
        out = cot[rows].astype(F32) + scale * n - value * (
            scale * scale * scale * jnp.mean(n * value, axis=-1, keepdims=True)
        )
        grad_in[rows] = out
        branch[rows] = out.astype(BF)
        return total

    total = lax.fori_loop(0, T // 64, second_norm, jnp.zeros((8, D), F32))
    gain_rows[1:2] = jnp.sum(total, axis=0, keepdims=True)

    loads[4].wait()

    def attended_grad(t):
        att_grad[at(t, BLOCK)] = against(slabs[at(t, BLOCK), WO:], branch[...]).astype(BF)

    loop(E // BLOCK, attended_grad)
    loads[5].wait()
    ar = D // (p.R * p.Z * 2)
    blocks = BLOCK // (2 * ar)

    def put(ref, t, lanes, value):
        if with_slab:
            ref[pl.ds(t * blocks, blocks), :, :, lanes] = value.astype(BF).reshape(
                blocks, 2, ar, value.shape[1]
            )
        else:
            ref[at(t, BLOCK), lanes] = value.astype(BF)

    def out_weight_grad(t):
        put(weight_grads[0], t, slice(0, E), product(att[at(t, BLOCK)], branch[...]))

    loop(E // BLOCK, out_weight_grad)

    class Near:
        def __init__(self, n):
            self.n, self.ref = n, weight_grads[n]
            self.copy = remote(
                self.ref.at[:, 1 - p.core], crossed[n], xsend.at[n], xrecv.at[n], mate
            )
            self.copy.start()

        def block(self, s, r):
            return self.ref.at[r * p.Z + p.z_at(s), p.core]

        def fold(self):
            self.copy.wait()
            ref, other = self.ref, crossed[self.n]

            def step(n):
                ref[n, p.core] = (ref[n, p.core].astype(F32) + other[n].astype(F32)).astype(BF)

            loop(p.R * p.Z, step)
            block = self.block
            self.scatter = Scatter(
                block, cut, p, Sems(*nsems[2 * self.n : 2 * self.n + 2]),
                lambda s, d: cut(block(s, p.row_at(dx=d)), 1),
                lambda s, e: cut(block(s, p.row_at(dy=e)), 0),
                lambda s: block(s, p.row), *works[self.n]
            )
            for s in self.order():
                self.scatter.first(s)

        def order(self):
            return list(range(1, p.Z)) + [0]

        def second(self):
            for s in self.order():
                self.scatter.second(s)

        def third(self):
            for s in self.order()[:-1]:
                self.scatter.third(s)

        def last(self, out):
            self.scatter.third(0, out)
            self.scatter.finish()

    if with_slab:
        near_out = Near(0)

    for load in loads[6:]:
        load.wait()

    def first_norm(t):
        cols = at(t, 128)
        value = tokens[cols].astype(F32)
        attn_in_t[:, cols] = (value * rms_scale(value) * gains[0:1]).astype(BF).T

    loop(T // 128, first_norm)
    keys_t[...] = window[:, 0:DH].T
    kv_sum[...] = jnp.zeros_like(kv_sum)
    if with_slab:
        near_out.fold()

    factor = LOG2E / math.sqrt(DH)
    scale = 1.0 / math.sqrt(DH)

    def head(i, h):
        lanes = at(h, DH)
        here = pl.ds(i * BLOCK, BLOCK)
        seen = pl.ds(i * BLOCK, span)
        part_query = query[here, lanes]
        part_grad = att_grad[lanes, here]
        scores = against(window[seen, 0:DH], part_query) * factor + bias[i]
        probs = jnp.exp2(scores - lse[h * B + i][0:1])
        grad_probs = product(window[seen, DH:], part_grad)
        centre = jnp.sum(
            att[lanes, here].astype(F32) * part_grad.astype(F32), axis=0, keepdims=True
        )
        grad_scores = (probs * (grad_probs - centre)).astype(BF)
        kv_sum[seen, DH:] += against(probs.astype(BF), part_grad)
        kv_sum[seen, 0:DH] += product(grad_scores, part_query)
        query_grad_t[lanes, here] = (product(keys_t[:, seen], grad_scores) * scale).astype(BF)

    for i in range(B):
        loop(H, lambda h: head(i, h))

    kv_send[:, 0:DH] = (kv_sum[pl.ds(0, 2 * T), 0:DH] * scale).astype(BF)
    kv_send[:, DH:] = kv_sum[pl.ds(0, 2 * T), DH:].astype(BF)
    returns = []
    for d in (1, 2):
        to = (p.row, lax.rem(p.col - d + 2 * p.Z, 2 * p.Z))
        copy = remote(
            kv_send.at[pl.ds((2 - d) * T, T)], kv_recv.at[d - 1], ksend.at[d - 1], krecv.at[d - 1], to
        )
        pl.when(spot - d >= 0)(copy.start)
        returns.append((d, copy))

    far_second()
    if with_slab:
        near_out.second()

    def turn(t):
        query_grad[at(t, BLOCK)] = query_grad_t[:, at(t, BLOCK)].T

    loop(B, turn)

    def query_weight_grad(t):
        put(weight_grads[1], t, slice(0, E), product(attn_in_t[at(t, BLOCK)], query_grad[...]))

    loop(D // BLOCK, query_weight_grad)
    if with_slab:
        near_query = Near(1)

    def input_grad_query(t):
        rows = at(t, 128)
        grad_tokens[rows] = against(query_grad[rows], slabs[:, 0:E])

    loop(T // 128, input_grad_query)
    kv_grad[:, 0:DH] = kv_sum[pl.ds(2 * T, T), 0:DH] * scale
    kv_grad[:, DH:] = kv_sum[pl.ds(2 * T, T), DH:]
    if with_slab:
        near_query.fold()
    for d, copy in returns:
        @pl.when(spot + d < pack.size)
        def _():
            copy.wait_recv()
            kv_grad[...] += kv_recv[d - 1].astype(F32)

    window[pl.ds(0, T)] = kv_grad[...].astype(BF)

    def keyval_weight_grad(t):
        put(weight_grads[2], t, slice(0, 2 * DH), product(attn_in_t[at(t, BLOCK)], window[pl.ds(0, T)]))

    loop(D // BLOCK, keyval_weight_grad)

    def input_grad(t, total):
        rows = at(t, 128)
        grad = grad_tokens[rows] + against(window[rows], slabs[:, E:QK])
        value = tokens[rows].astype(F32)
        scale_first = rms_scale(value)
        total = total + fold_rows(grad * (value * scale_first))
        m = grad * gains[0:1]
        grad_tokens[rows] = grad_in[rows] + scale_first * m - value * (
            scale_first * scale_first * scale_first * jnp.mean(m * value, axis=-1, keepdims=True)
        )
        return total

    total = lax.fori_loop(0, T // 128, input_grad, jnp.zeros((8, D), F32))
    gain_rows[0:1] = jnp.sum(total, axis=0, keepdims=True)

    def gain_grad(t):
        put(weight_grads[2], t, slice(2 * DH, 2 * DH + 128), gain_rows[:, at(t, BLOCK)].T)

    loop(D // BLOCK, gain_grad)
    if with_slab:
        near_rest = Near(2)
    for s in order[:-1]:
        far.third(s)
    if with_slab:
        near_query.second()
        near_rest.fold()
        near_out.third()
        near_query.third()
        near_rest.second()
        near_rest.third()
        near_out.last(out_slab)
    else:
        for ref, out in zip(weight_grads, (out_slab, query_slab, keyval_slab)):
            out[...] = ref[...]
    out_copy.wait_recv()

    def join(t):
        rows = at(t, 64)
        output[rows] = (out_own[rows] + out_pair[rows].astype(F32)).astype(BF)

    loop(T // 64, join)
    far.third(0, ffn_sum)
    gate_out[...] = ffn_sum[:, 0:hz]
    up_out[...] = ffn_sum[:, hz : 2 * hz]
    down_out[...] = ffn_sum[:, 2 * hz :].T
    if with_slab:
        near_query.last(query_slab)
        near_rest.last(rest_sum)
        keyval_slab[...] = rest_sum[:, 0 : 2 * DH]
        gain_slab[...] = rest_sum[:, 2 * DH :]
    out_copy.wait_send()
    for d, copy in returns:
        pl.when(spot - d >= 0)(copy.wait_send)
    far.finish()


def backward(
    shape, with_slab, tokens, cot, grad_in, middle, out_own, out_far, gains, slabs, query, window, bias, att, lse, grads
):
    X, Y, Z = sides(shape)
    R = shape[0]
    T, D = tokens.shape
    E, hz = H * DH, grads.shape[2] // 3
    W = slabs.shape[1]
    B = T // BLOCK
    span = WINDOW + BLOCK
    K = Z // 2
    near, far = scatter_count(X, Y, Z), scatter_count(X, Y, K)
    S, V = jax.ShapeDtypeStruct, pltpu.VMEM
    block = (D // R, 3 * hz)
    half = (block[0] // 2, block[1])
    widths = (E, E, 2 * DH + 128)
    ar = D // (R * Z * 2)
    if with_slab:
        slab_outs = [S((ar, w), F32) for w in (E, E, 2 * DH, 128)]
        slab_work = [V((R * Z, 2, ar, w), BF) for w in widths]
    else:
        slab_outs = [S((D, w), BF) for w in widths]
        slab_work = [V((D, w), BF) for w in widths]
    outs = [S((T, D), BF), S((T, D), F32)]
    outs += [S((D // R, hz), F32), S((D // R, hz), F32), S((hz, D // R), F32)] + slab_outs
    scratch = [
        V((T, D), BF), V((T, D), BF), V((T, D), F32), V((T, D), F32), V((D, W), BF), V((T, E), BF),
        V((3 * T, 2 * DH), BF), V((B, span, BLOCK), F32), V((E, T), BF), V((H * B, 8, BLOCK), F32),
        V((T, D), F32), V((T, D), BF),
        V((8, D), F32), V((DH, 3 * T), BF), V((T, D), BF), V((E, T), BF), V((E, T), BF), V((T, E), BF),
        V((3 * T, 2 * DH), F32), V((2 * T, 2 * DH), BF), V((2, T, 2 * DH), BF), V((T, 2 * DH), F32),
        V((D, T), BF), V((128, D), F32),
        V((K, X - 1) + half, BF), V((K, Y - 1) + half, BF), V((K,) + block, BF), V(block, F32),
        *slab_work,
        *scatter_scratch(X, Y, K, block),
    ]
    if with_slab:
        scratch += [V((ar, widths[2]), F32)] + [V((R * Z, ar, w), BF) for w in widths]
        for w in widths:
            scratch += scatter_scratch(X, Y, Z, (ar, w))
    scratch += [
        DMA((far,)), DMA((far,)), DMA((3,)), DMA((3,)), DMA((12,)), DMA((K * (X + Y - 1),)),
    ]
    if with_slab:
        scratch += [DMA((near,))] * 6 + [DMA((3,))] * 2
    return pl.pallas_call(
        functools.partial(backward_kernel, shape, with_slab, (D, T, W, hz)),
        out_shape=outs,
        in_specs=[ANY] * 14,
        out_specs=[VM] * len(outs),
        scratch_shapes=scratch,
        compiler_params=pltpu.CompilerParams(
            collective_id=1, has_side_effects=True, vmem_limit_bytes=62 << 20
        ),
        name="backward",
    )(tokens, cot, grad_in, middle, out_own, out_far, gains, slabs, query, window, bias, att, lse, grads)


def hand_over_kernel(count, *refs):
    sources, results, held, sems = refs[:count], refs[count : 2 * count], refs[2 * count : -1], refs[-1]
    reads = [pltpu.make_async_copy(a, b, sems.at[0, n]) for n, (a, b) in enumerate(zip(sources, held))]
    writes = [pltpu.make_async_copy(a, b, sems.at[1, n]) for n, (a, b) in enumerate(zip(held, results))]
    for read in reads:
        read.start()
    for read, write in zip(reads, writes):
        read.wait()
        write.start()
    for write in writes:
        write.wait()


def hand_over(arrays):
    count = len(arrays)
    return pl.pallas_call(
        functools.partial(hand_over_kernel, count),
        out_shape=[jax.ShapeDtypeStruct(a.shape, a.dtype) for a in arrays],
        in_specs=[ANY] * count,
        out_specs=[ANY] * count,
        scratch_shapes=[pltpu.VMEM(a.shape, a.dtype) for a in arrays] + [DMA((2, count))],
        compiler_params=pltpu.CompilerParams(vmem_limit_bytes=62 << 20),
        name="hand_over",
    )(*arrays)


def shards(
    shape,
    tokens, gain_attn, w_query, w_keyval, w_out, gain_mlp, w_gate, w_up, w_down, segment, cotangent
):
    with_slab = w_query.shape[0] % 32 == 0
    gain_columns = jnp.pad(jnp.stack([gain_attn, gain_mlp], axis=1), ((0, 0), (0, 126)))
    slab = [w_query, w_keyval, gain_columns, w_out]
    if not with_slab:
        slab = [lax.all_gather(jnp.concatenate(slab, axis=1), ("row", "col"), axis=0, tiled=True)]
    kept = forward(shape, with_slab, tokens, cotangent, segment[None], w_gate, w_up, w_down, *slab)
    results = backward(shape, with_slab, tokens, cotangent, *kept)
    output, grad_tokens, gate_grad, up_grad, down_grad = results[:5]
    if with_slab:
        *arrays, gain_grad = results
        output, grad_tokens, gate_grad, up_grad, down_grad, out_grad, query_grad, keyval_grad = hand_over(
            arrays)
    else:
        out_grad, query_grad, rest_grad = [
            lax.psum_scatter(g.astype(F32), ("row", "col"), scatter_dimension=0, tiled=True)
            for g in results[5:]
        ]
        keyval_grad, gain_grad = rest_grad[:, : 2 * DH], rest_grad[:, 2 * DH :]
    return (
        output,
        grad_tokens,
        gain_grad[:, 0],
        query_grad,
        keyval_grad,
        out_grad,
        gain_grad[:, 1],
        gate_grad,
        up_grad,
        down_grad,
    )


def solution(mesh):
    shape = (mesh.shape["row"], mesh.shape["col"])
    return jax.shard_map(
        functools.partial(shards, shape),
        mesh=mesh,
        in_specs=(
            P(("row", "col"), None),
            P(("row", "col")),
            P(("row", "col"), None),
            P(("row", "col"), None),
            P(("row", "col"), None),
            P(("row", "col")),
            P("row", "col"),
            P("row", "col"),
            P("col", "row"),
            P(("row", "col")),
            P(("row", "col"), None),
        ),
        out_specs=(
            P(("row", "col"), None),
            P(("row", "col"), None),
            P(("row", "col")),
            P(("row", "col"), None),
            P(("row", "col"), None),
            P(("row", "col"), None),
            P(("row", "col")),
            P("row", "col"),
            P("row", "col"),
            P("col", "row"),
        ),
        check_vma=False,
    )
```

```python
import functools
import math

import jax
import jax.numpy as jnp
from jax import lax
from jax.experimental import pallas as pl
from jax.experimental.pallas import tpu as pltpu
from jax.sharding import PartitionSpec as P

H = 8
DH = 128
WINDOW = 1024
PACK = 2048

EPS = 1e-06
NEGATIVE = -1e30
MESH = pl.DeviceIdType.MESH
BF = jnp.bfloat16
F32 = jnp.float32


def product(left, right):
    return jnp.dot(left, right, preferred_element_type=jnp.float32)


def inner(left, right):
    return lax.dot_general(
        left, right, (((0,), (0,)), ((), ())), preferred_element_type=jnp.float32
    )


def against(left, right):
    return lax.dot_general(
        left, right, (((1,), (1,)), ((), ())), preferred_element_type=jnp.float32
    )


class Place:
    def __init__(self, shape):
        rows, cols = shape
        self.X = math.isqrt(rows)
        while rows % self.X:
            self.X -= 1
        self.Y = rows // self.X
        self.Z = cols // 2
        self.R = rows
        self.row, self.col = lax.axis_index("row"), lax.axis_index("col")
        self.y, self.x = self.row // self.X, self.row % self.X
        self.z, self.core = self.col // 2, self.col % 2
        self.xs, self.ys, self.zs = range(1, self.X), range(1, self.Y), range(1, self.Z)

    def row_at(self, dy=0, dx=0):
        return lax.rem(self.y + dy + self.Y, self.Y) * self.X + lax.rem(
            self.x + dx + self.X, self.X
        )

    def z_at(self, dz):
        return lax.rem(self.z + dz + self.Z, self.Z)

    def device(self, dy=0, dx=0, dz=0, other=False):
        core = 1 - self.core if other else self.core
        return (self.row_at(dy, dx), self.z_at(dz) * 2 + core)


def remote(src, dst, send, recv, device):
    return pltpu.make_async_remote_copy(
        src_ref=src, dst_ref=dst, send_sem=send, recv_sem=recv, device_id=device,
        device_id_type=MESH,
    )


class Sems:
    def __init__(self, send, recv):
        self.send, self.recv, self.count = send, recv, 0

    def take(self):
        self.count += 1
        return self.send.at[self.count - 1], self.recv.at[self.count - 1]


def gather_count(X, Y, K):
    return (K - 1) + K * ((X - 1) + (Y - 1) + 2 * (X - 1) * (Y - 1))


class Gather:
    def __init__(self, at, dest, here, sems, own, stride=1):
        self.at, self.dest, self.p, self.own = at, dest, here, own
        self.stride, self.K = stride, here.Z // stride
        self.sent = []
        p = here
        self.zsem = {k: sems.take() for k in range(1, self.K)}
        self.xsem = {(s, d): sems.take() for s in range(self.K) for d in p.xs}
        self.ysem = {(s, d): sems.take() for s in range(self.K) for d in p.ys}
        self.dsem = {
            (s, h, dx, dy): sems.take()
            for s in range(self.K) for h in (0, 1) for dx in p.xs for dy in p.ys
        }

    def push(self, src, dst, sem, device):
        copy = remote(src, dst, sem[0], sem[1], device)
        copy.start()
        self.sent.append(copy)

    def arrive(self, place, sem):
        remote(place, place, sem[0], sem[1], self.p.device(other=True)).wait_recv()

    def spread_z(self):
        p = self.p
        for k in range(1, self.K):
            self.push(self.own, self.dest(k), self.zsem[k], p.device(dz=-self.stride * k))

    def spread_xy(self, s):
        if s >= self.K:
            return
        p = self.p
        place = self.at(s, p.row, None)
        src = self.own
        if s:
            self.arrive(place, self.zsem[s])
            src = place
        for d in p.xs:
            self.push(src, place, self.xsem[s, d], p.device(dx=d))
        for d in p.ys:
            self.push(src, place, self.ysem[s, d], p.device(dy=d))

    def spread_diagonal(self, s):
        if s >= self.K:
            return
        p = self.p
        for d in p.xs:
            r = p.row_at(dx=-d)
            self.arrive(self.at(s, r, None), self.xsem[s, d])
            half = self.at(s, r, 0)
            for e in p.ys:
                self.push(half, half, self.dsem[s, 0, d, e], p.device(dy=e))
        for e in p.ys:
            r = p.row_at(dy=-e)
            self.arrive(self.at(s, r, None), self.ysem[s, e])
            half = self.at(s, r, 1)
            for d in p.xs:
                self.push(half, half, self.dsem[s, 1, d, e], p.device(dx=d))

    def close(self, s):
        p = self.p
        for d in p.xs:
            for e in p.ys:
                r = p.row_at(dy=-e, dx=-d)
                for h in (0, 1):
                    self.arrive(self.at(s, r, h), self.dsem[s, h, d, e])

    def finish(self):
        for copy in self.sent:
            copy.wait_send()


def scatter_count(X, Y, K):
    return (K - 1) + K * (2 * (X - 1) * (Y - 1) + 2 * (X - 1) + 2 * (Y - 1))


class Scatter:
    def __init__(
        self, part, cut, here, sems, termx, termy, own, diag, fromx, fromy, fromz, stride=1
    ):
        self.part, self.cut, self.p = part, cut, here
        self.termx, self.termy, self.own = termx, termy, own
        self.diag, self.fromx, self.fromy, self.fromz = diag, fromx, fromy, fromz
        self.stride, self.K = stride, here.Z // stride
        self.sent = []
        p = here
        self.zsem = {k: sems.take() for k in range(1, self.K)}
        self.xsem = {(s, h, d): sems.take() for s in range(self.K) for h in (0, 1) for d in p.xs}
        self.ysem = {(s, h, d): sems.take() for s in range(self.K) for h in (0, 1) for d in p.ys}
        self.dsem = {
            (s, h, dx, dy): sems.take()
            for s in range(self.K) for h in (0, 1) for dx in p.xs for dy in p.ys
        }

    def push(self, src, dst, sem, device):
        copy = remote(src, dst, sem[0], sem[1], device)
        copy.start()
        self.sent.append(copy)

    def arrive(self, place, sem):
        remote(place, place, sem[0], sem[1], self.p.device(other=True)).wait_recv()

    def spot(self, d, e):
        return (d - 1) * (self.p.Y - 1) + e - 1

    def first(self, s):
        p, cut = self.p, self.cut
        for d in p.xs:
            for e in p.ys:
                far = self.part(s, p.row_at(dy=e, dx=d))
                n = self.spot(d, e)
                self.push(cut(far, 0), self.diag.at[s, 0, n], self.dsem[s, 0, d, e], p.device(dx=d))
                self.push(cut(far, 1), self.diag.at[s, 1, n], self.dsem[s, 1, d, e], p.device(dy=e))
        for d in p.xs:
            near = self.part(s, p.row_at(dx=d))
            self.push(cut(near, 0), cut(self.fromx.at[s, d - 1], 0), self.xsem[s, 0, d], p.device(dx=d))
        for e in p.ys:
            near = self.part(s, p.row_at(dy=e))
            self.push(cut(near, 1), cut(self.fromy.at[s, e - 1], 1), self.ysem[s, 1, e], p.device(dy=e))

    def second(self, s):
        p, cut = self.p, self.cut
        for e in p.ys:
            term = self.termy(s, e)
            total = term[...].astype(F32)
            for d in p.xs:
                place = self.diag.at[s, 0, self.spot(d, e)]
                self.arrive(place, self.dsem[s, 0, d, e])
                total = total + place[...].astype(F32)
            term[...] = total.astype(BF)
            self.push(term, cut(self.fromy.at[s, e - 1], 0), self.ysem[s, 0, e], p.device(dy=e))
        for d in p.xs:
            term = self.termx(s, d)
            total = term[...].astype(F32)
            for e in p.ys:
                place = self.diag.at[s, 1, self.spot(d, e)]
                self.arrive(place, self.dsem[s, 1, d, e])
                total = total + place[...].astype(F32)
            term[...] = total.astype(BF)
            self.push(term, cut(self.fromx.at[s, d - 1], 1), self.xsem[s, 1, d], p.device(dx=d))

    def third(self, s, out=None):
        p, cut = self.p, self.cut
        own = self.own(s)
        total = own[...].astype(F32)
        for d in p.xs:
            for h in (0, 1):
                self.arrive(cut(self.fromx.at[s, d - 1], h), self.xsem[s, h, d])
            total = total + self.fromx[s, d - 1].astype(F32)
        for e in p.ys:
            for h in (0, 1):
                self.arrive(cut(self.fromy.at[s, e - 1], h), self.ysem[s, h, e])
            total = total + self.fromy[s, e - 1].astype(F32)
        if s:
            own[...] = total.astype(BF)
            self.push(own, self.fromz.at[s - 1], self.zsem[s], p.device(dz=self.stride * s))
            return
        for k in range(1, self.K):
            self.arrive(self.fromz.at[k - 1], self.zsem[k])
            total = total + self.fromz[k - 1].astype(F32)
        out[...] = total

    def finish(self):
        for copy in self.sent:
            copy.wait_send()


def scatter_scratch(X, Y, K, block):
    half = (block[0] // 2, block[1])
    return [
        pltpu.VMEM((K, 2, (X - 1) * (Y - 1)) + half, BF),
        pltpu.VMEM((K, X - 1) + block, BF),
        pltpu.VMEM((K, Y - 1) + block, BF),
        pltpu.VMEM((max(K - 1, 1),) + block, BF),
    ]


def sides(shape):
    x = math.isqrt(shape[0])
    while shape[0] % x:
        x -= 1
    return x, shape[0] // x, shape[1] // 2


VM = pl.BlockSpec(memory_space=pltpu.VMEM)
ANY = pl.BlockSpec(memory_space=pl.ANY)
DMA = pltpu.SemaphoreType.DMA
LOG2E = math.log2(math.e)
BLOCK = 256


def loop(count, body):
    def step(t, carry):
        body(t)
        return carry

    lax.fori_loop(0, count, step, 0)


def at(t, size):
    return pl.ds(pl.multiple_of(t * size, size), size)


def rms_scale(value):
    return lax.rsqrt(jnp.mean(value * value, axis=-1, keepdims=True) + EPS)


def gelu_parts(gate):
    square = gate * gate
    t = jnp.tanh(gate * (0.7978845608 + (0.7978845608 * 0.044715) * square))
    half = 0.5 + 0.5 * t
    slope = half + (0.5 * gate) * (1.0 - t * t) * (
        0.7978845608 + (3 * 0.7978845608 * 0.044715) * square
    )
    return gate * half, slope


class Pack:
    def __init__(self, here, T):
        p = here
        self.p, self.size = p, PACK // T
        self.spot = lax.rem(p.col, self.size)
        pair = (p.z // 2) * 2 + 1 - lax.rem(p.z, 2)
        self.mate = p.device(other=True)
        self.pair = (p.row, pair * 2 + p.core)
        self.across = (p.row, pair * 2 + 1 - p.core)

    def greet(self):
        p = self.p
        barrier = pltpu.get_barrier_semaphore()
        mates = [p.device(dx=d) for d in p.xs] + [p.device(dy=d) for d in p.ys]
        mates += [p.device(dz=d) for d in p.zs] + [self.mate, self.across]
        for mate in mates:
            pl.semaphore_signal(barrier, inc=1, device_id=mate, device_id_type=MESH)
        return lambda: pl.semaphore_wait(barrier, len(mates))


def slab_lanes():
    E, QK = H * DH, H * DH + 2 * DH
    return E, QK, QK + 128


def forward_kernel(shape, with_slab, sizes, *refs):
    D, T, W, hz = sizes
    (tokens, cot, segment, w_gate, w_up, w_down, *slab_in) = refs[: 10 if with_slab else 7]
    (grad_in, middle, out_own, out_far, gains, slabs_out, query_out, window_out, bias_out, att_out, lse_out, grads_out,
     slabs, ffns, query, window, values_t, marks_all, bias, att, lse, mlp, cots,
     grad_tile, out_tile, hidden, grad_act, side_grad, side_out, cross_grad, cross_out, far_grad,
     mate_grad, mate_out, pre_grad, pre_out, pair_grad,
     vsend, vrecv, asend, arecv, osend, orecv, fsend, frecv, csend, crecv, ksend, krecv, tsend, trecv,
     msend, mrecv, gsend, grecv, lsem, gsem) = refs[10 if with_slab else 7 :]
    p = Place(shape)
    pack = Pack(p, T)
    mate, pair, spot = pack.mate, pack.pair, pack.spot
    E, QK, WO = slab_lanes()
    B = T // BLOCK
    span = WINDOW + BLOCK
    K = p.Z // 2

    def local(src, dst, n):
        copy = pltpu.make_async_copy(src, dst, lsem.at[n])
        copy.start()
        return copy

    ready = pack.greet()
    load_cot = local(cot, cots.at[pl.ds(0, T)], 0)
    if not with_slab:
        load_slab = local(slab_in[0], slabs, 1)
    br = w_gate.shape[0]
    own_rows = at(p.row, br)
    ffns[0, own_rows, 0:hz] = w_gate[...]
    ffns[0, own_rows, hz : 2 * hz] = w_up[...]
    ffns[0, own_rows, 2 * hz :] = w_down[...].T

    def ffn_at(s, r, half):
        if half is None:
            return ffns.at[s, at(r, br)]
        return ffns.at[s, pl.ds(pl.multiple_of(r * br + half * (br // 2), br // 2), br // 2)]

    far = Gather(
        ffn_at, lambda k: ffn_at(k, p.row, None), p, Sems(fsend, frecv), ffn_at(0, p.row, None), 2
    )

    if with_slab:
        ar = slab_in[0].shape[0]
        slab_rows = pl.ds(pl.multiple_of(((p.row * p.Z + p.z) * 2 + p.core) * ar, ar), ar)
        widths = ((0, E), (E, QK), (QK, WO), (WO, W))
        for piece, (start, stop) in zip(slab_in, widths):
            slabs[slab_rows, start:stop] = piece[...]

        def slab_place(lanes, core):
            def place(s, r, half):
                start = ((r * p.Z + p.z_at(s)) * 2 + core) * ar
                if half is None:
                    return slabs.at[pl.ds(pl.multiple_of(start, ar), ar), lanes]
                start = pl.multiple_of(start + half * (ar // 2), ar // 2)
                return slabs.at[pl.ds(start, ar // 2), lanes]

            return place

        def slab_gather(lanes, sems):
            place = slab_place(lanes, p.core)
            own = place(0, p.row, None)
            return Gather(place, lambda k: own, p, sems, own)

        rest_lanes, act_lanes, out_lanes = slice(E, WO), slice(0, E), slice(WO, W)
        near_rest = slab_gather(rest_lanes, Sems(vsend, vrecv))
        near = slab_gather(act_lanes, Sems(asend, arecv))
        near_out = slab_gather(out_lanes, Sems(osend, orecv))
        hands = Sems(csend, crecv)

        def hand(gather, lanes):
            mine, theirs = slab_place(lanes, p.core), slab_place(lanes, 1 - p.core)
            passed = []
            for s in range(p.Z):
                gather.close(s)
                for dy in range(p.Y):
                    for dx in range(p.X):
                        r = p.row_at(dy, dx)
                        send, recv = hands.take()
                        place, other = mine(s, r, None), theirs(s, r, None)
                        copy = remote(place, place, send, recv, mate)
                        copy.start()
                        passed.append((copy, remote(other, other, send, recv, mate)))
            return passed

        def settle(passed):
            for copy, arrival in passed:
                copy.wait_send()
                arrival.wait_recv()

    ready()
    if with_slab:
        near_rest.spread_z()
        near_rest.spread_xy(0)
        near.spread_z()
        near.spread_xy(0)
        near_out.spread_z()

    marks_all[:, pl.ds(2 * T, T)] = jnp.broadcast_to(segment[...].astype(F32), (8, T))

    @pl.when(spot == 0)
    def _():
        window[pl.ds(0, 2 * T), :] = jnp.zeros((2 * T, 2 * DH), BF)
        marks_all[:, pl.ds(0, 2 * T)] = jnp.full((8, 2 * T), -1.0, F32)

    @pl.when(spot == 1)
    def _():
        window[pl.ds(0, T), :] = jnp.zeros((T, 2 * DH), BF)
        marks_all[:, pl.ds(0, T)] = jnp.full((8, T), -1.0, F32)

    def behind(src, place, n, op):
        for d in (1, 2):
            to = (p.row, lax.rem(p.col + d, 2 * p.Z))
            copy = remote(src, place(2 - d), ksend.at[n + d], krecv.at[n + d], to)
            if op == "start":
                pl.when(spot + d < pack.size)(copy.start)
            elif op == "arrive":
                pl.when(spot - d >= 0)(copy.wait_recv)
            else:
                pl.when(spot + d < pack.size)(copy.wait_send)

    mark_place = lambda k: marks_all.at[:, pl.ds(k * T, T)]
    mark_own = mark_place(2)
    behind(mark_own, mark_place, 0, "start")

    def whole(ref, n):
        return ref.at[pl.ds(n * T, T)]

    load_cot.wait()
    cot_mate = remote(whole(cots, 0), whole(cots, 1), tsend.at[0], trecv.at[0], mate)
    cot_mate.start()

    def tile_of(ref, n, i):
        return ref.at[pl.ds(pl.multiple_of(n * T + i * BLOCK, BLOCK), BLOCK)]

    def cot_copy(n, i):
        to, src, sem = (pair, 0, 1 + i) if n == 2 else (mate, 2, 1 + B + i)
        return remote(tile_of(cots, src, i), tile_of(cots, n, i), tsend.at[sem], trecv.at[sem], to)

    if with_slab:
        for s in range(p.Z):
            near_rest.spread_xy(s + 1)
            near_rest.spread_diagonal(s)
        for s in range(1, p.Z):
            near.spread_xy(s)
        passed = hand(near_rest, rest_lanes)
        for s in range(p.Z):
            near.spread_diagonal(s)
        settle(passed)
    else:
        load_slab.wait()
    gains[...] = slabs[:, QK:WO].astype(F32).T[0:8]

    def first_norm(t):
        rows = at(t, 64)
        value = tokens[rows].astype(F32)
        mlp[rows] = (value * rms_scale(value) * gains[0:1]).astype(BF)

    loop(T // 64, first_norm)
    window[pl.ds(2 * T, T)] = product(mlp[pl.ds(0, T)], slabs[:, E:QK]).astype(BF)
    key_place = lambda k: window.at[pl.ds(k * T, T)]
    behind(key_place(2), key_place, 3, "start")

    far.spread_z()
    cot_copy(2, 0).start()
    if with_slab:
        for s in range(p.Z):
            near_out.spread_xy(s)
        settle(hand(near, act_lanes))

    def project(t):
        query[at(t, BLOCK)] = product(mlp[at(t, BLOCK)], slabs[:, 0:E]).astype(BF)

    loop(B, project)
    save_query = local(query, query_out, 2)
    if with_slab:
        for s in range(p.Z):
            near_out.spread_diagonal(s)
    far.spread_xy(0)
    behind(mark_own, mark_place, 0, "arrive")
    column = jnp.broadcast_to(marks_all[0:1], (128, 3 * T)).T
    for i in range(B):
        keys_at = jnp.concatenate([column[i * BLOCK : i * BLOCK + span]] * (BLOCK // 128), axis=1)
        own = marks_all[0:1, 2 * T + i * BLOCK : 2 * T + (i + 1) * BLOCK]
        gap = (
            WINDOW
            + lax.broadcasted_iota(jnp.int32, (span, BLOCK), 1)
            - lax.broadcasted_iota(jnp.int32, (span, BLOCK), 0)
        )
        allowed = (keys_at == own) & (gap >= 0) & (gap < WINDOW)
        bias[i] = jnp.where(allowed, 0.0, NEGATIVE)
    save_bias = local(bias, bias_out, 3)
    if with_slab:
        passed = hand(near_out, out_lanes)
    behind(key_place(2), key_place, 3, "arrive")
    for i in range(1, B):
        cot_copy(2, i).start()
    save_window = local(window, window_out, 4)
    values_t[...] = window[:, DH:].T
    factor = LOG2E / math.sqrt(DH)

    def head(i, h):
        lanes = at(h, DH)
        keys = window[pl.ds(i * BLOCK, span), 0:DH]
        scores = against(keys, query[pl.ds(i * BLOCK, BLOCK), lanes]) * factor + bias[i]
        top = jnp.max(scores, axis=0, keepdims=True)
        expo = jnp.exp2(scores - top)
        total = jnp.sum(expo, axis=0, keepdims=True)
        mixed = product(values_t[:, pl.ds(i * BLOCK, span)], expo.astype(BF))
        att[lanes, pl.ds(i * BLOCK, BLOCK)] = (mixed / total).astype(BF)
        lse[h * B + i] = jnp.broadcast_to(top + jnp.log2(total), (8, BLOCK))

    def mlp_copy(n, i):
        to = pair if n == 2 else mate
        src = 2 if n == 3 else 0
        sem = (n - 1) * B + i
        return remote(tile_of(mlp, src, i), tile_of(mlp, n, i), msend.at[sem], mrecv.at[sem], to)

    for i in range(B):
        if i == 0:
            loop(H // 2, lambda h: head(i, h))
            far.spread_xy(1)
            far.spread_diagonal(0)
            loop(H // 2, lambda h: head(i, h + H // 2))
            if with_slab:
                settle(passed)
            save_slabs = local(slabs, slabs_out, 1)
        else:
            loop(H, lambda h: head(i, h))
        cols = pl.ds(i * BLOCK, BLOCK)
        middle[cols] = product(att[:, cols].T, slabs[:, WO:]) + tokens[cols].astype(F32)

        def second_norm(t):
            rows = pl.ds(pl.multiple_of(i * BLOCK + t * 64, 64), 64)
            value = middle[rows]
            mlp[rows] = (value * rms_scale(value) * gains[1:2]).astype(BF)

        loop(BLOCK // 64, second_norm)
        mlp_copy(1, i).start()
        mlp_copy(2, i).start()
        cot_copy(2, i).wait_recv()
        cot_copy(3, i).start()
    save_att = local(att, att_out, 5)
    save_lse = local(lse, lse_out, 6)
    for s in range(2, K):
        far.spread_xy(s)
    for s in range(1, K):
        far.spread_diagonal(s)
    mlp_copy(2, 0).wait_recv()
    mlp_copy(3, 0).start()
    for s in range(K):
        far.close(s)
    cot_mate.wait()
    for i in range(B):
        cot_copy(3, i).wait_recv()

    def grad_copy(i):
        return [
            remote(tile_of(side_grad, 0, i), tile_of(mate_grad, 0, i), gsend.at[i], grecv.at[i], mate),
            remote(tile_of(side_out, 0, i), tile_of(mate_out, 0, i), gsend.at[B + i], grecv.at[B + i], mate),
        ]

    def cross_copy(i):
        n = 2 * B
        return [
            remote(tile_of(cross_grad, 0, i), tile_of(pre_grad, 0, i), gsend.at[n + i], grecv.at[n + i], mate),
            remote(tile_of(cross_out, 0, i), tile_of(pre_out, 0, i), gsend.at[n + B + i], grecv.at[n + B + i], mate),
        ]

    def far_copy(i):
        n = 4 * B + i
        return remote(tile_of(far_grad, 0, i), tile_of(pair_grad, 0, i), gsend.at[n], grecv.at[n], pair)

    def feed(t):
        i, kind = t // 4, lax.rem(t, 4)
        n = jnp.where(kind == 2, 3, jnp.where(kind == 3, 2, kind))

        @pl.when(kind == 1)
        def _():
            mlp_copy(1, i).wait_recv()

        @pl.when(kind == 2)
        def _():
            mlp_copy(3, i).wait_recv()

        rows = pl.ds(pl.multiple_of(n * T + i * BLOCK, BLOCK), BLOCK)
        for s in range(K):
            gate_up = product(mlp[rows], ffns[s, :, 0 : 2 * hz])
            grad_hidden = product(cots[rows], ffns[s, :, 2 * hz :])
            up = gate_up[:, hz:]
            act, slope = gelu_parts(gate_up[:, :hz])
            hidden[s, rows] = (act * up).astype(BF)
            grad_act[s, rows, 0:hz] = (grad_hidden * up * slope).astype(BF)
            grad_act[s, rows, hz : 2 * hz] = (grad_hidden * act).astype(BF)
            outs = against(hidden[s, rows], ffns[s, :, 2 * hz :])
            grads = against(grad_act[s, rows], ffns[s, :, 0 : 2 * hz])
            if s == 0:
                out_tile[...] = outs
                grad_tile[...] = grads
            else:
                out_tile[...] += outs
                grad_tile[...] += grads
        here = pl.ds(pl.multiple_of(i * BLOCK, BLOCK), BLOCK)

        @pl.when(kind == 0)
        def _():
            grad_in[here] = grad_tile[...]
            out_own[here] = middle[here] + out_tile[...]

        @pl.when(kind == 1)
        def _():
            side_grad[here] = grad_tile[...].astype(BF)
            side_out[here] = out_tile[...].astype(BF)
            for copy in grad_copy(i):
                copy.start()

        @pl.when(kind == 2)
        def _():
            cross_grad[here] = grad_tile[...].astype(BF)
            cross_out[here] = out_tile[...].astype(BF)
            for copy in cross_copy(i):
                copy.start()

        @pl.when(kind == 3)
        def _():
            for copy in cross_copy(i):
                copy.wait_recv()
            far_grad[here] = (grad_tile[...] + pre_grad[here].astype(F32)).astype(BF)
            out_far[here] = (out_tile[...] + pre_out[here].astype(F32)).astype(BF)
            far_copy(i).start()

    loop(4, feed)
    for i in range(1, B):
        mlp_copy(2, i).wait_recv()
        mlp_copy(3, i).start()
        loop(4, lambda t: feed(t + 4 * i))

    far.finish()

    def weight_tile(t):
        rows = at(t, BLOCK)
        for s in range(K):
            ffns[s, rows, 0 : 2 * hz] = inner(mlp[:, rows], grad_act[s]).astype(BF)
            ffns[s, rows, 2 * hz :] = inner(cots[:, rows], hidden[s]).astype(BF)
        save_grads(t).start()

    def save_grads(t):
        rows = at(t, BLOCK)
        return pltpu.make_async_copy(ffns.at[:, rows], grads_out.at[:, rows], gsem.at[t])

    loop(D // BLOCK, weight_tile)

    def join(t):
        rows = at(t, 64)
        out_own[rows] = out_own[rows] + mate_out[rows].astype(F32)
        grad_in[rows] = grad_in[rows] + mate_grad[rows].astype(F32) + pair_grad[rows].astype(F32)

    for i in range(B):
        for copy in grad_copy(i):
            copy.wait()
        for copy in cross_copy(i):
            copy.wait_send()
        far_copy(i).wait()
        for n in (1, 2, 3):
            mlp_copy(n, i).wait_send()
    loop(T // 64, join)
    for save in (save_slabs, save_query, save_bias, save_window, save_att, save_lse):
        save.wait()
    for t in range(D // BLOCK):
        save_grads(t).wait()
    behind(mark_own, mark_place, 0, "sent")
    behind(key_place(2), key_place, 3, "sent")
    for i in range(B):
        cot_copy(2, i).wait_send()
        cot_copy(3, i).wait_send()
    if with_slab:
        for gather in (near_rest, near, near_out):
            gather.finish()


def forward(shape, with_slab, tokens, cot, segment, w_gate, w_up, w_down, *slab):
    X, Y, Z = sides(shape)
    R = shape[0]
    T, D = tokens.shape
    E, hz = H * DH, w_gate.shape[1]
    W = 2 * E + 2 * DH + 128
    B = T // BLOCK
    span = WINDOW + BLOCK
    K = Z // 2
    S, V = jax.ShapeDtypeStruct, pltpu.VMEM
    outs = [
        S((T, D), F32), S((T, D), F32), S((T, D), F32), S((T, D), BF), S((8, D), F32),
        S((D, W), BF), S((T, E), BF), S((3 * T, 2 * DH), BF), S((B, span, BLOCK), F32),
        S((E, T), BF), S((H * B, 8, BLOCK), F32), S((K, D, 3 * hz), BF),
    ]
    near, far = gather_count(X, Y, Z), gather_count(X, Y, K)
    scratch = [
        V((D, W), BF), V((K, D, 3 * hz), BF), V((T, E), BF), V((3 * T, 2 * DH), BF),
        V((DH, 3 * T), BF), V((8, 3 * T), F32), V((B, span, BLOCK), F32), V((E, T), BF),
        V((H * B, 8, BLOCK), F32), V((4 * T, D), BF), V((4 * T, D), BF),
        V((BLOCK, D), F32), V((BLOCK, D), F32), V((K, 4 * T, hz), BF), V((K, 4 * T, 2 * hz), BF),
        *[V((T, D), BF)] * 10,
        *[DMA((near,))] * 6, *[DMA((far,))] * 2, *[DMA((3 * R * Z,))] * 2, *[DMA((6,))] * 2,
        *[DMA((1 + 2 * B,))] * 2, *[DMA((3 * B,))] * 2, *[DMA((5 * B,))] * 2, DMA((7,)), DMA((D // BLOCK,)),
    ]
    return pl.pallas_call(
        functools.partial(forward_kernel, shape, with_slab, (D, T, W, hz)),
        out_shape=outs,
        in_specs=[VM, ANY] + [VM] * 4 + [VM if with_slab else ANY] * len(slab),
        out_specs=[VM] * 5 + [ANY] * 7,
        scratch_shapes=scratch,
        compiler_params=pltpu.CompilerParams(
            collective_id=0, has_side_effects=True, vmem_limit_bytes=62 << 20
        ),
        name="forward",
    )(tokens, cot, segment, w_gate, w_up, w_down, *slab)


def backward_kernel(shape, with_slab, sizes, *refs):
    D, T, W, hz = sizes
    E, QK, WO = slab_lanes()
    B = T // BLOCK
    span = WINDOW + BLOCK
    refs = list(refs)

    def some(n):
        taken = refs[:n]
        del refs[:n]
        return taken

    (tokens_in, cot_in, grad_in_in, middle_in, out_own_in, out_far,
     gains_in, slabs_in, query_in, window_in, bias_in, att_in, lse_in, grads) = some(14)
    output, grad_tokens, gate_out, up_out, down_out, out_slab, query_slab = some(7)
    keyval_slab, gain_slab = some(2) if with_slab else (some(1)[0], None)
    (tokens, cot, middle, grad_in, slabs, query, window, bias, att, lse, out_own, out_pair,
     gains, keys_t, branch, att_grad, query_grad_t, query_grad, kv_sum, kv_send, kv_recv, kv_grad, attn_in_t,
     gain_rows, termx, termy, own, ffn_sum) = some(28)
    weight_grads = some(3)
    fwork = some(4)
    if with_slab:
        rest_sum, *crossed = some(4)
        works = [some(4) for _ in range(3)]
    fsend, frecv, ksend, krecv, lsem, tsem = some(6)
    if with_slab:
        nsems = some(6)
        xsend, xrecv = some(2)
    p = Place(shape)
    pack = Pack(p, T)
    mate, spot = pack.mate, pack.spot
    K = p.Z // 2
    br = D // p.R

    def part(s, r):
        return grads.at[s, at(r, br)]

    def cut(ref, h):
        rows = ref.shape[0] // 2
        return ref.at[pl.ds(h * rows, rows)]

    ready = pack.greet()
    order = list(range(1, K)) + [0]
    terms = {}
    for s in order:
        copies = []
        for d in p.xs:
            copies.append((cut(part(s, p.row_at(dx=d)), 1), termx.at[s, d - 1]))
        for e in p.ys:
            copies.append((cut(part(s, p.row_at(dy=e)), 0), termy.at[s, e - 1]))
        copies.append((part(s, p.row), own.at[s]))
        n = s * (p.X + p.Y - 1)
        terms[s] = [
            pltpu.make_async_copy(a, b, tsem.at[n + i]) for i, (a, b) in enumerate(copies)
        ]
    pairs = [
        (middle_in, middle), (grad_in_in, grad_in), (cot_in, cot), (gains_in, gains), (slabs_in, slabs), (att_in, att),
        (tokens_in, tokens), (window_in, window), (query_in, query), (bias_in, bias), (lse_in, lse),
        (out_own_in, out_own),
    ]
    loads = [pltpu.make_async_copy(a, b, lsem.at[n]) for n, (a, b) in enumerate(pairs)]
    for load in loads[:4]:
        load.start()
    ready()
    far = Scatter(
        part, cut, p, Sems(fsend, frecv),
        lambda s, d: termx.at[s, d - 1], lambda s, e: termy.at[s, e - 1], lambda s: own.at[s],
        *fwork, 2
    )
    def far_second():
        for s in order:
            for copy in terms[s]:
                copy.wait()
            far.second(s)

    for s in order:
        far.first(s)
    out_copy = remote(out_far, out_pair, ksend.at[2], krecv.at[2], pack.pair)
    out_copy.start()

    for load in loads[:4]:
        load.wait()
    for load in loads[4:]:
        load.start()
    for s in order:
        for copy in terms[s]:
            copy.start()
    gain_rows[...] = jnp.zeros_like(gain_rows)

    def fold_rows(value):
        return jnp.sum(value.reshape(value.shape[0] // 8, 8, D), axis=0)

    def second_norm(t, total):
        rows = at(t, 64)
        value, grad = middle[rows], grad_in[rows]
        scale = rms_scale(value)
        total = total + fold_rows(grad * (value * scale))
        n = grad * gains[1:2]
        out = cot[rows].astype(F32) + scale * n - value * (
            scale * scale * scale * jnp.mean(n * value, axis=-1, keepdims=True)
        )
        grad_in[rows] = out
        branch[rows] = out.astype(BF)
        return total

    total = lax.fori_loop(0, T // 64, second_norm, jnp.zeros((8, D), F32))
    gain_rows[1:2] = jnp.sum(total, axis=0, keepdims=True)

    loads[4].wait()

    def attended_grad(t):
        att_grad[at(t, BLOCK)] = against(slabs[at(t, BLOCK), WO:], branch[...]).astype(BF)

    loop(E // BLOCK, attended_grad)
    loads[5].wait()
    ar = D // (p.R * p.Z * 2)
    blocks = BLOCK // (2 * ar)

    def put(ref, t, lanes, value):
        if with_slab:
            ref[pl.ds(t * blocks, blocks), :, :, lanes] = value.astype(BF).reshape(
                blocks, 2, ar, value.shape[1]
            )
        else:
            ref[at(t, BLOCK), lanes] = value.astype(BF)

    def out_weight_grad(t):
        put(weight_grads[0], t, slice(0, E), product(att[at(t, BLOCK)], branch[...]))

    loop(E // BLOCK, out_weight_grad)

    class Near:
        def __init__(self, n):
            self.n, self.ref = n, weight_grads[n]
            self.copy = remote(
                self.ref.at[:, 1 - p.core], crossed[n], xsend.at[n], xrecv.at[n], mate
            )
            self.copy.start()

        def block(self, s, r):
            return self.ref.at[r * p.Z + p.z_at(s), p.core]

        def fold(self):
            self.copy.wait()
            ref, other = self.ref, crossed[self.n]

            def step(n):
                ref[n, p.core] = (ref[n, p.core].astype(F32) + other[n].astype(F32)).astype(BF)

            loop(p.R * p.Z, step)
            block = self.block
            self.scatter = Scatter(
                block, cut, p, Sems(*nsems[2 * self.n : 2 * self.n + 2]),
                lambda s, d: cut(block(s, p.row_at(dx=d)), 1),
                lambda s, e: cut(block(s, p.row_at(dy=e)), 0),
                lambda s: block(s, p.row), *works[self.n]
            )
            for s in self.order():
                self.scatter.first(s)

        def order(self):
            return list(range(1, p.Z)) + [0]

        def second(self):
            for s in self.order():
                self.scatter.second(s)

        def third(self):
            for s in self.order()[:-1]:
                self.scatter.third(s)

        def last(self, out):
            self.scatter.third(0, out)
            self.scatter.finish()

    if with_slab:
        near_out = Near(0)

    for load in loads[6:]:
        load.wait()

    def first_norm(t):
        cols = at(t, 128)
        value = tokens[cols].astype(F32)
        attn_in_t[:, cols] = (value * rms_scale(value) * gains[0:1]).astype(BF).T

    loop(T // 128, first_norm)
    keys_t[...] = window[:, 0:DH].T
    kv_sum[...] = jnp.zeros_like(kv_sum)
    if with_slab:
        near_out.fold()

    factor = LOG2E / math.sqrt(DH)
    scale = 1.0 / math.sqrt(DH)

    def head(i, h):
        lanes = at(h, DH)
        here = pl.ds(i * BLOCK, BLOCK)
        seen = pl.ds(i * BLOCK, span)
        part_query = query[here, lanes]
        part_grad = att_grad[lanes, here]
        scores = against(window[seen, 0:DH], part_query) * factor + bias[i]
        probs = jnp.exp2(scores - lse[h * B + i][0:1])
        grad_probs = product(window[seen, DH:], part_grad)
        centre = jnp.sum(
            att[lanes, here].astype(F32) * part_grad.astype(F32), axis=0, keepdims=True
        )
        grad_scores = (probs * (grad_probs - centre)).astype(BF)
        kv_sum[seen, DH:] += against(probs.astype(BF), part_grad)
        kv_sum[seen, 0:DH] += product(grad_scores, part_query)
        query_grad_t[lanes, here] = (product(keys_t[:, seen], grad_scores) * scale).astype(BF)

    for i in range(B):
        loop(H, lambda h: head(i, h))

    kv_send[:, 0:DH] = (kv_sum[pl.ds(0, 2 * T), 0:DH] * scale).astype(BF)
    kv_send[:, DH:] = kv_sum[pl.ds(0, 2 * T), DH:].astype(BF)
    returns = []
    for d in (1, 2):
        to = (p.row, lax.rem(p.col - d + 2 * p.Z, 2 * p.Z))
        copy = remote(
            kv_send.at[pl.ds((2 - d) * T, T)], kv_recv.at[d - 1], ksend.at[d - 1], krecv.at[d - 1], to
        )
        pl.when(spot - d >= 0)(copy.start)
        returns.append((d, copy))

    far_second()
    if with_slab:
        near_out.second()

    def turn(t):
        query_grad[at(t, BLOCK)] = query_grad_t[:, at(t, BLOCK)].T

    loop(B, turn)

    def query_weight_grad(t):
        put(weight_grads[1], t, slice(0, E), product(attn_in_t[at(t, BLOCK)], query_grad[...]))

    loop(D // BLOCK, query_weight_grad)
    if with_slab:
        near_query = Near(1)

    def input_grad_query(t):
        rows = at(t, 128)
        grad_tokens[rows] = against(query_grad[rows], slabs[:, 0:E])

    loop(T // 128, input_grad_query)
    kv_grad[:, 0:DH] = kv_sum[pl.ds(2 * T, T), 0:DH] * scale
    kv_grad[:, DH:] = kv_sum[pl.ds(2 * T, T), DH:]
    if with_slab:
        near_query.fold()
    for d, copy in returns:
        @pl.when(spot + d < pack.size)
        def _():
            copy.wait_recv()
            kv_grad[...] += kv_recv[d - 1].astype(F32)

    window[pl.ds(0, T)] = kv_grad[...].astype(BF)

    for s in order[:-1]:
        far.third(s)

    def keyval_weight_grad(t):
        put(weight_grads[2], t, slice(0, 2 * DH), product(attn_in_t[at(t, BLOCK)], window[pl.ds(0, T)]))

    loop(D // BLOCK, keyval_weight_grad)

    def input_grad(t, total):
        rows = at(t, 128)
        grad = grad_tokens[rows] + against(window[rows], slabs[:, E:QK])
        value = tokens[rows].astype(F32)
        scale_first = rms_scale(value)
        total = total + fold_rows(grad * (value * scale_first))
        m = grad * gains[0:1]
        grad_tokens[rows] = grad_in[rows] + scale_first * m - value * (
            scale_first * scale_first * scale_first * jnp.mean(m * value, axis=-1, keepdims=True)
        )
        return total

    total = lax.fori_loop(0, T // 128, input_grad, jnp.zeros((8, D), F32))
    gain_rows[0:1] = jnp.sum(total, axis=0, keepdims=True)

    def gain_grad(t):
        put(weight_grads[2], t, slice(2 * DH, 2 * DH + 128), gain_rows[:, at(t, BLOCK)].T)

    loop(D // BLOCK, gain_grad)
    if with_slab:
        near_rest = Near(2)
    if with_slab:
        near_query.second()
        near_rest.fold()
        near_out.third()
        near_query.third()
        near_rest.second()
        near_rest.third()
        near_out.last(out_slab)
    else:
        for ref, out in zip(weight_grads, (out_slab, query_slab, keyval_slab)):
            out[...] = ref[...]
    out_copy.wait_recv()

    def join(t):
        rows = at(t, 64)
        output[rows] = (out_own[rows] + out_pair[rows].astype(F32)).astype(BF)

    loop(T // 64, join)
    far.third(0, ffn_sum)
    gate_out[...] = ffn_sum[:, 0:hz]
    up_out[...] = ffn_sum[:, hz : 2 * hz]
    down_out[...] = ffn_sum[:, 2 * hz :].T
    if with_slab:
        near_query.last(query_slab)
        near_rest.last(rest_sum)
        keyval_slab[...] = rest_sum[:, 0 : 2 * DH]
        gain_slab[...] = rest_sum[:, 2 * DH :]
    out_copy.wait_send()
    for d, copy in returns:
        pl.when(spot - d >= 0)(copy.wait_send)
    far.finish()


def backward(
    shape, with_slab, tokens, cot, grad_in, middle, out_own, out_far, gains, slabs, query, window, bias, att, lse, grads
):
    X, Y, Z = sides(shape)
    R = shape[0]
    T, D = tokens.shape
    E, hz = H * DH, grads.shape[2] // 3
    W = slabs.shape[1]
    B = T // BLOCK
    span = WINDOW + BLOCK
    K = Z // 2
    near, far = scatter_count(X, Y, Z), scatter_count(X, Y, K)
    S, V = jax.ShapeDtypeStruct, pltpu.VMEM
    block = (D // R, 3 * hz)
    half = (block[0] // 2, block[1])
    widths = (E, E, 2 * DH + 128)
    ar = D // (R * Z * 2)
    if with_slab:
        slab_outs = [S((ar, w), F32) for w in (E, E, 2 * DH, 128)]
        slab_work = [V((R * Z, 2, ar, w), BF) for w in widths]
    else:
        slab_outs = [S((D, w), BF) for w in widths]
        slab_work = [V((D, w), BF) for w in widths]
    outs = [S((T, D), BF), S((T, D), F32)]
    outs += [S((D // R, hz), F32), S((D // R, hz), F32), S((hz, D // R), F32)] + slab_outs
    scratch = [
        V((T, D), BF), V((T, D), BF), V((T, D), F32), V((T, D), F32), V((D, W), BF), V((T, E), BF),
        V((3 * T, 2 * DH), BF), V((B, span, BLOCK), F32), V((E, T), BF), V((H * B, 8, BLOCK), F32),
        V((T, D), F32), V((T, D), BF),
        V((8, D), F32), V((DH, 3 * T), BF), V((T, D), BF), V((E, T), BF), V((E, T), BF), V((T, E), BF),
        V((3 * T, 2 * DH), F32), V((2 * T, 2 * DH), BF), V((2, T, 2 * DH), BF), V((T, 2 * DH), F32),
        V((D, T), BF), V((128, D), F32),
        V((K, X - 1) + half, BF), V((K, Y - 1) + half, BF), V((K,) + block, BF), V(block, F32),
        *slab_work,
        *scatter_scratch(X, Y, K, block),
    ]
    if with_slab:
        scratch += [V((ar, widths[2]), F32)] + [V((R * Z, ar, w), BF) for w in widths]
        for w in widths:
            scratch += scatter_scratch(X, Y, Z, (ar, w))
    scratch += [
        DMA((far,)), DMA((far,)), DMA((3,)), DMA((3,)), DMA((12,)), DMA((K * (X + Y - 1),)),
    ]
    if with_slab:
        scratch += [DMA((near,))] * 6 + [DMA((3,))] * 2
    return pl.pallas_call(
        functools.partial(backward_kernel, shape, with_slab, (D, T, W, hz)),
        out_shape=outs,
        in_specs=[ANY] * 14,
        out_specs=[VM] * len(outs),
        scratch_shapes=scratch,
        compiler_params=pltpu.CompilerParams(
            collective_id=1, has_side_effects=True, vmem_limit_bytes=62 << 20
        ),
        name="backward",
    )(tokens, cot, grad_in, middle, out_own, out_far, gains, slabs, query, window, bias, att, lse, grads)


def hand_over_kernel(count, *refs):
    sources, results, held, sems = refs[:count], refs[count : 2 * count], refs[2 * count : -1], refs[-1]
    reads = [pltpu.make_async_copy(a, b, sems.at[0, n]) for n, (a, b) in enumerate(zip(sources, held))]
    writes = [pltpu.make_async_copy(a, b, sems.at[1, n]) for n, (a, b) in enumerate(zip(held, results))]
    for read in reads:
        read.start()
    for read, write in zip(reads, writes):
        read.wait()
        write.start()
    for write in writes:
        write.wait()


def hand_over(arrays):
    count = len(arrays)
    return pl.pallas_call(
        functools.partial(hand_over_kernel, count),
        out_shape=[jax.ShapeDtypeStruct(a.shape, a.dtype) for a in arrays],
        in_specs=[ANY] * count,
        out_specs=[ANY] * count,
        scratch_shapes=[pltpu.VMEM(a.shape, a.dtype) for a in arrays] + [DMA((2, count))],
        compiler_params=pltpu.CompilerParams(vmem_limit_bytes=62 << 20),
        name="hand_over",
    )(*arrays)


def shards(
    shape,
    tokens, gain_attn, w_query, w_keyval, w_out, gain_mlp, w_gate, w_up, w_down, segment, cotangent
):
    with_slab = w_query.shape[0] % 32 == 0
    gain_columns = jnp.pad(jnp.stack([gain_attn, gain_mlp], axis=1), ((0, 0), (0, 126)))
    slab = [w_query, w_keyval, gain_columns, w_out]
    if not with_slab:
        slab = [lax.all_gather(jnp.concatenate(slab, axis=1), ("row", "col"), axis=0, tiled=True)]
    kept = forward(shape, with_slab, tokens, cotangent, segment[None], w_gate, w_up, w_down, *slab)
    results = backward(shape, with_slab, tokens, cotangent, *kept)
    output, grad_tokens, gate_grad, up_grad, down_grad = results[:5]
    if with_slab:
        *arrays, gain_grad = results
        output, grad_tokens, gate_grad, up_grad, down_grad, out_grad, query_grad, keyval_grad = hand_over(
            arrays)
    else:
        out_grad, query_grad, rest_grad = [
            lax.psum_scatter(g.astype(F32), ("row", "col"), scatter_dimension=0, tiled=True)
            for g in results[5:]
        ]
        keyval_grad, gain_grad = rest_grad[:, : 2 * DH], rest_grad[:, 2 * DH :]
    return (
        output,
        grad_tokens,
        gain_grad[:, 0],
        query_grad,
        keyval_grad,
        out_grad,
        gain_grad[:, 1],
        gate_grad,
        up_grad,
        down_grad,
    )


def solution(mesh):
    shape = (mesh.shape["row"], mesh.shape["col"])
    return jax.shard_map(
        functools.partial(shards, shape),
        mesh=mesh,
        in_specs=(
            P(("row", "col"), None),
            P(("row", "col")),
            P(("row", "col"), None),
            P(("row", "col"), None),
            P(("row", "col"), None),
            P(("row", "col")),
            P("row", "col"),
            P("row", "col"),
            P("col", "row"),
            P(("row", "col")),
            P(("row", "col"), None),
        ),
        out_specs=(
            P(("row", "col"), None),
            P(("row", "col"), None),
            P(("row", "col")),
            P(("row", "col"), None),
            P(("row", "col"), None),
            P(("row", "col"), None),
            P(("row", "col")),
            P("row", "col"),
            P("row", "col"),
            P("col", "row"),
        ),
        check_vma=False,
    )
```
